32 devices in a mesh: field: 2 (over x), slab: 16 (over z, y, core).
Axes of the slice: x: 2, y: 2, z: 4, core: 2. Of those that a mesh axis runs over, the one named last changes fastest.
Arguments:
- right_side: float32 [128, 64, 512], P(('field', 'slab')), parts along dimension 0, may hold values from -7.3 to 8
- cond_x: float32 [64, 64, 512], P('slab'), may hold values from 0.2 to 5
- cond_y: float32 [64, 64, 512], P('slab'), may hold values from 0.2 to 5
- cond_z: float32 [64, 64, 512], P('slab'), may hold values from 0.2 to 5
- kappa_sq: float32 [64, 64, 512], P('slab'), may hold values from 0.05 to 2
- shifts: float32 [8], replicated, may hold values from 0.01 to 20
- weights: float32 [8], replicated, may hold values from 0.3 to 3
Outputs:
- matern_field: float32 [128, 64, 512], P(('field', 'slab')), parts along dimension 0
The draws below stay inside these ranges and needn't reach their ends.
There are 2 independent parts, one for each index of `field`. The reference program is written for one: setup_inputs(seed, part) draws one part's arguments, and reference() takes and returns one part's arrays. A program takes and returns all parts, laid end to end along the dimension named above; an argument that names none is the same for every part. Nothing has to cross between parts.
All inputs are finite; a program needn't handle non-finite values.
Results may differ from the reference program's by a relative error of at most 0.0001.
Values sent between devices are 32-bit elements; how exact they have to be, the bound alone decides.
No kernel may reach another device: no remote copies, remote signals or barrier semaphores. Data moves between devices by JAX's collectives and lax.ppermute only.
A program may use at most 64 MiB of HBM per device.

```python
import math
import jax
import jax.numpy as jnp
from jax import lax

NSHIFT = 8
ITERS = 3
NZ = 64
NY = 512
NX = 64


def draw_right_side(key, part):
    key = jax.random.fold_in(key, 7)
    position = jnp.arange(NX, dtype=jnp.float32) / (NX - 1)
    ramp = (0.6 + 1.2 * position)[:, None, None]
    noise = jnp.clip(jax.random.normal(key, (NX, NZ, NY), jnp.float32), -4.0, 4.0)
    return ramp * noise


def levels(key, dims, shards, smallest, top_value):
    gain = 1.0
    for axis_at, shards_of in shards:
        steps = jax.random.uniform(jax.random.fold_in(jax.random.fold_in(key, 6), axis_at), (shards_of,), jnp.float32, smallest / len(shards), top_value / len(shards))
        gain = gain * jnp.repeat(jnp.exp(steps), dims[axis_at] // shards_of).reshape((-1,) + (1,) * (len(dims) - 1 - axis_at))
    return gain


def setup_inputs(seed: int = 0, part: int = 0) -> dict:
    seeds = jax.random.split(jax.random.key(seed), 8)
    part_keys = jax.random.split(jax.random.fold_in(seeds[7], part), 8)
    right_side = draw_right_side(jax.random.fold_in(jax.random.fold_in(seeds[7], part), 71), part)
    cond_x = jnp.clip(jnp.exp(math.log(5.0) - 3.218876 * jax.random.uniform(seeds[1], (NX, NZ, NY), jnp.float32) ** levels(seeds[1], (NX, NZ, NY), ((0, 16),), -0.2, 0.2)), 0.2, 5.0)
    cond_y = jnp.clip(jnp.exp(math.log(5.0) - 3.218876 * jax.random.uniform(seeds[2], (NX, NZ, NY), jnp.float32) ** levels(seeds[2], (NX, NZ, NY), ((0, 16),), -0.2, 0.2)), 0.2, 5.0)
    cond_z = jnp.clip(jnp.exp(math.log(5.0) - 3.218876 * jax.random.uniform(seeds[3], (NX, NZ, NY), jnp.float32) ** levels(seeds[3], (NX, NZ, NY), ((0, 16),), -0.2, 0.2)), 0.2, 5.0)
    kappa_sq = jnp.clip(jnp.exp(math.log(2.0) - 3.6888794 * jax.random.uniform(seeds[4], (NX, NZ, NY), jnp.float32) ** levels(seeds[4], (NX, NZ, NY), ((0, 16),), -0.2, 0.2)), 0.05, 2.0)
    shifts = jnp.clip(jnp.exp(jax.random.uniform(seeds[5], (NSHIFT,), jnp.float32, math.log(0.01), math.log(20.0))), 0.01, 20.0)
    weights = jnp.clip(jnp.exp(jax.random.uniform(seeds[6], (NSHIFT,), jnp.float32, math.log(0.3), math.log(3.0))), 0.3, 3.0)
    return dict(right_side=right_side, cond_x=cond_x, cond_y=cond_y, cond_z=cond_z, kappa_sq=kappa_sq, shifts=shifts, weights=weights)


def face_pair(values, axis):
    count = values.shape[axis]
    widths = [(1, 1) if number == axis else (0, 0) for number in range(values.ndim)]
    padded = jnp.pad(values, widths)
    faces = 0.5 * (lax.slice_in_dim(padded, 0, count + 1, axis=axis) + lax.slice_in_dim(padded, 1, count + 2, axis=axis))
    return lax.slice_in_dim(faces, 0, count, axis=axis), lax.slice_in_dim(faces, 1, count + 1, axis=axis)


def neighbours(field, axis, low, high):
    count = field.shape[axis]
    widths = [(1, 1) if number == axis else (0, 0) for number in range(field.ndim)]
    padded = jnp.pad(field, widths)
    return low * lax.slice_in_dim(padded, 0, count, axis=axis) + high * lax.slice_in_dim(padded, 2, count + 2, axis=axis)


def operate(field, shifted_diag, coefficients):
    low_x, high_x, low_z, high_z, low_y, high_y = coefficients
    result = shifted_diag * field - neighbours(field, 0, low_x, high_x)
    result = result - neighbours(field, 1, low_z, high_z)
    result = result - neighbours(field, 2, low_y, high_y)
    return result


def reference(right_side, cond_x, cond_y, cond_z, kappa_sq, shifts, weights):
    low_x, high_x = face_pair(cond_x, 0)
    low_z, high_z = face_pair(cond_z, 1)
    low_y, high_y = face_pair(cond_y, 2)
    diagonal = kappa_sq + low_x + high_x + low_z + high_z + low_y + high_y
    coefficients = (low_x, high_x, low_z, high_z, low_y, high_y)

    def solve_one(operands):
        shift, weight = operands
        shifted_diag = diagonal + shift
        iterate = jnp.zeros_like(right_side)
        residual = right_side
        precond = residual / shifted_diag
        direction = precond
        norm_now = jnp.sum(residual * precond)
        for number in range(ITERS):
            image = operate(direction, shifted_diag, coefficients)
            step_size = norm_now / jnp.sum(direction * image)
            iterate = iterate + step_size * direction
            residual = residual - step_size * image
            if number + 1 < ITERS:
                precond = residual / shifted_diag
                norm_next = jnp.sum(residual * precond)
                direction = precond + (norm_next / norm_now) * direction
                norm_now = norm_next
        return weight * iterate

    return jnp.sum(lax.map(solve_one, (shifts, weights)), axis=0)
```

```python
import functools
import jax
import jax.numpy as jnp
from jax import lax
from jax.experimental import pallas as pl
from jax.experimental.pallas import tpu as pltpu
from jax.sharding import PartitionSpec as P

LANES = 128
PAD = 8
VMEM_LIMIT = 52 * 1024 * 1024


class Dims:
    def __init__(self, shape):
        self.nl, self.nz, self.ny = shape
        self.nc = self.ny // LANES
        self.plane = self.nc * self.nz
        self.half = self.nz // 2
        self.more = self.half + 8
        self.own = self.nl * self.plane
        self.np = self.nl + 6
        self.rows = self.np * self.plane + 2 * PAD
        names = ["b1", "d1", "x1", "fy1", "fz1", "d2", "b2", "fx2"]
        sizes = [self.plane] * 8 + [self.nc * self.half] * 3 + [self.nc * self.more]
        self.at = {}
        total = 0
        for name, size in zip(names + ["fy2", "d3", "g3", "fz2"], sizes):
            self.at[name] = total
            total += size
        self.sent = total


def lane_ids():
    return lax.broadcasted_iota(jnp.int32, (8, LANES), 1)


def row_ids():
    return lax.broadcasted_iota(jnp.int32, (8, LANES), 0)


def from_higher(tiles):
    lane = lane_ids()
    n = len(tiles)
    return [
        pltpu.roll(jnp.where(lane == 0, tiles[(c + 1) % n], tiles[c]), LANES - 1, 1)
        for c in range(n)
    ]


def from_lower(tiles):
    lane = lane_ids()
    n = len(tiles)
    return [
        pltpu.roll(jnp.where(lane == LANES - 1, tiles[(c - 1) % n], tiles[c]), 1, 1)
        for c in range(n)
    ]


def prepare(dm, par, cx, cy, cz, kappa, b, bf, df, xf, yf, zf, first):
    nc, nz, nl = dm.nc, dm.nz, dm.nl
    lane = lane_ids()
    sub = row_ids()

    def layer(p):
        return jnp.where(par == 0, p, nl - 1 - p)

    for p in range(nl):
        at = layer(p)

        def copy(zb, carry, at=at, p=p):
            z = pl.multiple_of(zb * 8, 8)
            base = PAD + (first + p) * dm.plane
            blocks = [ref[at, pl.ds(z, 8), :] for ref in (b, cx, cz)]
            for block, dst in zip(blocks, (bf, xf, zf)):
                for c in range(nc):
                    dst[pl.ds(base + c * nz + z, 8), :] = block[:, c * LANES : (c + 1) * LANES]
            return carry

        lax.fori_loop(0, nz // 8, copy, 0)

    for p in range(nl):
        at = layer(p)

        def faces(zb, carry, at=at, p=p):
            z = pl.multiple_of(zb * 8, 8)
            base = PAD + (first + p) * dm.plane
            conds = cy[at, pl.ds(z, 8), :]
            kap = kappa[at, pl.ds(z, 8), :]
            ys = [conds[:, c * LANES : (c + 1) * LANES] for c in range(nc)]
            up, down = from_higher(ys), from_lower(ys)
            up[-1] = jnp.where(lane == LANES - 1, 0.0, up[-1])
            down[0] = jnp.where(lane == 0, 0.0, down[0])
            for c in range(nc):
                row = base + c * nz + z
                high_y = 0.5 * (ys[c] + up[c])
                low_y = 0.5 * (ys[c] + down[c])
                here = zf[pl.ds(row, 8), :]
                above = zf[pl.ds(row + 1, 8), :]
                below = zf[pl.ds(row - 1, 8), :]
                high_z = 0.5 * (here + jnp.where(sub + z == nz - 1, 0.0, above))
                low_z = 0.5 * (here + jnp.where(sub + z == 0, 0.0, below))
                total = kap[:, c * LANES : (c + 1) * LANES]
                mine = xf[pl.ds(row, 8), :]
                if p > 0:
                    total = total + 0.5 * (mine + xf[pl.ds(row - dm.plane, 8), :])
                else:
                    total = total + 0.5 * mine
                if p < nl - 1:
                    total = total + 0.5 * (mine + xf[pl.ds(row + dm.plane, 8), :])
                else:
                    total = total + 0.5 * mine
                df[pl.ds(row, 8), :] = total + low_z + high_z + low_y + high_y
                if c == nc - 1:
                    high_y = jnp.where(lane == LANES - 1, 0.0, high_y)
                yf[pl.ds(row, 8), :] = high_y
            return carry

        lax.fori_loop(0, nz // 8, faces, 0)

    for p in range(nl):

        def faces_z(zb, carry, p=p):
            z = pl.multiple_of(zb * 8, 8)
            for c in range(nc):
                row = PAD + (first + p) * dm.plane + c * nz + z
                face = 0.5 * (zf[pl.ds(row, 8), :] + zf[pl.ds(row + 1, 8), :])
                zf[pl.ds(row, 8), :] = jnp.where(sub + z == nz - 1, 0.0, face)
            return carry

        lax.fori_loop(0, nz // 8, faces_z, 0)


def pack_body(dm, cx, cy, cz, kappa, b, to_off, to_in, bf, df, xf, yf, zf):
    par = lax.rem(lax.axis_index("slab"), 2)
    nc, nz, nl = dm.nc, dm.nz, dm.nl
    prepare(dm, par, cx, cy, cz, kappa, b, bf, df, xf, yf, zf, 0)
    at = dm.at
    other = 1 - par

    for out, edge, step in ((to_off, 0, 1), (to_in, nl - 1, -1)):

        def row_of(p):
            return PAD + p * dm.plane

        def put(name, ref, p, out=out, row_of=row_of):
            out[at[name] : at[name] + dm.plane, :] = ref[row_of(p) : row_of(p) + dm.plane, :]

        second, third = edge + step, edge + 2 * step
        put("b1", bf, edge)
        put("d1", df, edge)
        put("x1", xf, edge)
        put("fy1", yf, edge)
        put("fz1", zf, edge)
        put("d2", df, second)
        put("b2", bf, second)
        e, s, t = row_of(edge), row_of(second), row_of(third)
        out[at["fx2"] : at["fx2"] + dm.plane, :] = 0.5 * (
            xf[e : e + dm.plane, :] + xf[s : s + dm.plane, :]
        )
        for c in range(nc):
            z = pl.multiple_of(other * dm.half, 8) + c * nz
            z2 = pl.multiple_of(other * (nz - dm.more), 8) + c * nz
            h = c * dm.half
            out[at["fy2"] + h : at["fy2"] + h + dm.half, :] = yf[pl.ds(s + z, dm.half), :]
            out[at["d3"] + h : at["d3"] + h + dm.half, :] = df[pl.ds(t + z, dm.half), :]
            out[at["g3"] + h : at["g3"] + h + dm.half, :] = (
                0.5
                * (xf[pl.ds(s + z, dm.half), :] + xf[pl.ds(t + z, dm.half), :])
                * bf[pl.ds(t + z, dm.half), :]
            )
            h = c * dm.more
            out[at["fz2"] + h : at["fz2"] + h + dm.more, :] = zf[pl.ds(s + z2, dm.more), :]


def basis_body(
    dm, nk, cx, cy, cz, kappa, b, from_off, from_in, shifts, w0_out, w1_out, w2_out, moments,
    bf, df, xf, yf, zf, rf, w0, w1, w2, acc, sems,
):
    index = lax.axis_index("slab")
    count = lax.axis_size("slab")
    par = lax.rem(index, 2)
    has_off = jnp.where(jnp.logical_and(index > 0, index < count - 1), 1.0, 0.0)
    nc, nz, nl, plane = dm.nc, dm.nz, dm.nl, dm.plane
    at = dm.at
    first = 3
    last = first + nl - 1

    def row_of(i):
        return PAD + i * plane

    for ref in (bf, df, xf, yf, zf):
        ref[0:PAD, :] = jnp.zeros((PAD, LANES), jnp.float32)
        ref[dm.rows - PAD :, :] = jnp.zeros((PAD, LANES), jnp.float32)
    prepare(dm, par, cx, cy, cz, kappa, b, bf, df, xf, yf, zf, first)
    acc[...] = jnp.zeros(acc.shape, jnp.float32)
    for ref in (w0, w1, w2):
        rows = ref.shape[1]
        for k in range(nk):
            ref[k, 0:PAD, :] = jnp.zeros((PAD, LANES), jnp.float32)
            ref[k, plane : PAD + plane, :] = jnp.zeros((PAD, LANES), jnp.float32)
            ref[k, rows - PAD - plane : rows - plane, :] = jnp.zeros((PAD, LANES), jnp.float32)
            ref[k, rows - PAD :, :] = jnp.zeros((PAD, LANES), jnp.float32)

    zs = pl.multiple_of(par * dm.half, 8)
    zm = pl.multiple_of(par * (nz - dm.more), 8)

    cx_off = from_off[at["x1"] : at["x1"] + plane, :]
    cx_in = from_in[at["x1"] : at["x1"] + plane, :]
    e, l = row_of(first), row_of(last)
    df[e : e + plane, :] = df[e : e + plane, :] + 0.5 * cx_off
    df[l : l + plane, :] = df[l : l + plane, :] + 0.5 * cx_in
    xf[row_of(first - 1) : e, :] = has_off * 0.5 * (cx_off + xf[e : e + plane, :])
    df[row_of(first - 1) : e, :] = from_off[at["d1"] : at["d1"] + plane, :] + 0.5 * xf[e : e + plane, :]
    df[row_of(last + 1) : row_of(last + 2), :] = (
        from_in[at["d1"] : at["d1"] + plane, :] + 0.5 * xf[l : l + plane, :]
    )
    for i in range(first, last):
        xf[row_of(i) : row_of(i + 1), :] = 0.5 * (
            xf[row_of(i) : row_of(i + 1), :] + xf[row_of(i + 1) : row_of(i + 2), :]
        )
    xf[l : l + plane, :] = 0.5 * (xf[l : l + plane, :] + cx_in)

    for halo, edge, step in ((from_off, first - 1, -1), (from_in, last + 1, 1)):

        def get(name, halo=halo):
            return halo[at[name] : at[name] + plane, :]

        second, third = edge + step, edge + 2 * step
        e, s, t = row_of(edge), row_of(second), row_of(third)
        bf[e : e + plane, :] = get("b1")
        yf[e : e + plane, :] = get("fy1")
        zf[e : e + plane, :] = get("fz1")
        df[s : s + plane, :] = get("d2")
        bf[s : s + plane, :] = get("b2")
        face = row_of(min(edge, second))
        xf[face : face + plane, :] = get("fx2")
        far = row_of(min(second, third))
        xf[far : far + plane, :] = jnp.ones((plane, LANES), jnp.float32)
        zf[s : s + plane, :] = jnp.zeros((plane, LANES), jnp.float32)
        for c in range(nc):
            z, z2, h = zs + c * nz, zm + c * nz, c * dm.half
            yf[pl.ds(s + z, dm.half), :] = halo[at["fy2"] + h : at["fy2"] + h + dm.half, :]
            df[pl.ds(t + z, dm.half), :] = halo[at["d3"] + h : at["d3"] + h + dm.half, :]
            bf[pl.ds(t + z, dm.half), :] = halo[at["g3"] + h : at["g3"] + h + dm.half, :]
            h = c * dm.more
            zf[pl.ds(s + z2, dm.more), :] = halo[at["fz2"] + h : at["fz2"] + h + dm.more, :]

    def tiles(ref, row):
        return [ref[pl.ds(row + c * nz, 8), :] for c in range(nc)]

    def tiles_of(ref, k, row):
        return [ref[k, pl.ds(row + c * nz, 8), :] for c in range(nc)]

    def add(j, k, value):
        at_ = (j * nk + k) * 8
        acc[at_ : at_ + 8, :] += value

    def total(first_tiles, second_tiles):
        products = [p * q for p, q in zip(first_tiles, second_tiles)]
        return functools.reduce(jnp.add, products)

    def over(planes, z_from, z_count, body):
        low, high = planes
        blocks = z_count // 8

        def step(n, carry):
            i = low + lax.div(n, blocks)
            z = pl.multiple_of(z_from + lax.rem(n, blocks) * 8, 8)
            body(i, z)
            return carry

        lax.fori_loop(0, (high - low) * blocks, step, 0)

    def start(i, z, own):
        row = pl.multiple_of(PAD + i * plane + z, 8)
        d, rhs = tiles(df, row), tiles(bf, row)
        for k in range(nk):
            s = shifts[k]
            inverse = [1.0 / (t + s) for t in d]
            value = [x * y for x, y in zip(rhs, inverse)]
            for c in range(nc):
                rf[k, pl.ds(row + c * nz, 8), :] = inverse[c]
                w0[k, pl.ds(row + c * nz, 8), :] = value[c]
            if own:
                add(0, k, total(rhs, value))

    over((first, last + 1), 0, nz, functools.partial(start, own=True))
    over((first - 2, first), 0, nz, functools.partial(start, own=False))
    over((last + 1, last + 3), 0, nz, functools.partial(start, own=False))
    over((first - 3, first - 2), zs, dm.half, functools.partial(start, own=False))
    over((last + 3, last + 4), zs, dm.half, functools.partial(start, own=False))

    def apply(i, z, src, src_first, dst, dst_first, moment):
        row = pl.multiple_of(PAD + i * plane + z, 8)
        src_row = pl.multiple_of(PAD + (i - src_first) * plane + z, 8)
        dst_row = pl.multiple_of(PAD + (i - dst_first) * plane + z, 8)
        x_low, x_high = tiles(xf, row - plane), tiles(xf, row)
        z_low, z_high = tiles(zf, row - 1), tiles(zf, row)
        y_high = tiles(yf, row)
        y_low = from_lower(y_high)
        lane = lane_ids()
        y_low[0] = jnp.where(lane == 0, 0.0, y_low[0])
        for k in range(nk):
            v = tiles_of(src, k, src_row)
            below, above = tiles_of(src, k, src_row - 1), tiles_of(src, k, src_row + 1)
            before, after = tiles_of(src, k, src_row - plane), tiles_of(src, k, src_row + plane)
            left, right = from_lower(v), from_higher(v)
            inverse = tiles_of(rf, k, row)
            image = []
            for c in range(nc):
                image.append(
                    (x_low[c] * before[c] + x_high[c] * after[c])
                    + (z_low[c] * below[c] + z_high[c] * above[c])
                    + (y_low[c] * left[c] + y_high[c] * right[c])
                )
            value = [x * y for x, y in zip(image, inverse)]
            for c in range(nc):
                dst[k, pl.ds(dst_row + c * nz, 8), :] = value[c]
            if moment is not None:
                add(moment, k, total(v, image))
                add(moment + 1, k, total(value, image))

    one = functools.partial(apply, src=w0, src_first=0, dst=w1, dst_first=1)
    over((first, last + 1), 0, nz, functools.partial(one, moment=1))
    over((first - 1, first), 0, nz, functools.partial(one, moment=None))
    over((last + 1, last + 2), 0, nz, functools.partial(one, moment=None))
    over((first - 2, first - 1), zs, dm.half, functools.partial(one, moment=None))
    over((last + 2, last + 3), zs, dm.half, functools.partial(one, moment=None))

    def send_out(src, slot, dst, which):
        copies = []
        for p in range(nl):
            layer = jnp.where(par == 0, p, nl - 1 - p)
            copy = pltpu.make_async_copy(
                src.at[:, pl.ds(PAD + (slot + p) * plane, plane), :],
                dst.at[:, pl.ds(pl.multiple_of(layer * plane, 8), plane), :],
                sems.at[which, p],
            )
            copy.start()
            copies.append(copy)
        return copies

    copies = send_out(w0, first, w0_out, 0) + send_out(w1, first - 1, w1_out, 1)

    two = functools.partial(apply, src=w1, src_first=1, dst=w2, dst_first=2)
    over((first, last + 1), 0, nz, functools.partial(two, moment=3))
    over((first - 1, first), zs, dm.half, functools.partial(two, moment=None))
    over((last + 1, last + 2), zs, dm.half, functools.partial(two, moment=None))
    copies += send_out(w2, first - 2, w2_out, 2)

    def face_sum(i, z, inner, with_x):
        row = pl.multiple_of(PAD + i * plane + z, 8)
        src_row = pl.multiple_of(PAD + (i - 2) * plane + z, 8)
        x_high = tiles(xf, row) if with_x else None
        z_high, y_high = tiles(zf, row), tiles(yf, row)
        for k in range(nk):
            v = tiles_of(w2, k, src_row)
            image = [jnp.zeros((8, LANES), jnp.float32)] * nc
            if inner:
                above, right = tiles_of(w2, k, src_row + 1), from_higher(v)
                image = [z_high[c] * above[c] + y_high[c] * right[c] for c in range(nc)]
            if with_x:
                after = tiles_of(w2, k, src_row + plane)
                image = [image[c] + x_high[c] * after[c] for c in range(nc)]
            add(5, k, 2.0 * total(v, image))

    over((first, last), 0, nz, functools.partial(face_sum, inner=True, with_x=True))
    over((last, last + 1), 0, nz, functools.partial(face_sum, inner=True, with_x=False))
    over((first - 1, first), zs, dm.half, functools.partial(face_sum, inner=False, with_x=True))
    over((last, last + 1), zs, dm.half, functools.partial(face_sum, inner=False, with_x=True))

    count48 = 6 * nk
    sums = jnp.sum(acc[...].reshape(count48, 8, LANES), axis=1)
    sums = jnp.concatenate([sums, jnp.zeros((LANES - count48, LANES), jnp.float32)], axis=0)
    moments[...] = jnp.sum(jnp.transpose(sums), axis=0, keepdims=True)
    for copy in copies:
        copy.wait()


def combine_body(dm, nk, moments, weights, w0, w1, w2, out, coeff):
    nc, nz = dm.nc, dm.nz

    @pl.when(pl.program_id(0) == 0)
    def _():
        sums = jnp.sum(moments[...].reshape(-1, LANES), axis=0, keepdims=True)
        sums = jnp.broadcast_to(sums, (8, LANES))
        nu = [sums] + [pltpu.roll(sums, LANES - j * nk, 1) for j in range(1, 6)]

        def inner(p, q, shift=0):
            total = None
            for i, x in enumerate(p):
                for j, y in enumerate(q):
                    term = x * y * nu[i + j + shift]
                    total = term if total is None else total + term
            return total

        def energy(p):
            return inner(p, p) - inner(p, p, 1)

        one = jnp.ones((8, LANES), jnp.float32)
        zero = jnp.zeros((8, LANES), jnp.float32)
        z = [one]
        p = [one]
        x = [zero, zero, zero]
        norm = nu[0]
        for number in range(3):
            step = norm / energy(p)
            x = [x[j] + step * p[j] if j < len(p) else x[j] for j in range(3)]
            if number < 2:
                p_ext, z_ext = p + [zero], z + [zero]
                z = [
                    z_ext[j] - step * (p_ext[j] - (p_ext[j - 1] if j else zero))
                    for j in range(len(p_ext))
                ]
                norm_next = inner(z, z)
                beta = norm_next / norm
                p = [z[j] + beta * p_ext[j] for j in range(len(z))]
                norm = norm_next
        for j in range(3):
            for k in range(nk):
                at = (j * nk + k) * 8
                coeff[at : at + 8, :] = jnp.broadcast_to(
                    x[j][:, k : k + 1] * weights[k], (8, LANES)
                )

    def block(zb, carry):
        z = pl.multiple_of(zb * 8, 8)
        for c in range(nc):
            row = c * nz + z
            total = None
            for j, ref in enumerate((w0, w1, w2)):
                for k in range(nk):
                    at = (j * nk + k) * 8
                    term = coeff[at : at + 8, :] * ref[k, pl.ds(row, 8), :]
                    total = term if total is None else total + term
            out[0, pl.ds(z, 8), c * LANES : (c + 1) * LANES] = total
        return carry

    lax.fori_loop(0, nz // 8, block, 0)


def on_device(right_side, cond_x, cond_y, cond_z, kappa_sq, shifts, weights):
    dm = Dims(right_side.shape)
    nk = shifts.shape[0]
    count = lax.axis_size("slab")
    f32 = jnp.float32
    vmem = pl.BlockSpec(memory_space=pltpu.VMEM)
    smem = pl.BlockSpec(memory_space=pltpu.SMEM)
    anywhere = pl.BlockSpec(memory_space=pl.ANY)
    params = pltpu.CompilerParams(vmem_limit_bytes=VMEM_LIMIT)
    sent = jax.ShapeDtypeStruct((dm.sent, LANES), f32)
    to_off, to_in = pl.pallas_call(
        functools.partial(pack_body, dm),
        out_shape=(sent, sent),
        in_specs=[vmem] * 5,
        out_specs=(vmem, vmem),
        scratch_shapes=[pltpu.VMEM((dm.own + 2 * PAD, LANES), f32)] * 5,
        compiler_params=params,
        name="pack",
    )(cond_x, cond_y, cond_z, kappa_sq, right_side)

    from_off = lax.ppermute(
        to_off,
        "slab",
        [pair for i in range(1, count - 1, 2) for pair in ((i, i + 1), (i + 1, i))],
    )
    from_in = lax.ppermute(to_in, "slab", [(i, i ^ 1) for i in range(count)])

    fields = jax.ShapeDtypeStruct((nk, dm.own, LANES), f32)
    flat = pltpu.VMEM((dm.rows, LANES), f32)

    def stack(planes):
        return pltpu.VMEM((nk, planes * dm.plane + 2 * PAD, LANES), f32)

    w0, w1, w2, moments = pl.pallas_call(
        functools.partial(basis_body, dm, nk),
        out_shape=(fields, fields, fields, jax.ShapeDtypeStruct((1, LANES), f32)),
        in_specs=[vmem] * 7 + [smem],
        out_specs=(anywhere, anywhere, anywhere, vmem),
        scratch_shapes=[flat] * 5
        + [stack(dm.np), stack(dm.np), stack(dm.np - 2), stack(dm.np - 4)]
        + [pltpu.VMEM((6 * nk * 8, LANES), f32), pltpu.SemaphoreType.DMA((3, dm.nl))],
        compiler_params=params,
        name="basis",
    )(cond_x, cond_y, cond_z, kappa_sq, right_side, from_off, from_in, shifts)

    everywhere = jnp.broadcast_to(moments[None], (count, 1, LANES))
    gathered = lax.all_to_all(everywhere, "slab", 0, 0)

    stacked = pl.BlockSpec((nk, dm.plane, LANES), lambda i: (0, i, 0))
    return pl.pallas_call(
        functools.partial(combine_body, dm, nk),
        out_shape=jax.ShapeDtypeStruct(right_side.shape, f32),
        grid=(dm.nl,),
        in_specs=[
            pl.BlockSpec((count, 1, LANES), lambda i: (0, 0, 0)),
            smem,
            stacked,
            stacked,
            stacked,
        ],
        out_specs=pl.BlockSpec((1, dm.nz, dm.ny), lambda i: (i, 0, 0)),
        scratch_shapes=[pltpu.VMEM((3 * nk * 8, LANES), f32)],
        compiler_params=params,
        name="combine",
    )(gathered, weights, w0, w1, w2)


def solution(mesh):
    return jax.shard_map(
        on_device,
        mesh=mesh,
        in_specs=(
            P(("field", "slab"), None, None),
            P("slab", None, None),
            P("slab", None, None),
            P("slab", None, None),
            P("slab", None, None),
            P(),
            P(),
        ),
        out_specs=P(("field", "slab"), None, None),
        check_vma=False,
    )
```

```python
import functools
import jax
import jax.numpy as jnp
from jax import lax
from jax.experimental import pallas as pl
from jax.experimental.pallas import tpu as pltpu
from jax.sharding import PartitionSpec as P

LANES = 128
PAD = 8
MIB = 1024 * 1024


class Dims:
    def __init__(self, shape):
        self.nl, self.nz, self.ny = shape
        self.nc = self.ny // LANES
        self.plane = self.nc * self.nz
        self.slot = self.plane + PAD
        self.half = self.nz // 2
        self.more = self.half + 8
        full, half = self.plane, self.nc * self.half
        layout = [
            ("pad", PAD), ("fz1", full), ("d1", full), ("x1", full), ("fy1", full),
            ("d2", full), ("fx2", full), ("b1", full), ("b2", full),
            ("fy2", half), ("d3", half), ("g3", half), ("fz2", self.nc * self.more),
        ]
        self.at = {}
        total = 0
        for name, size in layout:
            self.at[name] = total
            total += size
        self.sent = total

    def stack_rows(self, slots):
        return slots * self.slot + PAD


class Plane:
    def __init__(self, ref, base, stride, zoff=0):
        self.ref, self.base, self.stride, self.zoff = ref, base, stride, zoff

    def row(self, c, z):
        return pl.multiple_of(z - self.zoff, 8) + (self.base + c * self.stride)

    def get(self, c, z, k=None, d=0):
        rows = pl.ds(self.row(c, z) + d, 8)
        return self.ref[rows, :] if k is None else self.ref[k, rows, :]

    def put(self, c, z, value, k=None):
        rows = pl.ds(self.row(c, z), 8)
        if k is None:
            self.ref[rows, :] = value
        else:
            self.ref[k, rows, :] = value


def lane_ids():
    return lax.broadcasted_iota(jnp.int32, (8, LANES), 1)


def row_ids():
    return lax.broadcasted_iota(jnp.int32, (8, LANES), 0)


def from_higher(tiles):
    lane = lane_ids()
    n = len(tiles)
    return [
        pltpu.roll(jnp.where(lane == 0, tiles[(c + 1) % n], tiles[c]), LANES - 1, 1)
        for c in range(n)
    ]


def from_lower(tiles):
    lane = lane_ids()
    n = len(tiles)
    return [
        pltpu.roll(jnp.where(lane == LANES - 1, tiles[(c - 1) % n], tiles[c]), 1, 1)
        for c in range(n)
    ]


def blocks(z_from, z_count, body, unroll=1):
    def step(n, carry):
        for u in range(unroll):
            body(pl.multiple_of(z_from + (n * unroll + u) * 8, 8))
        return carry

    lax.fori_loop(0, z_count // (8 * unroll), step, 0)


def own_planes(dm, ref):
    return [Plane(ref, PAD + p * dm.slot, dm.nz) for p in range(dm.nl)]


def prepare(dm, par, cx, cy, cz, kappa, b, flats):
    nc, nz, nl = dm.nc, dm.nz, dm.nl
    bf, df, xf, yf, zf, tf = [own_planes(dm, ref) for ref in flats]
    for ref in (flats[4], flats[5]):
        for p in range(nl + 1):
            ref[p * dm.slot : p * dm.slot + PAD, :] = jnp.zeros((PAD, LANES), jnp.float32)
    layers = [jnp.where(par == 0, p, nl - 1 - p) for p in range(nl)]

    def copy(z):
        for p in range(nl):
            for src, dst in ((b, bf), (cx, xf), (cz, tf)):
                block = src[layers[p], pl.ds(z, 8), :]
                for c in range(nc):
                    dst[p].put(c, z, block[:, c * LANES : (c + 1) * LANES])

    blocks(0, nz, copy)

    def faces(p, z):
        lane, sub = lane_ids(), row_ids()
        conds = cy[layers[p], pl.ds(z, 8), :]
        kap = kappa[layers[p], pl.ds(z, 8), :]
        ys = [conds[:, c * LANES : (c + 1) * LANES] for c in range(nc)]
        up, down = from_higher(ys), from_lower(ys)
        up[-1] = jnp.where(lane == LANES - 1, 0.0, up[-1])
        down[0] = jnp.where(lane == 0, 0.0, down[0])
        for c in range(nc):
            high_y = 0.5 * (ys[c] + up[c])
            low_y = 0.5 * (ys[c] + down[c])
            here = tf[p].get(c, z)
            high_z = 0.5 * (here + jnp.where(sub + z == nz - 1, 0.0, tf[p].get(c, z, d=1)))
            low_z = 0.5 * (here + jnp.where(sub + z == 0, 0.0, tf[p].get(c, z, d=-1)))
            mine = xf[p].get(c, z)
            total = kap[:, c * LANES : (c + 1) * LANES]
            total = total + 0.5 * (mine + xf[p - 1].get(c, z) if p > 0 else mine)
            total = total + 0.5 * (mine + xf[p + 1].get(c, z) if p < nl - 1 else mine)
            df[p].put(c, z, total + low_z + high_z + low_y + high_y)
            if c == nc - 1:
                high_y = jnp.where(lane == LANES - 1, 0.0, high_y)
            yf[p].put(c, z, high_y)
            zf[p].put(c, z, jnp.where(sub + z == nz - 1, 0.0, high_z))

    def all_faces(z):
        for p in range(nl):
            faces(p, z)

    blocks(0, nz, all_faces)


def load_own(sources, targets, sems):
    copies = [
        pltpu.make_async_copy(src, dst, sems.at[n])
        for n, (src, dst) in enumerate(zip(sources, targets))
    ]
    for copy in copies:
        copy.start()
    for copy in copies:
        copy.wait()


def pack_body(dm, cx, cy, cz, kappa, b, to_off, to_in, raw, flats, fx2, g3, zero, in_sems, out_sems):
    par = lax.rem(lax.axis_index("slab"), 2)
    nc, nz, nl = dm.nc, dm.nz, dm.nl
    load_own((cx, cy, cz, kappa, b), raw, in_sems)
    prepare(dm, par, *raw, flats)
    bf, df, xf, yf, zf = [own_planes(dm, ref) for ref in flats[:5]]
    other = 1 - par
    zs = pl.multiple_of(other * dm.half, 8)
    zm = pl.multiple_of(other * (nz - dm.more), 8)
    zero[...] = jnp.zeros(zero.shape, jnp.float32)
    copies = []

    def send(out, name, src, start, rows, shift=0):
        copy = pltpu.make_async_copy(
            src.at[pl.ds(start, rows), :],
            out.at[pl.ds(dm.at[name] + shift, rows), :],
            out_sems.at[len(copies)],
        )
        copy.start()
        copies.append(copy)

    for side, (out, edge, step) in enumerate(((to_off, 0, 1), (to_in, nl - 1, -1))):
        one, two, three = edge, edge + step, edge + 2 * step
        for name, planes, p in (
            ("fz1", zf, one), ("d1", df, one), ("x1", xf, one), ("fy1", yf, one),
            ("d2", df, two), ("b1", bf, one), ("b2", bf, two),
        ):
            send(out, name, planes[p].ref, planes[p].base, dm.plane)
        send(out, "pad", zero, 0, PAD)
        for c in range(nc):
            half = c * dm.half
            send(out, "fy2", yf[two].ref, yf[two].base + c * nz + zs, dm.half, half)
            send(out, "d3", df[three].ref, df[three].base + c * nz + zs, dm.half, half)
            send(out, "fz2", zf[two].ref, zf[two].base + c * nz + zm, dm.more, c * dm.more)

        def derived(z, side=side, one=one, two=two):
            for c in range(nc):
                fx2[pl.ds(side * dm.plane + c * nz + z, 8), :] = 0.5 * (
                    xf[one].get(c, z) + xf[two].get(c, z)
                )

        def derived_half(n, side=side, two=two, three=three):
            z = pl.multiple_of(zs + n, 8)
            for c in range(nc):
                g3[pl.ds((side * nc + c) * dm.half + n, 8), :] = (
                    0.5 * (xf[two].get(c, z) + xf[three].get(c, z)) * bf[three].get(c, z)
                )

        blocks(0, nz, derived)
        blocks(0, dm.half, derived_half)
        send(out, "fx2", fx2, side * dm.plane, dm.plane)
        send(out, "g3", g3, side * nc * dm.half, nc * dm.half)
    for copy in copies:
        copy.wait()


class Steps:
    def __init__(self, dm, nk, par, acc, shifts):
        self.dm, self.nk, self.acc, self.shifts = dm, nk, acc, shifts
        self.zs = pl.multiple_of(par * dm.half, 8)
        self.zm = pl.multiple_of(par * (dm.nz - dm.more), 8)

    def sweep(self, half, body, unroll=2):
        if half:
            blocks(self.zs, self.dm.half, body, unroll)
        else:
            blocks(0, self.dm.nz, body, unroll)

    def add(self, j, k, value):
        at = (j * self.nk + k) * 8
        self.acc[at : at + 8, :] += value

    def total(self, first, second):
        return functools.reduce(jnp.add, [p * q for p, q in zip(first, second)])

    def tiles(self, plane, z, k=None, d=0):
        return [plane.get(c, z, k, d) for c in range(self.dm.nc)]

    def start(self, d, b, w, r=None, half=False, own=False):
        def body(z):
            diagonal, rhs = self.tiles(d, z), self.tiles(b, z)
            for k in range(self.nk):
                s = self.shifts[k]
                inverse = [1.0 / (t + s) for t in diagonal]
                value = [x * y for x, y in zip(rhs, inverse)]
                for c in range(self.dm.nc):
                    if r is not None:
                        r.put(c, z, inverse[c], k)
                    w.put(c, z, value[c], k)
                if own:
                    self.add(0, k, self.total(rhs, value))

        self.sweep(half, body, 1)

    def inverses(self, d, r):
        def body(z):
            diagonal = self.tiles(d, z)
            for k in range(self.nk):
                s = self.shifts[k]
                for c in range(self.dm.nc):
                    r.put(c, z, 1.0 / (diagonal[c] + s), k)

        self.sweep(False, body, 1)

    def apply(self, v, sides, out, r=None, yz=None, base=None, half=False, moment=None):
        nc = self.dm.nc

        def body(z):
            xs = [(None if x is None else self.tiles(x, z), w) for x, w in sides]
            if yz is not None:
                fy, fz = yz
                lane, sub = lane_ids(), row_ids()
                y_high = self.tiles(fy, z)
                y_low = from_lower(y_high)
                y_low[0] = jnp.where(lane == 0, 0.0, y_low[0])
                z_high = self.tiles(fz, z)
                z_low = self.tiles(fz, z, d=-1)
                if half:
                    z_low = [jnp.where(sub + z == 0, 0.0, t) for t in z_low]
            for k in range(self.nk):
                value = self.tiles(v, z, k) if v is not None else None
                image = None if base is None else self.tiles(base, z, k)
                parts = []
                if yz is not None:
                    below, above = self.tiles(v, z, k, -1), self.tiles(v, z, k, 1)
                    left, right = from_lower(value), from_higher(value)
                    parts.append([z_low[c] * below[c] + z_high[c] * above[c] for c in range(nc)])
                for x, w in xs:
                    near = self.tiles(w, z, k)
                    parts.append(near if x is None else [x[c] * near[c] for c in range(nc)])
                if yz is not None:
                    parts.append([y_low[c] * left[c] + y_high[c] * right[c] for c in range(nc)])
                for part in parts:
                    image = part if image is None else [p + q for p, q in zip(image, part)]
                if r is None:
                    for c in range(nc):
                        out.put(c, z, image[c], k)
                    continue
                result = [p * q for p, q in zip(image, self.tiles(r, z, k))]
                for c in range(nc):
                    out.put(c, z, result[c], k)
                if moment is not None:
                    self.add(moment, k, self.total(value, image))
                    self.add(moment + 1, k, self.total(result, image))

        self.sweep(half, body)

    def face_sum(self, v, side=None, yz=None, half=False):
        nc = self.dm.nc

        def body(z):
            x = self.tiles(side[0], z) if side is not None else None
            if yz is not None:
                y_high, z_high = self.tiles(yz[0], z), self.tiles(yz[1], z)
            for k in range(self.nk):
                value = self.tiles(v, z, k)
                parts = []
                if yz is not None:
                    above, right = self.tiles(v, z, k, 1), from_higher(value)
                    parts.append([z_high[c] * above[c] + y_high[c] * right[c] for c in range(nc)])
                if side is not None:
                    near = self.tiles(side[1], z, k)
                    parts.append([x[c] * near[c] for c in range(nc)])
                image = parts[0]
                if len(parts) == 2:
                    image = [p + q for p, q in zip(*parts)]
                self.add(5, k, 2.0 * self.total(value, image))

        self.sweep(half, body)


def stack(dm, ref, planes):
    return {p: Plane(ref, PAD + n * dm.slot, dm.nz) for n, p in enumerate(planes)}


def clear_pads(dm, nk, ref):
    for n in range((ref.shape[1] - PAD) // dm.slot + 1):
        for k in range(nk):
            ref[k, n * dm.slot : n * dm.slot + PAD, :] = jnp.zeros((PAD, LANES), jnp.float32)


def halo_planes(dm, ref, st):
    planes = {n: Plane(ref, dm.at[n], dm.nz) for n in ("fz1", "d1", "x1", "fy1", "d2", "fx2", "b1", "b2")}
    for n in ("fy2", "d3", "g3"):
        planes[n] = Plane(ref, dm.at[n], dm.half, st.zs)
    planes["fz2"] = Plane(ref, dm.at["fz2"], dm.more, st.zm)
    return planes


def near_body(
    dm, nk, cx, cy, cz, kappa, b, from_in, shifts,
    coef, w0a, w1a, w2a, part1, part2, acc,
    raw, temp, extra, w0h, w1h, w2h, inv, sems,
):
    par = lax.rem(lax.axis_index("slab"), 2)
    nl, nc, nz = dm.nl, dm.nc, dm.nz
    last = nl - 1
    load_own((cx, cy, cz, kappa, b), raw, sems)
    prepare(dm, par, *raw, [coef.at[n] for n in range(5)] + [temp])
    bf, df, xf, yf, zf = [own_planes(dm, coef.at[n]) for n in range(5)]
    st = Steps(dm, nk, par, acc, shifts)
    hp = halo_planes(dm, from_in, st)
    acc[...] = jnp.zeros(acc.shape, jnp.float32)
    for ref in (w0a, w1a, w2a, w0h, w1h, w2h):
        clear_pads(dm, nk, ref)
    d_next = Plane(extra, 0, nz)
    raw0 = Plane(coef.at[5], PAD, nz)

    def edges(z):
        for c in range(nc):
            here, there = xf[last].get(c, z), hp["x1"].get(c, z)
            raw0.put(c, z, xf[0].get(c, z))
            df[last].put(c, z, df[last].get(c, z) + 0.5 * there)
            d_next.put(c, z, hp["d1"].get(c, z) + 0.5 * here)
            for p in range(last):
                xf[p].put(c, z, 0.5 * (xf[p].get(c, z) + xf[p + 1].get(c, z)))
            xf[last].put(c, z, 0.5 * (here + there))

    blocks(0, nz, edges)

    W0 = stack(dm, w0a, range(1, nl)) | stack(dm, w0h, (nl, nl + 1))
    far = Plane(w0h, PAD + 2 * dm.slot, dm.half, st.zs)
    W1 = stack(dm, w1a, range(2, nl)) | stack(dm, w1h, (nl,))
    W1[nl + 1] = Plane(w1h, PAD + dm.slot, nz)
    W2 = stack(dm, w2a, range(3, nl)) | stack(dm, w2h, (nl,))
    R = stack(dm, inv, range(1, nl + 2))
    I1, I2 = Plane(part1, 0, nz), Plane(part2, 0, nz)

    for p in range(1, nl):
        st.start(df[p], bf[p], W0[p], R[p], own=True)
    st.start(d_next, hp["b1"], W0[nl], R[nl])
    st.start(hp["d2"], hp["b2"], W0[nl + 1], R[nl + 1])
    st.start(hp["d3"], hp["g3"], far, half=True)

    yz = [(yf[p], zf[p]) for p in range(nl)]
    st.apply(W0[1], [(xf[1], W0[2])], I1, yz=yz[1])
    for p in range(2, nl):
        st.apply(W0[p], [(xf[p - 1], W0[p - 1]), (xf[p], W0[p + 1])], W1[p], R[p], yz[p], moment=1)
    st.apply(
        W0[nl], [(xf[last], W0[last]), (hp["fx2"], W0[nl + 1])], W1[nl], R[nl], (hp["fy1"], hp["fz1"])
    )
    st.apply(
        W0[nl + 1], [(hp["fx2"], W0[nl]), (None, far)], W1[nl + 1], R[nl + 1],
        (hp["fy2"], hp["fz2"]), half=True,
    )
    st.apply(W1[2], [(xf[2], W1[3])], I2, yz=yz[2])
    for p in range(3, nl):
        st.apply(W1[p], [(xf[p - 1], W1[p - 1]), (xf[p], W1[p + 1])], W2[p], R[p], yz[p], moment=3)
    st.apply(
        W1[nl], [(xf[last], W1[last]), (hp["fx2"], W1[nl + 1])], W2[nl], R[nl],
        (hp["fy1"], hp["fz1"]), half=True,
    )
    for p in range(3, nl):
        st.face_sum(W2[p], None if p == last else (xf[p], W2[p + 1]), yz[p])
    st.face_sum(W2[last], (xf[last], W2[nl]), half=True)


def far_body(
    dm, nk, coef, w0a, w1a, w2a, part1, part2, acc_in, from_off, shifts,
    w0b, w1b, w2b, moments, acc, extra, w0h, w1h, w2h, inv,
):
    index = lax.axis_index("slab")
    par = lax.rem(index, 2)
    has_off = jnp.where(jnp.logical_and(index > 0, index < lax.axis_size("slab") - 1), 0.5, 0.0)
    nl, nc, nz = dm.nl, dm.nc, dm.nz
    bf, df, xf, yf, zf = [own_planes(dm, coef.at[n]) for n in range(5)]
    raw0 = Plane(coef.at[5], PAD, nz)
    st = Steps(dm, nk, par, acc, shifts)
    hp = halo_planes(dm, from_off, st)
    acc[...] = acc_in[...]
    for ref in (w0b, w1b, w2b, w0h, w1h, w2h):
        clear_pads(dm, nk, ref)
    d_here, d_next, x_edge = [Plane(extra.at[n], 0, nz) for n in range(3)]

    def edges(z):
        for c in range(nc):
            here, there = raw0.get(c, z), hp["x1"].get(c, z)
            d_here.put(c, z, df[0].get(c, z) + 0.5 * there)
            d_next.put(c, z, hp["d1"].get(c, z) + 0.5 * here)
            x_edge.put(c, z, has_off * (here + there))

    blocks(0, nz, edges)

    W0 = stack(dm, w0a, range(1, nl)) | stack(dm, w0b, (0,)) | stack(dm, w0h, (-1, -2))
    far = Plane(w0h, PAD + 2 * dm.slot, dm.half, st.zs)
    W1 = stack(dm, w1a, range(2, nl)) | stack(dm, w1b, (0, 1)) | stack(dm, w1h, (-1, -2))
    W2 = stack(dm, w2a, range(3, nl)) | stack(dm, w2b, (0, 1, 2)) | stack(dm, w2h, (-1,))
    R = stack(dm, inv, (-2, -1, 0, 1, 2))
    I1, I2 = Plane(part1, 0, nz), Plane(part2, 0, nz)
    yz = [(yf[p], zf[p]) for p in range(nl)]

    st.inverses(df[1], R[1])
    st.inverses(df[2], R[2])
    st.start(d_here, bf[0], W0[0], R[0], own=True)
    st.start(d_next, hp["b1"], W0[-1], R[-1])
    st.start(hp["d2"], hp["b2"], W0[-2], R[-2])
    st.start(hp["d3"], hp["g3"], far, half=True)

    st.apply(W0[1], [(xf[0], W0[0])], W1[1], R[1], base=I1, moment=1)
    st.apply(W0[0], [(x_edge, W0[-1]), (xf[0], W0[1])], W1[0], R[0], yz[0], moment=1)
    st.apply(
        W0[-1], [(hp["fx2"], W0[-2]), (x_edge, W0[0])], W1[-1], R[-1], (hp["fy1"], hp["fz1"])
    )
    st.apply(
        W0[-2], [(None, far), (hp["fx2"], W0[-1])], W1[-2], R[-2], (hp["fy2"], hp["fz2"]), half=True
    )
    st.apply(W1[2], [(xf[1], W1[1])], W2[2], R[2], base=I2, moment=3)
    st.apply(W1[1], [(xf[0], W1[0]), (xf[1], W1[2])], W2[1], R[1], yz[1], moment=3)
    st.apply(W1[0], [(x_edge, W1[-1]), (xf[0], W1[1])], W2[0], R[0], yz[0], moment=3)
    st.apply(
        W1[-1], [(hp["fx2"], W1[-2]), (x_edge, W1[0])], W2[-1], R[-1],
        (hp["fy1"], hp["fz1"]), half=True,
    )
    for p in range(min(3, nl - 1)):
        st.face_sum(W2[p], (xf[p], W2[p + 1]), yz[p])
    st.face_sum(W2[0], (x_edge, W2[-1]), half=True)

    number = 6 * nk
    sums = jnp.sum(acc[...].reshape(number, 8, LANES), axis=1)
    sums = jnp.concatenate([sums, jnp.zeros((LANES - number, LANES), jnp.float32)], axis=0)
    moments[...] = jnp.sum(jnp.transpose(sums), axis=0, keepdims=True)


def coefficients(sums, nk):
    nu = [sums] + [pltpu.roll(sums, LANES - j * nk, 1) for j in range(1, 6)]

    def inner(p, q, shift=0):
        total = None
        for i, x in enumerate(p):
            for j, y in enumerate(q):
                term = x * y * nu[i + j + shift]
                total = term if total is None else total + term
        return total

    one = jnp.ones((8, LANES), jnp.float32)
    zero = jnp.zeros((8, LANES), jnp.float32)
    z = [one]
    p = [one]
    x = [zero, zero, zero]
    norm = nu[0]
    for number in range(3):
        step = norm / (inner(p, p) - inner(p, p, 1))
        x = [x[j] + step * p[j] if j < len(p) else x[j] for j in range(3)]
        if number < 2:
            p, z = p + [zero], z + [zero]
            z = [z[j] - step * (p[j] - (p[j - 1] if j else zero)) for j in range(len(p))]
            norm_next = inner(z, z)
            beta = norm_next / norm
            p = [z[j] + beta * p[j] for j in range(len(z))]
            norm = norm_next
    return x


def combine_body(dm, nk, moments, weights, w0a, w0b, w1a, w1b, w2a, w2b, out):
    par = lax.rem(lax.axis_index("slab"), 2)
    nl, nc, nz = dm.nl, dm.nc, dm.nz
    sums = jnp.sum(moments[...].reshape(-1, LANES), axis=0, keepdims=True)
    x = coefficients(jnp.broadcast_to(sums, (8, LANES)), nk)
    scale = [
        [jnp.broadcast_to(x[j][:, k : k + 1] * weights[k], (8, LANES)) for k in range(nk)]
        for j in range(3)
    ]
    W0 = stack(dm, w0a, range(1, nl)) | stack(dm, w0b, (0,))
    W1 = stack(dm, w1a, range(2, nl)) | stack(dm, w1b, (0, 1))
    W2 = stack(dm, w2a, range(3, nl)) | stack(dm, w2b, (0, 1, 2))
    for p in range(nl):
        layer = jnp.where(par == 0, p, nl - 1 - p)

        def body(z, p=p, layer=layer):
            for c in range(nc):
                terms = [
                    scale[j][k] * w[p].get(c, z, k) for j, w in enumerate((W0, W1, W2)) for k in range(nk)
                ]
                while len(terms) > 1:
                    terms = [sum(terms[n : n + 2][1:], terms[n]) for n in range(0, len(terms), 2)]
                out[layer, pl.ds(z, 8), c * LANES : (c + 1) * LANES] = terms[0]

        blocks(0, nz, body)


def on_device(right_side, cond_x, cond_y, cond_z, kappa_sq, shifts, weights):
    dm = Dims(right_side.shape)
    nk = shifts.shape[0]
    nl = dm.nl
    count = lax.axis_size("slab")
    f32 = jnp.float32
    vmem = pl.BlockSpec(memory_space=pltpu.VMEM)
    smem = pl.BlockSpec(memory_space=pltpu.SMEM)
    anywhere = pl.BlockSpec(memory_space=pl.ANY)

    def params(mib):
        return pltpu.CompilerParams(vmem_limit_bytes=mib * MIB)

    def shape(*dims):
        return jax.ShapeDtypeStruct(dims, f32)

    def stacked(slots):
        return (nk, dm.stack_rows(slots), LANES)

    own = (dm.stack_rows(nl), LANES)
    raw = [pltpu.VMEM(right_side.shape, f32)] * 5
    sent = shape(dm.sent, LANES)
    inputs = (cond_x, cond_y, cond_z, kappa_sq, right_side)
    to_off, to_in = pl.pallas_call(
        functools.partial(pack_body, dm),
        out_shape=(sent, sent),
        in_specs=[anywhere] * 5,
        out_specs=(anywhere, anywhere),
        scratch_shapes=[
            raw,
            [pltpu.VMEM(own, f32)] * 6,
            pltpu.VMEM((2 * dm.plane, LANES), f32),
            pltpu.VMEM((2 * dm.nc * dm.half, LANES), f32),
            pltpu.VMEM((PAD, LANES), f32),
            pltpu.SemaphoreType.DMA((5,)),
            pltpu.SemaphoreType.DMA((2 * (10 + 3 * dm.nc),)),
        ],
        compiler_params=params(16),
        name="pack",
    )(*inputs)

    from_off = lax.ppermute(
        to_off,
        "slab",
        [pair for i in range(1, count - 1, 2) for pair in ((i, i + 1), (i + 1, i))],
    )
    from_in = lax.ppermute(to_in, "slab", [(i, i ^ 1) for i in range(count)])

    plane_stack = shape(nk, dm.plane, LANES)
    near_shapes = (
        shape(6, *own), shape(*stacked(nl - 1)), shape(*stacked(nl - 2)), shape(*stacked(nl - 3)),
        plane_stack, plane_stack, shape(6 * nk * 8, LANES),
    )
    near = pl.pallas_call(
        functools.partial(near_body, dm, nk),
        out_shape=near_shapes,
        in_specs=[anywhere] * 5 + [vmem, smem],
        out_specs=(vmem,) * 7,
        scratch_shapes=[
            raw,
            pltpu.VMEM(own, f32),
            pltpu.VMEM((dm.plane, LANES), f32),
            pltpu.VMEM(stacked(3), f32),
            pltpu.VMEM(stacked(2), f32),
            pltpu.VMEM(stacked(1), f32),
            pltpu.VMEM(stacked(nl + 1), f32),
            pltpu.SemaphoreType.DMA((5,)),
        ],
        compiler_params=params(36),
        cost_estimate=pl.CostEstimate(flops=10**7, bytes_accessed=30 * 10**6, transcendentals=0),
        name="near",
    )(*inputs, from_in, shifts)
    coef, w0a, w1a, w2a, part1, part2, acc = near

    w0b, w1b, w2b, moments = pl.pallas_call(
        functools.partial(far_body, dm, nk),
        out_shape=(shape(*stacked(1)), shape(*stacked(2)), shape(*stacked(3)), shape(1, LANES)),
        in_specs=[vmem] * 8 + [smem],
        out_specs=(vmem,) * 4,
        scratch_shapes=[
            pltpu.VMEM((6 * nk * 8, LANES), f32),
            pltpu.VMEM((3, dm.plane, LANES), f32),
            pltpu.VMEM(stacked(3), f32),
            pltpu.VMEM(stacked(2), f32),
            pltpu.VMEM(stacked(1), f32),
            pltpu.VMEM(stacked(5), f32),
        ],
        compiler_params=params(36),
        name="far",
    )(*near, from_off, shifts)

    everywhere = jnp.broadcast_to(moments[None], (count, 1, LANES))
    gathered = lax.all_to_all(everywhere, "slab", 0, 0)

    return pl.pallas_call(
        functools.partial(combine_body, dm, nk),
        out_shape=jax.ShapeDtypeStruct(right_side.shape, f32),
        in_specs=[vmem, smem] + [vmem] * 6,
        out_specs=vmem,
        compiler_params=params(20),
        name="combine",
    )(gathered, weights, w0a, w0b, w1a, w1b, w2a, w2b)


def solution(mesh):
    return jax.shard_map(
        on_device,
        mesh=mesh,
        in_specs=(
            P(("field", "slab"), None, None),
            P("slab", None, None),
            P("slab", None, None),
            P("slab", None, None),
            P("slab", None, None),
            P(),
            P(),
        ),
        out_specs=P(("field", "slab"), None, None),
        check_vma=False,
    )
```

```python
import functools
import jax
import jax.numpy as jnp
from jax import lax
from jax.experimental import pallas as pl
from jax.experimental.pallas import tpu as pltpu
from jax.sharding import PartitionSpec as P

LANES = 128
PAD = 8
MIB = 1024 * 1024


class Dims:
    def __init__(self, shape):
        self.nl, self.nz, self.ny = shape
        self.nc = self.ny // LANES
        self.plane = self.nc * self.nz
        self.slot = self.plane + PAD
        self.half = self.nz // 2
        self.more = self.half + 8
        full, half = self.plane, self.nc * self.half
        faces_yz = [("pad", PAD), ("fz1", full), ("fy1", full)]
        faces_x = [("gap", PAD), ("fx2", full), ("d2", full)]
        edge = [("x1", full), ("d1", full), ("b1", full), ("b2", full)]
        rest = [("fy2", half), ("d3", half), ("g3", half), ("fz2", self.nc * self.more)]
        self.at_yz, self.rows_yz = self.layout(faces_yz)
        self.at_x, self.rows_x = self.layout(faces_x)
        self.at_edge, self.rows_edge = self.layout(edge)
        self.at_rest, self.rows_rest = self.layout(rest)
        self.at_all, self.rows_all = self.layout(faces_yz + faces_x + edge + rest)

    @staticmethod
    def layout(parts):
        at, total = {}, 0
        for name, rows in parts:
            at[name] = total
            total += rows
        return at, total

    def stack_rows(self, slots):
        return slots * self.slot + PAD


class Plane:
    def __init__(self, ref, base, stride, zoff=0):
        self.ref, self.base, self.stride, self.zoff = ref, base, stride, zoff

    def row(self, c, z):
        return pl.multiple_of(z - self.zoff, 8) + (self.base + c * self.stride)

    def get(self, c, z, k=None, d=0):
        rows = pl.ds(self.row(c, z) + d, 8)
        return self.ref[rows, :] if k is None else self.ref[k, rows, :]

    def put(self, c, z, value, k=None):
        rows = pl.ds(self.row(c, z), 8)
        if k is None:
            self.ref[rows, :] = value
        else:
            self.ref[k, rows, :] = value


def lane_ids():
    return lax.broadcasted_iota(jnp.int32, (8, LANES), 1)


def row_ids():
    return lax.broadcasted_iota(jnp.int32, (8, LANES), 0)


def from_higher(tiles):
    lane = lane_ids()
    n = len(tiles)
    return [
        pltpu.roll(jnp.where(lane == 0, tiles[(c + 1) % n], tiles[c]), LANES - 1, 1)
        for c in range(n)
    ]


def from_lower(tiles):
    lane = lane_ids()
    n = len(tiles)
    return [
        pltpu.roll(jnp.where(lane == LANES - 1, tiles[(c - 1) % n], tiles[c]), 1, 1)
        for c in range(n)
    ]


def blocks(z_from, z_count, body, unroll=1):
    def step(n, carry):
        for u in range(unroll):
            body(pl.multiple_of(z_from + (n * unroll + u) * 8, 8))
        return carry

    lax.fori_loop(0, z_count // (8 * unroll), step, 0)


def own_planes(dm, ref):
    return [Plane(ref, PAD + p * dm.slot, dm.nz) for p in range(dm.nl)]


def prepare(dm, par, cx, cy, cz, kappa, b, flats):
    nc, nz, nl = dm.nc, dm.nz, dm.nl
    bf, df, xf, yf, zf, tf = [own_planes(dm, ref) for ref in flats]
    for ref in (flats[4], flats[5]):
        for p in range(nl + 1):
            ref[p * dm.slot : p * dm.slot + PAD, :] = jnp.zeros((PAD, LANES), jnp.float32)
    layers = [jnp.where(par == 0, p, nl - 1 - p) for p in range(nl)]

    def copy(z):
        for p in range(nl):
            for src, dst in ((b, bf), (cx, xf), (cz, tf)):
                block = src[layers[p], pl.ds(z, 8), :]
                for c in range(nc):
                    dst[p].put(c, z, block[:, c * LANES : (c + 1) * LANES])

    blocks(0, nz, copy)

    def faces(p, z):
        lane, sub = lane_ids(), row_ids()
        conds = cy[layers[p], pl.ds(z, 8), :]
        kap = kappa[layers[p], pl.ds(z, 8), :]
        ys = [conds[:, c * LANES : (c + 1) * LANES] for c in range(nc)]
        up, down = from_higher(ys), from_lower(ys)
        up[-1] = jnp.where(lane == LANES - 1, 0.0, up[-1])
        down[0] = jnp.where(lane == 0, 0.0, down[0])
        for c in range(nc):
            high_y = 0.5 * (ys[c] + up[c])
            low_y = 0.5 * (ys[c] + down[c])
            here = tf[p].get(c, z)
            high_z = 0.5 * (here + jnp.where(sub + z == nz - 1, 0.0, tf[p].get(c, z, d=1)))
            low_z = 0.5 * (here + jnp.where(sub + z == 0, 0.0, tf[p].get(c, z, d=-1)))
            mine = xf[p].get(c, z)
            total = kap[:, c * LANES : (c + 1) * LANES]
            total = total + 0.5 * (mine + xf[p - 1].get(c, z) if p > 0 else mine)
            total = total + 0.5 * (mine + xf[p + 1].get(c, z) if p < nl - 1 else mine)
            df[p].put(c, z, total + low_z + high_z + low_y + high_y)
            if c == nc - 1:
                high_y = jnp.where(lane == LANES - 1, 0.0, high_y)
            yf[p].put(c, z, high_y)
            zf[p].put(c, z, jnp.where(sub + z == nz - 1, 0.0, high_z))

    def all_faces(z):
        for p in range(nl):
            faces(p, z)

    blocks(0, nz, all_faces)


def pack_body(
    dm, conds, cz, kappa, b, to_swap, to_edge, to_rest, to_in, coef, temp,
):
    par = lax.rem(lax.axis_index("slab"), 2)
    side_field = lax.rem(lax.axis_index("field"), 2)
    nc, nz, nl = dm.nc, dm.nz, dm.nl
    raw = [conds.at[0], conds.at[1], cz, kappa, b]
    prepare(dm, par, *raw, [coef.at[n] for n in range(5)] + [temp])
    bf, df, xf, yf, zf = [own_planes(dm, coef.at[n]) for n in range(5)]
    zs = pl.multiple_of((1 - par) * dm.half, 8)
    zm = pl.multiple_of((1 - par) * (nz - dm.more), 8)

    def x_face(c, z, one, two):
        return 0.5 * (xf[one].get(c, z) + xf[two].get(c, z))

    def fill(out, at, z_count, sources):
        def body(n):
            for name, value in sources:
                for c in range(nc):
                    out[pl.ds(pl.multiple_of(n, 8) + (at[name] + c * z_count), 8), :] = value(c, n)

        blocks(0, z_count, body, min(4, z_count // 8) if z_count % 32 == 0 else 1)

    def edge(out, at, one, two):
        fill(out, at, nz, [
            ("x1", lambda c, n: xf[one].get(c, n)),
            ("d1", lambda c, n: df[one].get(c, n)),
            ("b1", lambda c, n: bf[one].get(c, n)),
            ("b2", lambda c, n: bf[two].get(c, n)),
        ])

    def rest(out, at, two, three):
        fill(out, at, dm.half, [
            ("fy2", lambda c, n: yf[two].get(c, zs + n)),
            ("d3", lambda c, n: df[three].get(c, zs + n)),
            ("g3", lambda c, n: x_face(c, zs + n, two, three) * bf[three].get(c, zs + n)),
        ])
        fill(out, at, dm.more, [("fz2", lambda c, n: zf[two].get(c, zm + n))])

    def yz(out, at, one):
        out[at["pad"] : at["pad"] + PAD, :] = jnp.zeros((PAD, LANES), jnp.float32)
        fill(out, at, nz, [
            ("fz1", lambda c, n: zf[one].get(c, n)),
            ("fy1", lambda c, n: yf[one].get(c, n)),
        ])

    def x(out, at, one, two):
        out[at["gap"] : at["gap"] + PAD, :] = jnp.zeros((PAD, LANES), jnp.float32)
        fill(out, at, nz, [
            ("fx2", lambda c, n: x_face(c, n, one, two)),
            ("d2", lambda c, n: df[two].get(c, n)),
        ])

    @pl.when(side_field == 0)
    def _():
        yz(to_swap, dm.at_yz, 0)

    @pl.when(side_field == 1)
    def _():
        x(to_swap, dm.at_x, 0, 1)

    edge(to_edge, dm.at_edge, 0, 1)
    rest(to_rest, dm.at_rest, 1, 2)
    last = nl - 1
    yz(to_in, dm.at_all, last)
    x(to_in, dm.at_all, last, last - 1)
    edge(to_in, dm.at_all, last, last - 1)
    rest(to_in, dm.at_all, last - 1, last - 2)


class Steps:
    def __init__(self, dm, nk, par, acc, shifts):
        self.dm, self.nk, self.acc, self.shifts = dm, nk, acc, shifts
        self.zs = pl.multiple_of(par * dm.half, 8)
        self.zm = pl.multiple_of(par * (dm.nz - dm.more), 8)

    def sweep(self, half, body, unroll=4):
        if half:
            blocks(self.zs, self.dm.half, body, unroll)
        else:
            blocks(0, self.dm.nz, body, unroll)

    def add(self, j, k, value):
        at = (j * self.nk + k) * 8
        self.acc[at : at + 8, :] += value

    def total(self, first, second):
        return functools.reduce(jnp.add, [p * q for p, q in zip(first, second)])

    def tiles(self, plane, z, k=None, d=0):
        return [plane.get(c, z, k, d) for c in range(self.dm.nc)]

    def start(self, d, b, w, r=None, half=False, own=False):
        def body(z):
            diagonal, rhs = self.tiles(d, z), self.tiles(b, z)
            for k in range(self.nk):
                s = self.shifts[k]
                inverse = [1.0 / (t + s) for t in diagonal]
                value = [x * y for x, y in zip(rhs, inverse)]
                for c in range(self.dm.nc):
                    if r is not None:
                        r.put(c, z, inverse[c], k)
                    w.put(c, z, value[c], k)
                if own:
                    self.add(0, k, self.total(rhs, value))

        self.sweep(half, body, 2)

    def apply(self, v, sides, out, r=None, yz=None, base=None, half=False, moment=None):
        nc = self.dm.nc

        def body(z):
            xs = [(None if x is None else self.tiles(x, z), w) for x, w in sides]
            if yz is not None:
                fy, fz = yz
                lane, sub = lane_ids(), row_ids()
                y_high = self.tiles(fy, z)
                y_low = from_lower(y_high)
                y_low[0] = jnp.where(lane == 0, 0.0, y_low[0])
                z_high = self.tiles(fz, z)
                z_low = self.tiles(fz, z, d=-1)
                if half:
                    z_low = [jnp.where(sub + z == 0, 0.0, t) for t in z_low]
            for k in range(self.nk):
                value = self.tiles(v, z, k) if v is not None else None
                image = None if base is None else self.tiles(base, z, k)
                parts = []
                if yz is not None:
                    below, above = self.tiles(v, z, k, -1), self.tiles(v, z, k, 1)
                    left, right = from_lower(value), from_higher(value)
                    parts.append([z_low[c] * below[c] + z_high[c] * above[c] for c in range(nc)])
                for x, w in xs:
                    near = self.tiles(w, z, k)
                    parts.append(near if x is None else [x[c] * near[c] for c in range(nc)])
                if yz is not None:
                    parts.append([y_low[c] * left[c] + y_high[c] * right[c] for c in range(nc)])
                for part in parts:
                    image = part if image is None else [p + q for p, q in zip(image, part)]
                if r is None:
                    for c in range(nc):
                        out.put(c, z, image[c], k)
                    continue
                result = [p * q for p, q in zip(image, self.tiles(r, z, k))]
                for c in range(nc):
                    out.put(c, z, result[c], k)
                if moment is not None:
                    self.add(moment, k, self.total(value, image))
                    self.add(moment + 1, k, self.total(result, image))

        self.sweep(half, body)

    def face_sum(self, v, side=None, yz=None, half=False):
        nc = self.dm.nc

        def body(z):
            x = self.tiles(side[0], z) if side is not None else None
            if yz is not None:
                y_high, z_high = self.tiles(yz[0], z), self.tiles(yz[1], z)
            for k in range(self.nk):
                value = self.tiles(v, z, k)
                parts = []
                if yz is not None:
                    above, right = self.tiles(v, z, k, 1), from_higher(value)
                    parts.append([z_high[c] * above[c] + y_high[c] * right[c] for c in range(nc)])
                if side is not None:
                    near = self.tiles(side[1], z, k)
                    parts.append([x[c] * near[c] for c in range(nc)])
                image = parts[0]
                if len(parts) == 2:
                    image = [p + q for p, q in zip(*parts)]
                self.add(5, k, 2.0 * self.total(value, image))

        self.sweep(half, body)


def stack(dm, ref, planes):
    return {p: Plane(ref, PAD + n * dm.slot, dm.nz) for n, p in enumerate(planes)}


def clear_pads(dm, nk, ref):
    for n in range((ref.shape[1] - PAD) // dm.slot + 1):
        for k in range(nk):
            ref[k, n * dm.slot : n * dm.slot + PAD, :] = jnp.zeros((PAD, LANES), jnp.float32)


def halo_planes(dm, st, *parts):
    planes = {}
    for ref, at in parts:
        for name, row in at.items():
            if name in ("fy2", "d3", "g3"):
                planes[name] = Plane(ref, row, dm.half, st.zs)
            elif name == "fz2":
                planes[name] = Plane(ref, row, dm.more, st.zm)
            else:
                planes[name] = Plane(ref, row, dm.nz)
    return planes


def near_body(
    dm, nk, flats, from_in, shifts, w0a, w1a, w2a, part1, part2, acc, coef, inv_out,
    extra, w0h, w1h, w2h, inv,
):
    par = lax.rem(lax.axis_index("slab"), 2)
    nl, nc, nz = dm.nl, dm.nc, dm.nz
    last = nl - 1
    bf, df, raw_x, yf, zf = [own_planes(dm, flats.at[n]) for n in range(5)]
    xf = own_planes(dm, coef)
    st = Steps(dm, nk, par, acc, shifts)
    hp = halo_planes(dm, st, (from_in, dm.at_all))
    acc[...] = jnp.zeros(acc.shape, jnp.float32)
    for ref in (w0a, w1a, w2a, w0h, w1h, w2h):
        clear_pads(dm, nk, ref)
    d_last, d_next = Plane(extra.at[0], 0, nz), Plane(extra.at[1], 0, nz)

    def edges(z):
        for c in range(nc):
            here, there = raw_x[last].get(c, z), hp["x1"].get(c, z)
            d_last.put(c, z, df[last].get(c, z) + 0.5 * there)
            d_next.put(c, z, hp["d1"].get(c, z) + 0.5 * here)
            for p in range(last):
                xf[p].put(c, z, 0.5 * (raw_x[p].get(c, z) + raw_x[p + 1].get(c, z)))
            xf[last].put(c, z, 0.5 * (here + there))

    blocks(0, nz, edges, 2)
    df[last] = d_last

    W0 = stack(dm, w0a, range(1, nl)) | stack(dm, w0h, (nl, nl + 1))
    far = Plane(w0h, PAD + 2 * dm.slot, dm.half, st.zs)
    W1 = stack(dm, w1a, range(2, nl)) | stack(dm, w1h, (nl,))
    W1[nl + 1] = Plane(w1h, PAD + dm.slot, nz)
    W2 = stack(dm, w2a, range(3, nl)) | stack(dm, w2h, (nl,))
    R = stack(dm, inv_out, (1, 2)) | stack(dm, inv, range(3, nl + 2))
    I1, I2 = Plane(part1, 0, nz), Plane(part2, 0, nz)

    for p in range(1, nl):
        st.start(df[p], bf[p], W0[p], R[p], own=True)
    st.start(d_next, hp["b1"], W0[nl], R[nl])
    st.start(hp["d2"], hp["b2"], W0[nl + 1], R[nl + 1])
    st.start(hp["d3"], hp["g3"], far, half=True)

    yz = [(yf[p], zf[p]) for p in range(nl)]
    st.apply(W0[1], [(xf[1], W0[2])], I1, yz=yz[1])
    for p in range(2, nl):
        st.apply(W0[p], [(xf[p - 1], W0[p - 1]), (xf[p], W0[p + 1])], W1[p], R[p], yz[p], moment=1)
    st.apply(
        W0[nl], [(xf[last], W0[last]), (hp["fx2"], W0[nl + 1])], W1[nl], R[nl], (hp["fy1"], hp["fz1"])
    )
    st.apply(
        W0[nl + 1], [(hp["fx2"], W0[nl]), (None, far)], W1[nl + 1], R[nl + 1],
        (hp["fy2"], hp["fz2"]), half=True,
    )
    st.apply(W1[2], [(xf[2], W1[3])], I2, yz=yz[2])
    for p in range(3, nl):
        st.apply(W1[p], [(xf[p - 1], W1[p - 1]), (xf[p], W1[p + 1])], W2[p], R[p], yz[p], moment=3)
    st.apply(
        W1[nl], [(xf[last], W1[last]), (hp["fx2"], W1[nl + 1])], W2[nl], R[nl],
        (hp["fy1"], hp["fz1"]), half=True,
    )
    for p in range(3, nl):
        st.face_sum(W2[p], None if p == last else (xf[p], W2[p + 1]), yz[p])
    st.face_sum(W2[last], (xf[last], W2[nl]), half=True)


def far_a_body(
    dm, nk, flats, coef, w0a, w1a, w2a, part1, part2, acc_in, inv, from_edge, shifts,
    w0b, w1b, w2b, part3, acc, edge, w0h, inv_out,
):
    index = lax.axis_index("slab")
    par = lax.rem(index, 2)
    has_off = jnp.where(jnp.logical_and(index > 0, index < lax.axis_size("slab") - 1), 0.5, 0.0)
    nl, nc, nz = dm.nl, dm.nc, dm.nz
    bf, df, raw_x, yf, zf = [own_planes(dm, flats.at[n]) for n in range(5)]
    xf = own_planes(dm, coef)
    st = Steps(dm, nk, par, acc, shifts)
    hp = halo_planes(dm, st, (from_edge, dm.at_edge))
    acc[...] = acc_in[...]
    for ref in (w0b, w1b, w2b, w0h):
        clear_pads(dm, nk, ref)
    d_here, d_next, x_edge = [Plane(edge.at[n], 0, nz) for n in range(3)]

    def edges(z):
        for c in range(nc):
            here, there = raw_x[0].get(c, z), hp["x1"].get(c, z)
            d_here.put(c, z, df[0].get(c, z) + 0.5 * there)
            d_next.put(c, z, hp["d1"].get(c, z) + 0.5 * here)
            x_edge.put(c, z, has_off * (here + there))

    blocks(0, nz, edges, 4)

    W0 = stack(dm, w0a, range(1, nl)) | stack(dm, w0b, (0,)) | stack(dm, w0h, (-1,))
    W1 = stack(dm, w1a, range(2, nl)) | stack(dm, w1b, (0, 1))
    W2 = stack(dm, w2a, range(3, nl)) | stack(dm, w2b, (1, 2))
    R = stack(dm, inv_out, (-1, 0)) | stack(dm, inv, (1, 2))
    I1, I2, I3 = Plane(part1, 0, nz), Plane(part2, 0, nz), Plane(part3, 0, nz)
    yz = [(yf[p], zf[p]) for p in range(nl)]

    st.start(d_here, bf[0], W0[0], R[0], own=True)
    st.start(d_next, hp["b1"], W0[-1], R[-1])

    st.apply(W0[1], [(xf[0], W0[0])], W1[1], R[1], base=I1, moment=1)
    st.apply(W0[0], [(x_edge, W0[-1]), (xf[0], W0[1])], W1[0], R[0], yz[0], moment=1)
    st.apply(W1[2], [(xf[1], W1[1])], W2[2], R[2], base=I2, moment=3)
    st.apply(W1[1], [(xf[0], W1[0]), (xf[1], W1[2])], W2[1], R[1], yz[1], moment=3)
    st.apply(W1[0], [(xf[0], W1[1])], I3, yz=yz[0])
    for p in range(1, min(3, nl - 1)):
        st.face_sum(W2[p], (xf[p], W2[p + 1]), yz[p])


def far_b_body(
    dm, nk, flats, coef, w0b, w0h, w1b, w2b, part3, acc_in, edge, inv_in, from_edge, swap_a, swap_b, shifts,
    w2c, acc, w1h, inv_out, w0f, shared,
):
    par = lax.rem(lax.axis_index("slab"), 2)
    side_field = lax.rem(lax.axis_index("field"), 2)
    nl, nc, nz = dm.nl, dm.nc, dm.nz
    bf, df, raw_x, yf, zf = [own_planes(dm, flats.at[n]) for n in range(5)]
    xf = own_planes(dm, coef)
    st = Steps(dm, nk, par, acc, shifts)

    @pl.when(side_field == 0)
    def _():
        shared[0 : dm.rows_yz, :] = swap_a[...]
        shared[dm.rows_yz :, :] = swap_b[...]

    @pl.when(side_field == 1)
    def _():
        shared[0 : dm.rows_yz, :] = swap_b[...]
        shared[dm.rows_yz :, :] = swap_a[...]

    at_x = {name: row + dm.rows_yz for name, row in dm.at_x.items()}
    hp = halo_planes(dm, st, (from_edge, dm.at_edge), (shared, dm.at_yz), (shared, at_x))
    acc[...] = acc_in[...]
    for ref in (w2c, w1h, w0f):
        clear_pads(dm, nk, ref)
    x_edge = Plane(edge.at[2], 0, nz)
    W0 = stack(dm, w0b, (0,)) | stack(dm, w0h, (-1,)) | stack(dm, w0f, (-2,))
    W1 = stack(dm, w1b, (0, 1)) | stack(dm, w1h, (-1,))
    W2 = stack(dm, w2b, (1, 2)) | stack(dm, w2c, (0,))
    R = stack(dm, inv_in, (-1, 0)) | stack(dm, inv_out, (-2,))
    st.start(hp["d2"], hp["b2"], W0[-2], R[-2])
    st.apply(
        W0[-1], [(hp["fx2"], W0[-2]), (x_edge, W0[0])], W1[-1], R[-1], (hp["fy1"], hp["fz1"])
    )
    st.apply(W1[0], [(x_edge, W1[-1])], W2[0], R[0], base=Plane(part3, 0, nz), moment=3)
    st.face_sum(W2[0], (xf[0], W2[1]), (yf[0], zf[0]))


def far_c_body(
    dm, nk, w0h, w0f, w1b, w1h, w2c, acc_in, edge, inv_in, inv2, from_rest, shared, shifts,
    moments, acc, w0g, w1g, w2g,
):
    par = lax.rem(lax.axis_index("slab"), 2)
    nz = dm.nz
    st = Steps(dm, nk, par, acc, shifts)
    at_x = {name: row + dm.rows_yz for name, row in dm.at_x.items()}
    hp = halo_planes(dm, st, (from_rest, dm.at_rest), (shared, dm.at_yz), (shared, at_x))
    acc[...] = acc_in[...]
    x_edge = Plane(edge.at[2], 0, nz)
    far, near, w2 = [Plane(ref, 0, dm.half, st.zs) for ref in (w0g, w1g, w2g)]
    W0 = stack(dm, w0h, (-1,)) | stack(dm, w0f, (-2,))
    W1 = stack(dm, w1b, (0, 1)) | stack(dm, w1h, (-1,))
    W2 = stack(dm, w2c, (0,))
    R = stack(dm, inv_in, (-1, 0)) | stack(dm, inv2, (-2,))
    st.start(hp["d3"], hp["g3"], far, half=True)
    st.apply(
        W0[-2], [(None, far), (hp["fx2"], W0[-1])], near, R[-2], (hp["fy2"], hp["fz2"]), half=True
    )
    st.apply(
        W1[-1], [(hp["fx2"], near), (x_edge, W1[0])], w2, R[-1], (hp["fy1"], hp["fz1"]), half=True
    )
    st.face_sum(W2[0], (x_edge, w2), half=True)

    number = 6 * nk
    sums = jnp.sum(acc[...].reshape(number, 8, LANES), axis=1)
    sums = jnp.concatenate([sums, jnp.zeros((LANES - number, LANES), jnp.float32)], axis=0)
    moments[...] = jnp.sum(jnp.transpose(sums), axis=0, keepdims=True)


def coefficients(sums, nk):
    nu = [sums] + [pltpu.roll(sums, LANES - j * nk, 1) for j in range(1, 6)]

    def inner(p, q, shift=0):
        total = None
        for i, x in enumerate(p):
            for j, y in enumerate(q):
                term = x * y * nu[i + j + shift]
                total = term if total is None else total + term
        return total

    one = jnp.ones((8, LANES), jnp.float32)
    zero = jnp.zeros((8, LANES), jnp.float32)
    z = [one]
    p = [one]
    x = [zero, zero, zero]
    norm = nu[0]
    for number in range(3):
        step = norm / (inner(p, p) - inner(p, p, 1))
        x = [x[j] + step * p[j] if j < len(p) else x[j] for j in range(3)]
        if number < 2:
            p, z = p + [zero], z + [zero]
            z = [z[j] - step * (p[j] - (p[j - 1] if j else zero)) for j in range(len(p))]
            norm_next = inner(z, z)
            beta = norm_next / norm
            p = [z[j] + beta * p[j] for j in range(len(z))]
            norm = norm_next
    return x


def combine_body(dm, nk, moments, weights, w0a, w0b, w1a, w1b, w2a, w2b, w2c, out):
    par = lax.rem(lax.axis_index("slab"), 2)
    nl, nc, nz = dm.nl, dm.nc, dm.nz
    sums = jnp.sum(moments[...].reshape(-1, LANES), axis=0, keepdims=True)
    x = coefficients(jnp.broadcast_to(sums, (8, LANES)), nk)
    scale = [
        [jnp.broadcast_to(x[j][:, k : k + 1] * weights[k], (8, LANES)) for k in range(nk)]
        for j in range(3)
    ]
    W0 = stack(dm, w0a, range(1, nl)) | stack(dm, w0b, (0,))
    W1 = stack(dm, w1a, range(2, nl)) | stack(dm, w1b, (0, 1))
    W2 = stack(dm, w2a, range(3, nl)) | stack(dm, w2b, (1, 2)) | stack(dm, w2c, (0,))
    for p in range(nl):
        layer = jnp.where(par == 0, p, nl - 1 - p)

        def body(z, p=p, layer=layer):
            for c in range(nc):
                terms = [
                    scale[j][k] * w[p].get(c, z, k) for j, w in enumerate((W0, W1, W2)) for k in range(nk)
                ]
                while len(terms) > 1:
                    terms = [sum(terms[n : n + 2][1:], terms[n]) for n in range(0, len(terms), 2)]
                out[layer, pl.ds(z, 8), c * LANES : (c + 1) * LANES] = terms[0]

        blocks(0, nz, body)


def on_device(right_side, cond_x, cond_y, cond_z, kappa_sq, shifts, weights):
    dm = Dims(right_side.shape)
    nk = shifts.shape[0]
    nl = dm.nl
    count = lax.axis_size("slab")
    f32 = jnp.float32
    vmem = pl.BlockSpec(memory_space=pltpu.VMEM)
    smem = pl.BlockSpec(memory_space=pltpu.SMEM)

    def params(mib):
        return pltpu.CompilerParams(vmem_limit_bytes=mib * MIB)

    def shape(*dims):
        return jax.ShapeDtypeStruct(dims, f32)

    def stacked(slots):
        return (nk, dm.stack_rows(slots), LANES)

    own = (dm.stack_rows(nl), LANES)
    half_stack = pltpu.VMEM((nk, dm.nc * dm.half, LANES), f32)
    plane_stack = shape(nk, dm.plane, LANES)
    sums = shape(6 * nk * 8, LANES)
    assert dm.rows_yz == dm.rows_x

    to_swap, to_edge, to_rest, to_in, flats = pl.pallas_call(
        functools.partial(pack_body, dm),
        out_shape=(
            shape(dm.rows_yz, LANES), shape(dm.rows_edge, LANES), shape(dm.rows_rest, LANES),
            shape(dm.rows_all, LANES), shape(5, *own),
        ),
        in_specs=[vmem] * 4,
        out_specs=(vmem,) * 5,
        scratch_shapes=[
            pltpu.VMEM(own, f32),
        ],
        compiler_params=params(20),
        name="pack",
    )(jnp.stack([cond_x, cond_y]), cond_z, kappa_sq, right_side)

    outward = [pair for i in range(1, count - 1, 2) for pair in ((i, i + 1), (i + 1, i))]
    swap_a = lax.ppermute(to_swap, "slab", outward)
    from_edge = lax.ppermute(to_edge, "slab", outward)
    from_rest = lax.ppermute(to_rest, "slab", outward)
    from_in = lax.ppermute(to_in, "slab", [(i, i ^ 1) for i in range(count)])
    fields = lax.axis_size("field")

    def call(body, name, mib, results, scratch, operands, cost):
        return pl.pallas_call(
            functools.partial(body, dm, nk),
            out_shape=results,
            in_specs=[vmem] * len(operands) + [smem],
            out_specs=(vmem,) * len(results),
            scratch_shapes=scratch,
            compiler_params=params(mib),
            cost_estimate=pl.CostEstimate(
                flops=10**6, bytes_accessed=cost * 3 * 10**6, transcendentals=0
            ),
            name=name,
        )(*operands, shifts)

    def wide(slots):
        return shape(*stacked(slots))

    def held(slots):
        return pltpu.VMEM(stacked(slots), f32)

    w0a, w1a, w2a, part1, part2, acc, coef, inv12 = call(
        near_body, "near", 20,
        (wide(nl - 1), wide(nl - 2), wide(nl - 3), plane_stack, plane_stack, sums, shape(*own), wide(2)),
        [pltpu.VMEM((2, dm.plane, LANES), f32), held(3), held(2), held(1), held(nl - 1)],
        (flats, from_in), 10,
    )
    swap_a, acc = lax.optimization_barrier((swap_a, acc))
    swap_b = lax.ppermute(swap_a, "field", [(i, i ^ 1) for i in range(fields)])
    w0b, w1b, w2b, part3, acc, edge, w0h, inv = call(
        far_a_body, "far_a", 20,
        (wide(1), wide(2), wide(2), plane_stack, sums, shape(3, dm.plane, LANES), wide(1), wide(2)),
        [],
        (flats, coef, w0a, w1a, w2a, part1, part2, acc, inv12, from_edge), 6,
    )
    w2c, acc, w1h, inv2, w0f, shared = call(
        far_b_body, "far_b", 20,
        (wide(1), sums, wide(1), wide(1), wide(1), shape(dm.rows_yz + dm.rows_x, LANES)),
        [],
        (flats, coef, w0b, w0h, w1b, w2b, part3, acc, edge, inv, from_edge, swap_a, swap_b), 3,
    )
    moments, _ = call(
        far_c_body, "far_c", 20,
        (shape(1, LANES), sums),
        [half_stack] * 3,
        (w0h, w0f, w1b, w1h, w2c, acc, edge, inv, inv2, from_rest, shared), 2,
    )

    everywhere = jnp.broadcast_to(moments[None], (count, 1, LANES))
    gathered = lax.all_to_all(everywhere, "slab", 0, 0)

    return pl.pallas_call(
        functools.partial(combine_body, dm, nk),
        out_shape=jax.ShapeDtypeStruct(right_side.shape, f32),
        in_specs=[vmem, smem] + [vmem] * 7,
        out_specs=vmem,
        compiler_params=params(20),
        name="combine",
    )(gathered, weights, w0a, w0b, w1a, w1b, w2a, w2b, w2c)


def solution(mesh):
    return jax.shard_map(
        on_device,
        mesh=mesh,
        in_specs=(
            P(("field", "slab"), None, None),
            P("slab", None, None),
            P("slab", None, None),
            P("slab", None, None),
            P("slab", None, None),
            P(),
            P(),
        ),
        out_specs=P(("field", "slab"), None, None),
        check_vma=False,
    )
```

```python
import functools
import jax
import jax.numpy as jnp
from jax import lax
from jax.experimental import pallas as pl
from jax.experimental.pallas import tpu as pltpu
from jax.sharding import PartitionSpec as P

LANES = 128
PAD = 8
MIB = 1024 * 1024


class Dims:
    def __init__(self, shape):
        self.nl, self.nz, self.ny = shape
        self.nc = self.ny // LANES
        self.plane = self.nc * self.nz
        self.slot = self.plane + PAD
        self.half = self.nz // 2
        self.more = self.half + 8
        full, half = self.plane, self.nc * self.half
        faces_yz = [("pad", PAD), ("fz1", full), ("fy1", full)]
        faces_x = [("gap", PAD), ("fx2", full), ("d2", full)]
        first = [("x1", full)]
        edge = [("d1", full), ("b1", full), ("b2", full)]
        rest = [("fy2", half), ("d3", half), ("g3", half), ("fz2", self.nc * self.more)]
        self.at_yz, self.rows_yz = self.layout(faces_yz)
        self.at_x, self.rows_x = self.layout(faces_x)
        self.at_first, self.rows_first = self.layout([("swapped", self.rows_yz)] + first)
        self.at_edge, self.rows_edge = self.layout(edge)
        self.at_rest, self.rows_rest = self.layout(rest)
        self.at_all, self.rows_all = self.layout(faces_yz + faces_x + first + edge + rest)

    @staticmethod
    def layout(parts):
        at, total = {}, 0
        for name, rows in parts:
            at[name] = total
            total += rows
        return at, total

    def stack_rows(self, slots):
        return slots * self.slot + PAD


class Plane:
    def __init__(self, ref, base, stride, zoff=0):
        self.ref, self.base, self.stride, self.zoff = ref, base, stride, zoff

    def row(self, c, z):
        return pl.multiple_of(z - self.zoff, 8) + (self.base + c * self.stride)

    def get(self, c, z, k=None, d=0):
        rows = pl.ds(self.row(c, z) + d, 8)
        return self.ref[rows, :] if k is None else self.ref[k, rows, :]

    def put(self, c, z, value, k=None):
        rows = pl.ds(self.row(c, z), 8)
        if k is None:
            self.ref[rows, :] = value
        else:
            self.ref[k, rows, :] = value


def lane_ids():
    return lax.broadcasted_iota(jnp.int32, (8, LANES), 1)


def row_ids():
    return lax.broadcasted_iota(jnp.int32, (8, LANES), 0)


def from_higher(tiles):
    lane = lane_ids()
    n = len(tiles)
    return [
        pltpu.roll(jnp.where(lane == 0, tiles[(c + 1) % n], tiles[c]), LANES - 1, 1)
        for c in range(n)
    ]


def from_lower(tiles):
    lane = lane_ids()
    n = len(tiles)
    return [
        pltpu.roll(jnp.where(lane == LANES - 1, tiles[(c - 1) % n], tiles[c]), 1, 1)
        for c in range(n)
    ]


def blocks(z_from, z_count, body, unroll=1):
    def step(n, carry):
        for u in range(unroll):
            body(pl.multiple_of(z_from + (n * unroll + u) * 8, 8))
        return carry

    lax.fori_loop(0, z_count // (8 * unroll), step, 0)


def own_planes(dm, ref):
    return [Plane(ref, PAD + p * dm.slot, dm.nz) for p in range(dm.nl)]


def prepare(dm, par, cx, cy, cz, kappa, b, flats):
    nc, nz, nl = dm.nc, dm.nz, dm.nl
    bf, df, xf, yf, zf, tf = [own_planes(dm, ref) for ref in flats]
    for ref in (flats[4], flats[5]):
        for p in range(nl + 1):
            ref[p * dm.slot : p * dm.slot + PAD, :] = jnp.zeros((PAD, LANES), jnp.float32)
    layers = [jnp.where(par == 0, p, nl - 1 - p) for p in range(nl)]

    def copy(z):
        for p in range(nl):
            for src, dst in ((b, bf), (cx, xf), (cz, tf)):
                block = src[layers[p], pl.ds(z, 8), :]
                for c in range(nc):
                    dst[p].put(c, z, block[:, c * LANES : (c + 1) * LANES])

    blocks(0, nz, copy)

    def faces(p, z):
        lane, sub = lane_ids(), row_ids()
        conds = cy[layers[p], pl.ds(z, 8), :]
        kap = kappa[layers[p], pl.ds(z, 8), :]
        ys = [conds[:, c * LANES : (c + 1) * LANES] for c in range(nc)]
        up, down = from_higher(ys), from_lower(ys)
        up[-1] = jnp.where(lane == LANES - 1, 0.0, up[-1])
        down[0] = jnp.where(lane == 0, 0.0, down[0])
        for c in range(nc):
            high_y = 0.5 * (ys[c] + up[c])
            low_y = 0.5 * (ys[c] + down[c])
            here = tf[p].get(c, z)
            high_z = 0.5 * (here + jnp.where(sub + z == nz - 1, 0.0, tf[p].get(c, z, d=1)))
            low_z = 0.5 * (here + jnp.where(sub + z == 0, 0.0, tf[p].get(c, z, d=-1)))
            mine = xf[p].get(c, z)
            total = kap[:, c * LANES : (c + 1) * LANES]
            total = total + 0.5 * (mine + xf[p - 1].get(c, z) if p > 0 else mine)
            total = total + 0.5 * (mine + xf[p + 1].get(c, z) if p < nl - 1 else mine)
            df[p].put(c, z, total + low_z + high_z + low_y + high_y)
            if c == nc - 1:
                high_y = jnp.where(lane == LANES - 1, 0.0, high_y)
            yf[p].put(c, z, high_y)
            zf[p].put(c, z, jnp.where(sub + z == nz - 1, 0.0, high_z))

    def all_faces(z):
        for p in range(nl):
            faces(p, z)

    blocks(0, nz, all_faces)


def pack_body(
    dm, nk, conds, cz, kappa, b, shifts, weights, to_swap, to_edge, to_rest, to_in, coef, scalars, temp,
):
    par = lax.rem(lax.axis_index("slab"), 2)
    side_field = lax.rem(lax.axis_index("field"), 2)
    nc, nz, nl = dm.nc, dm.nz, dm.nl
    for k in range(nk):
        scalars[k * 8 : k * 8 + 8, :] = jnp.broadcast_to(shifts[:, k : k + 1], (8, LANES))
    scalars[nk * 8 :, :] = jnp.zeros((8, LANES), jnp.float32)
    scalars[nk * 8 : nk * 8 + 1, 0:nk] = weights[...]
    raw = [conds.at[0], conds.at[1], cz, kappa, b]
    prepare(dm, par, *raw, [coef.at[n] for n in range(5)] + [temp])
    bf, df, xf, yf, zf = [own_planes(dm, coef.at[n]) for n in range(5)]
    zs = pl.multiple_of((1 - par) * dm.half, 8)
    zm = pl.multiple_of((1 - par) * (nz - dm.more), 8)

    def x_face(c, z, one, two):
        return 0.5 * (xf[one].get(c, z) + xf[two].get(c, z))

    def fill(out, at, z_count, sources):
        def body(n):
            for name, value in sources:
                for c in range(nc):
                    out[pl.ds(pl.multiple_of(n, 8) + (at[name] + c * z_count), 8), :] = value(c, n)

        blocks(0, z_count, body, min(4, z_count // 8) if z_count % 32 == 0 else 1)

    def first(out, at, one):
        fill(out, at, nz, [("x1", lambda c, n: xf[one].get(c, n))])

    def edge(out, at, one, two):
        fill(out, at, nz, [
            ("d1", lambda c, n: df[one].get(c, n)),
            ("b1", lambda c, n: bf[one].get(c, n)),
            ("b2", lambda c, n: bf[two].get(c, n)),
        ])

    def rest(out, at, two, three):
        fill(out, at, dm.half, [
            ("fy2", lambda c, n: yf[two].get(c, zs + n)),
            ("d3", lambda c, n: df[three].get(c, zs + n)),
            ("g3", lambda c, n: x_face(c, zs + n, two, three) * bf[three].get(c, zs + n)),
        ])
        fill(out, at, dm.more, [("fz2", lambda c, n: zf[two].get(c, zm + n))])

    def yz(out, at, one):
        out[at["pad"] : at["pad"] + PAD, :] = jnp.zeros((PAD, LANES), jnp.float32)
        fill(out, at, nz, [
            ("fz1", lambda c, n: zf[one].get(c, n)),
            ("fy1", lambda c, n: yf[one].get(c, n)),
        ])

    def x(out, at, one, two):
        out[at["gap"] : at["gap"] + PAD, :] = jnp.zeros((PAD, LANES), jnp.float32)
        fill(out, at, nz, [
            ("fx2", lambda c, n: x_face(c, n, one, two)),
            ("d2", lambda c, n: df[two].get(c, n)),
        ])

    @pl.when(side_field == 0)
    def _():
        yz(to_swap, dm.at_yz, 0)

    @pl.when(side_field == 1)
    def _():
        x(to_swap, dm.at_x, 0, 1)

    first(to_swap, dm.at_first, 0)
    edge(to_edge, dm.at_edge, 0, 1)
    rest(to_rest, dm.at_rest, 1, 2)
    last = nl - 1
    yz(to_in, dm.at_all, last)
    x(to_in, dm.at_all, last, last - 1)
    first(to_in, dm.at_all, last)
    edge(to_in, dm.at_all, last, last - 1)
    rest(to_in, dm.at_all, last - 1, last - 2)


class Steps:
    def __init__(self, dm, nk, par, acc, shifts):
        self.dm, self.nk, self.acc, self.shifts = dm, nk, acc, shifts
        self.zs = pl.multiple_of(par * dm.half, 8)
        self.zm = pl.multiple_of(par * (dm.nz - dm.more), 8)

    def sweep(self, half, body, unroll=4):
        if half:
            blocks(self.zs, self.dm.half, body, unroll)
        else:
            blocks(0, self.dm.nz, body, unroll)

    def add(self, j, k, value):
        at = (j * self.nk + k) * 8
        self.acc[at : at + 8, :] += value

    def total(self, first, second):
        return functools.reduce(jnp.add, [p * q for p, q in zip(first, second)])

    def tiles(self, plane, z, k=None, d=0):
        return [plane.get(c, z, k, d) for c in range(self.dm.nc)]

    def start(self, d, b, w, r=None, half=False, own=False):
        def body(z):
            diagonal, rhs = self.tiles(d, z), self.tiles(b, z)
            for k in range(self.nk):
                s = self.shifts[pl.ds(k * 8, 8), :]
                inverse = [1.0 / (t + s) for t in diagonal]
                value = [x * y for x, y in zip(rhs, inverse)]
                for c in range(self.dm.nc):
                    if r is not None:
                        r.put(c, z, inverse[c], k)
                    w.put(c, z, value[c], k)
                if own:
                    self.add(0, k, self.total(rhs, value))

        self.sweep(half, body, 2)

    def apply(self, v, sides, out, r=None, yz=None, base=None, half=False, moment=None):
        nc = self.dm.nc

        def body(z):
            xs = [(None if x is None else self.tiles(x, z), w) for x, w in sides]
            if yz is not None:
                fy, fz = yz
                lane, sub = lane_ids(), row_ids()
                y_high = self.tiles(fy, z)
                y_low = from_lower(y_high)
                y_low[0] = jnp.where(lane == 0, 0.0, y_low[0])
                z_high = self.tiles(fz, z)
                z_low = self.tiles(fz, z, d=-1)
                if half:
                    z_low = [jnp.where(sub + z == 0, 0.0, t) for t in z_low]
            for k in range(self.nk):
                value = self.tiles(v, z, k) if v is not None else None
                image = None if base is None else self.tiles(base, z, k)
                parts = []
                if yz is not None:
                    below, above = self.tiles(v, z, k, -1), self.tiles(v, z, k, 1)
                    left, right = from_lower(value), from_higher(value)
                    parts.append([z_low[c] * below[c] + z_high[c] * above[c] for c in range(nc)])
                for x, w in xs:
                    near = self.tiles(w, z, k)
                    parts.append(near if x is None else [x[c] * near[c] for c in range(nc)])
                if yz is not None:
                    parts.append([y_low[c] * left[c] + y_high[c] * right[c] for c in range(nc)])
                for part in parts:
                    image = part if image is None else [p + q for p, q in zip(image, part)]
                if r is None:
                    for c in range(nc):
                        out.put(c, z, image[c], k)
                    continue
                result = [p * q for p, q in zip(image, self.tiles(r, z, k))]
                for c in range(nc):
                    out.put(c, z, result[c], k)
                if moment is not None:
                    self.add(moment, k, self.total(value, image))
                    self.add(moment + 1, k, self.total(result, image))

        self.sweep(half, body)

    def face_sum(self, v, side=None, yz=None, half=False):
        nc = self.dm.nc

        def body(z):
            x = self.tiles(side[0], z) if side is not None else None
            if yz is not None:
                y_high, z_high = self.tiles(yz[0], z), self.tiles(yz[1], z)
            for k in range(self.nk):
                value = self.tiles(v, z, k)
                parts = []
                if yz is not None:
                    above, right = self.tiles(v, z, k, 1), from_higher(value)
                    parts.append([z_high[c] * above[c] + y_high[c] * right[c] for c in range(nc)])
                if side is not None:
                    near = self.tiles(side[1], z, k)
                    parts.append([x[c] * near[c] for c in range(nc)])
                image = parts[0]
                if len(parts) == 2:
                    image = [p + q for p, q in zip(*parts)]
                self.add(5, k, 2.0 * self.total(value, image))

        self.sweep(half, body)


def stack(dm, ref, planes):
    return {p: Plane(ref, PAD + n * dm.slot, dm.nz) for n, p in enumerate(planes)}


def clear_pads(dm, nk, ref):
    for n in range((ref.shape[1] - PAD) // dm.slot + 1):
        for k in range(nk):
            ref[k, n * dm.slot : n * dm.slot + PAD, :] = jnp.zeros((PAD, LANES), jnp.float32)


def halo_planes(dm, st, *parts):
    planes = {}
    for ref, at in parts:
        for name, row in at.items():
            if name in ("fy2", "d3", "g3"):
                planes[name] = Plane(ref, row, dm.half, st.zs)
            elif name == "fz2":
                planes[name] = Plane(ref, row, dm.more, st.zm)
            else:
                planes[name] = Plane(ref, row, dm.nz)
    return planes


def near_a_body(
    dm, nk, flats, from_in, shifts, w0a, w1a, w1h, part1, acc, coef, inv12, inv34,
    extra, w0h, inv5,
):
    par = lax.rem(lax.axis_index("slab"), 2)
    nl, nc, nz = dm.nl, dm.nc, dm.nz
    last = nl - 1
    bf, df, raw_x, yf, zf = [own_planes(dm, flats.at[n]) for n in range(5)]
    xf = own_planes(dm, coef)
    st = Steps(dm, nk, par, acc, shifts)
    hp = halo_planes(dm, st, (from_in, dm.at_all))
    acc[...] = jnp.zeros(acc.shape, jnp.float32)
    for ref in (w0a, w1a, w0h, w1h):
        clear_pads(dm, nk, ref)
    d_last, d_next = Plane(extra.at[0], 0, nz), Plane(extra.at[1], 0, nz)

    def edges(z):
        for c in range(nc):
            here, there = raw_x[last].get(c, z), hp["x1"].get(c, z)
            d_last.put(c, z, df[last].get(c, z) + 0.5 * there)
            d_next.put(c, z, hp["d1"].get(c, z) + 0.5 * here)
            for p in range(last):
                xf[p].put(c, z, 0.5 * (raw_x[p].get(c, z) + raw_x[p + 1].get(c, z)))
            xf[last].put(c, z, 0.5 * (here + there))

    blocks(0, nz, edges, 2)
    df[last] = d_last

    W0 = stack(dm, w0a, range(1, nl)) | stack(dm, w0h, (nl, nl + 1))
    far = Plane(w0h, PAD + 2 * dm.slot, dm.half, st.zs)
    W1 = stack(dm, w1a, range(2, nl)) | stack(dm, w1h, (nl, nl + 1))
    R = stack(dm, inv12, (1, 2)) | stack(dm, inv34, range(3, nl + 1)) | stack(dm, inv5, (nl + 1,))

    for p in range(1, nl):
        st.start(df[p], bf[p], W0[p], R[p], own=True)
    st.start(d_next, hp["b1"], W0[nl], R[nl])
    st.start(hp["d2"], hp["b2"], W0[nl + 1], R[nl + 1])
    st.start(hp["d3"], hp["g3"], far, half=True)

    st.apply(W0[1], [(xf[1], W0[2])], Plane(part1, 0, nz), yz=(yf[1], zf[1]))
    for p in range(2, nl):
        st.apply(
            W0[p], [(xf[p - 1], W0[p - 1]), (xf[p], W0[p + 1])], W1[p], R[p], (yf[p], zf[p]), moment=1
        )
    st.apply(
        W0[nl], [(xf[last], W0[last]), (hp["fx2"], W0[nl + 1])], W1[nl], R[nl], (hp["fy1"], hp["fz1"])
    )
    st.apply(
        W0[nl + 1], [(hp["fx2"], W0[nl]), (None, far)], W1[nl + 1], R[nl + 1],
        (hp["fy2"], hp["fz2"]), half=True,
    )


def near_b_body(
    dm, nk, flats, coef, w1a, w1h, acc_in, inv34, from_in, shifts, w2a, part2, acc, w2h,
):
    par = lax.rem(lax.axis_index("slab"), 2)
    nl, nz = dm.nl, dm.nz
    last = nl - 1
    bf, df, raw_x, yf, zf = [own_planes(dm, flats.at[n]) for n in range(5)]
    xf = own_planes(dm, coef)
    st = Steps(dm, nk, par, acc, shifts)
    hp = halo_planes(dm, st, (from_in, dm.at_all))
    acc[...] = acc_in[...]
    for ref in (w2a, w2h):
        clear_pads(dm, nk, ref)
    W1 = stack(dm, w1a, range(2, nl)) | stack(dm, w1h, (nl, nl + 1))
    W2 = stack(dm, w2a, range(3, nl)) | stack(dm, w2h, (nl,))
    R = stack(dm, inv34, range(3, nl + 1))

    st.apply(W1[2], [(xf[2], W1[3])], Plane(part2, 0, nz), yz=(yf[2], zf[2]))
    for p in range(3, nl):
        st.apply(
            W1[p], [(xf[p - 1], W1[p - 1]), (xf[p], W1[p + 1])], W2[p], R[p], (yf[p], zf[p]), moment=3
        )
    st.apply(
        W1[nl], [(xf[last], W1[last]), (hp["fx2"], W1[nl + 1])], W2[nl], R[nl],
        (hp["fy1"], hp["fz1"]), half=True,
    )
    for p in range(3, nl):
        st.face_sum(W2[p], None if p == last else (xf[p], W2[p + 1]), (yf[p], zf[p]))
    st.face_sum(W2[last], (xf[last], W2[nl]), half=True)


def far_0_body(
    dm, nk, flats, coef, w0a, w1a, w2a, part1, part2, acc_in, inv, from_first, shifts,
    w0b, w1b, w2b, acc, edge, inv_out,
):
    index = lax.axis_index("slab")
    par = lax.rem(index, 2)
    has_off = jnp.where(jnp.logical_and(index > 0, index < lax.axis_size("slab") - 1), 0.5, 0.0)
    nl, nc, nz = dm.nl, dm.nc, dm.nz
    bf, df, raw_x, yf, zf = [own_planes(dm, flats.at[n]) for n in range(5)]
    xf = own_planes(dm, coef)
    st = Steps(dm, nk, par, acc, shifts)
    x1 = Plane(from_first, dm.at_first["x1"], nz)
    acc[...] = acc_in[...]
    for ref in (w0b, w1b, w2b):
        clear_pads(dm, nk, ref)
    d_here, x_edge = [Plane(edge.at[n], 0, nz) for n in range(2)]

    def edges(z):
        for c in range(nc):
            here, there = raw_x[0].get(c, z), x1.get(c, z)
            d_here.put(c, z, df[0].get(c, z) + 0.5 * there)
            x_edge.put(c, z, has_off * (here + there))

    blocks(0, nz, edges, 4)

    W0 = stack(dm, w0a, range(1, nl)) | stack(dm, w0b, (0,))
    W1 = stack(dm, w1a, range(2, nl)) | stack(dm, w1b, (1,))
    W2 = stack(dm, w2a, range(3, nl)) | stack(dm, w2b, (2,))
    R = stack(dm, inv_out, (0,)) | stack(dm, inv, (1, 2))
    I1, I2 = Plane(part1, 0, nz), Plane(part2, 0, nz)

    st.start(d_here, bf[0], W0[0], R[0], own=True)
    st.apply(W0[1], [(xf[0], W0[0])], W1[1], R[1], base=I1, moment=1)
    st.apply(W1[2], [(xf[1], W1[1])], W2[2], R[2], base=I2, moment=3)
    st.face_sum(W2[2], (xf[2], W2[3]), (yf[2], zf[2]))


def far_a_body(
    dm, nk, flats, coef, w0a, w0b, w1a, w1b, w2b, acc_in, inv, inv0, edge, from_edge, shifts,
    w0h, w1c, w2c, part3, acc, inv_out, d_ref,
):
    par = lax.rem(lax.axis_index("slab"), 2)
    nl, nc, nz = dm.nl, dm.nc, dm.nz
    bf, df, raw_x, yf, zf = [own_planes(dm, flats.at[n]) for n in range(5)]
    xf = own_planes(dm, coef)
    st = Steps(dm, nk, par, acc, shifts)
    hp = halo_planes(dm, st, (from_edge, dm.at_edge))
    acc[...] = acc_in[...]
    for ref in (w0h, w1c, w2c):
        clear_pads(dm, nk, ref)
    x_edge, d_next = Plane(edge.at[1], 0, nz), Plane(d_ref, 0, nz)

    def edges(z):
        for c in range(nc):
            d_next.put(c, z, hp["d1"].get(c, z) + 0.5 * raw_x[0].get(c, z))

    blocks(0, nz, edges, 4)

    W0 = stack(dm, w0a, range(1, nl)) | stack(dm, w0b, (0,)) | stack(dm, w0h, (-1,))
    W1 = stack(dm, w1a, range(2, nl)) | stack(dm, w1b, (1,)) | stack(dm, w1c, (0,))
    W2 = stack(dm, w2b, (2,)) | stack(dm, w2c, (1,))
    R = stack(dm, inv_out, (-1,)) | stack(dm, inv0, (0,)) | stack(dm, inv, (1, 2))

    st.start(d_next, hp["b1"], W0[-1], R[-1])
    st.apply(W0[0], [(x_edge, W0[-1]), (xf[0], W0[1])], W1[0], R[0], (yf[0], zf[0]), moment=1)
    st.apply(W1[1], [(xf[0], W1[0]), (xf[1], W1[2])], W2[1], R[1], (yf[1], zf[1]), moment=3)
    st.apply(W1[0], [(xf[0], W1[1])], Plane(part3, 0, nz), yz=(yf[0], zf[0]))
    st.face_sum(W2[1], (xf[1], W2[2]), (yf[1], zf[1]))


def far_b_body(
    dm, nk, flats, coef, w0b, w0h, w1c, w2c, part3, acc_in, edge, inv0, inv1, from_edge,
    swap_a, swap_b, shifts, w2d, acc, w1h, inv_out, w0f, shared,
):
    par = lax.rem(lax.axis_index("slab"), 2)
    side_field = lax.rem(lax.axis_index("field"), 2)
    nl, nc, nz = dm.nl, dm.nc, dm.nz
    bf, df, raw_x, yf, zf = [own_planes(dm, flats.at[n]) for n in range(5)]
    xf = own_planes(dm, coef)
    st = Steps(dm, nk, par, acc, shifts)

    @pl.when(side_field == 0)
    def _():
        shared[0 : dm.rows_yz, :] = swap_a[...]
        shared[dm.rows_yz :, :] = swap_b[...]

    @pl.when(side_field == 1)
    def _():
        shared[0 : dm.rows_yz, :] = swap_b[...]
        shared[dm.rows_yz :, :] = swap_a[...]

    at_x = {name: row + dm.rows_yz for name, row in dm.at_x.items()}
    hp = halo_planes(dm, st, (from_edge, dm.at_edge), (shared, dm.at_yz), (shared, at_x))
    acc[...] = acc_in[...]
    for ref in (w2d, w1h, w0f):
        clear_pads(dm, nk, ref)
    x_edge = Plane(edge.at[1], 0, nz)
    W0 = stack(dm, w0b, (0,)) | stack(dm, w0h, (-1,)) | stack(dm, w0f, (-2,))
    W1 = stack(dm, w1c, (0,)) | stack(dm, w1h, (-1,))
    W2 = stack(dm, w2c, (1,)) | stack(dm, w2d, (0,))
    R = stack(dm, inv0, (0,)) | stack(dm, inv1, (-1,)) | stack(dm, inv_out, (-2,))
    st.start(hp["d2"], hp["b2"], W0[-2], R[-2])
    st.apply(
        W0[-1], [(hp["fx2"], W0[-2]), (x_edge, W0[0])], W1[-1], R[-1], (hp["fy1"], hp["fz1"])
    )
    st.apply(W1[0], [(x_edge, W1[-1])], W2[0], R[0], base=Plane(part3, 0, nz), moment=3)
    st.face_sum(W2[0], (xf[0], W2[1]), (yf[0], zf[0]))


def far_c_body(
    dm, nk, w0h, w0f, w1c, w1h, w2d, acc_in, edge, inv1, inv2, from_rest, shared, shifts,
    moments, acc, w0g, w1g, w2g,
):
    par = lax.rem(lax.axis_index("slab"), 2)
    nz = dm.nz
    st = Steps(dm, nk, par, acc, shifts)
    at_x = {name: row + dm.rows_yz for name, row in dm.at_x.items()}
    hp = halo_planes(dm, st, (from_rest, dm.at_rest), (shared, dm.at_yz), (shared, at_x))
    acc[...] = acc_in[...]
    x_edge = Plane(edge.at[1], 0, nz)
    far, near, w2 = [Plane(ref, 0, dm.half, st.zs) for ref in (w0g, w1g, w2g)]
    W0 = stack(dm, w0h, (-1,)) | stack(dm, w0f, (-2,))
    W1 = stack(dm, w1c, (0,)) | stack(dm, w1h, (-1,))
    W2 = stack(dm, w2d, (0,))
    R = stack(dm, inv1, (-1,)) | stack(dm, inv2, (-2,))
    st.start(hp["d3"], hp["g3"], far, half=True)
    st.apply(
        W0[-2], [(None, far), (hp["fx2"], W0[-1])], near, R[-2], (hp["fy2"], hp["fz2"]), half=True
    )
    st.apply(
        W1[-1], [(hp["fx2"], near), (x_edge, W1[0])], w2, R[-1], (hp["fy1"], hp["fz1"]), half=True
    )
    st.face_sum(W2[0], (x_edge, w2), half=True)

    number = 6 * nk
    sums = jnp.sum(acc[...].reshape(number, 8, LANES), axis=1)
    sums = jnp.concatenate([sums, jnp.zeros((LANES - number, LANES), jnp.float32)], axis=0)
    moments[...] = jnp.sum(jnp.transpose(sums), axis=0, keepdims=True)


def coefficients(sums, nk):
    nu = [sums] + [pltpu.roll(sums, LANES - j * nk, 1) for j in range(1, 6)]

    def inner(p, q, shift=0):
        total = None
        for i, x in enumerate(p):
            for j, y in enumerate(q):
                term = x * y * nu[i + j + shift]
                total = term if total is None else total + term
        return total

    one = jnp.ones((8, LANES), jnp.float32)
    zero = jnp.zeros((8, LANES), jnp.float32)
    z = [one]
    p = [one]
    x = [zero, zero, zero]
    norm = nu[0]
    for number in range(3):
        step = norm / (inner(p, p) - inner(p, p, 1))
        x = [x[j] + step * p[j] if j < len(p) else x[j] for j in range(3)]
        if number < 2:
            p, z = p + [zero], z + [zero]
            z = [z[j] - step * (p[j] - (p[j - 1] if j else zero)) for j in range(len(p))]
            norm_next = inner(z, z)
            beta = norm_next / norm
            p = [z[j] + beta * p[j] for j in range(len(z))]
            norm = norm_next
    return x


def combine_body(dm, nk, moments, scalars, w0a, w0b, w1a, w1b, w1c, w2a, w2b, w2c, w2d, out, made, sems):
    par = lax.rem(lax.axis_index("slab"), 2)
    nl, nc, nz = dm.nl, dm.nc, dm.nz
    sums = jnp.sum(moments[...].reshape(-1, LANES), axis=0, keepdims=True)
    x = coefficients(jnp.broadcast_to(sums, (8, LANES)), nk)
    x = [t * scalars[nk * 8 : nk * 8 + 1, :] for t in x]
    scale = [[jnp.broadcast_to(t[:, k : k + 1], (8, LANES)) for k in range(nk)] for t in x]
    W0 = stack(dm, w0a, range(1, nl)) | stack(dm, w0b, (0,))
    W1 = stack(dm, w1a, range(2, nl)) | stack(dm, w1b, (1,)) | stack(dm, w1c, (0,))
    W2 = stack(dm, w2a, range(3, nl)) | stack(dm, w2b, (2,)) | stack(dm, w2c, (1,)) | stack(dm, w2d, (0,))
    copies = []
    for p in range(nl):

        def body(z, p=p):
            for c in range(nc):
                terms = [
                    scale[j][k] * w[p].get(c, z, k) for j, w in enumerate((W0, W1, W2)) for k in range(nk)
                ]
                while len(terms) > 1:
                    terms = [sum(terms[n : n + 2][1:], terms[n]) for n in range(0, len(terms), 2)]
                made[p, pl.ds(z, 8), c * LANES : (c + 1) * LANES] = terms[0]

        blocks(0, nz, body)
        layer = jnp.where(par == 0, p, nl - 1 - p)
        copy = pltpu.make_async_copy(made.at[p], out.at[layer], sems.at[p])
        copy.start()
        copies.append(copy)
    for copy in copies:
        copy.wait()


def on_device(right_side, cond_x, cond_y, cond_z, kappa_sq, shifts, weights):
    dm = Dims(right_side.shape)
    nk = shifts.shape[0]
    nl = dm.nl
    count = lax.axis_size("slab")
    f32 = jnp.float32
    vmem = pl.BlockSpec(memory_space=pltpu.VMEM)

    def params(mib):
        return pltpu.CompilerParams(vmem_limit_bytes=mib * MIB)

    def shape(*dims):
        return jax.ShapeDtypeStruct(dims, f32)

    def stacked(slots):
        return (nk, dm.stack_rows(slots), LANES)

    own = (dm.stack_rows(nl), LANES)
    half_stack = pltpu.VMEM((nk, dm.nc * dm.half, LANES), f32)
    plane_stack = shape(nk, dm.plane, LANES)
    sums = shape(6 * nk * 8, LANES)
    assert dm.rows_yz == dm.rows_x

    to_swap, to_edge, to_rest, to_in, flats, scalars = pl.pallas_call(
        functools.partial(pack_body, dm, nk),
        out_shape=(
            shape(dm.rows_first, LANES), shape(dm.rows_edge, LANES), shape(dm.rows_rest, LANES),
            shape(dm.rows_all, LANES), shape(5, *own), shape(nk * 8 + 8, LANES),
        ),
        in_specs=[vmem] * 6,
        out_specs=(vmem,) * 6,
        scratch_shapes=[
            pltpu.VMEM(own, f32),
        ],
        compiler_params=params(20),
        name="pack",
    )(jnp.stack([cond_x, cond_y]), cond_z, kappa_sq, right_side, shifts[None], weights[None])

    outward = [pair for i in range(1, count - 1, 2) for pair in ((i, i + 1), (i + 1, i))]
    from_first = lax.ppermute(to_swap, "slab", outward)
    from_in = lax.ppermute(to_in, "slab", [(i, i ^ 1) for i in range(count)])
    fields = lax.axis_size("field")

    def call(body, name, mib, results, scratch, operands, cost):
        return pl.pallas_call(
            functools.partial(body, dm, nk),
            out_shape=results,
            in_specs=[vmem] * (len(operands) + 1),
            out_specs=(vmem,) * len(results),
            scratch_shapes=scratch,
            compiler_params=params(mib),
            cost_estimate=pl.CostEstimate(
                flops=10**6, bytes_accessed=cost * 3 * 10**6, transcendentals=0
            ),
            name=name,
        )(*operands, scalars)

    def wide(slots):
        return shape(*stacked(slots))

    def held(slots):
        return pltpu.VMEM(stacked(slots), f32)

    w0a, w1a, w1h, part1, acc, coef, inv12, inv34 = call(
        near_a_body, "near_a", 20,
        (wide(nl - 1), wide(nl - 2), wide(2), plane_stack, sums, shape(*own), wide(2), wide(nl - 2)),
        [pltpu.VMEM((2, dm.plane, LANES), f32), held(3), held(1)],
        (flats, from_in), 6,
    )
    to_edge, acc = lax.optimization_barrier((to_edge, acc))
    from_edge = lax.ppermute(to_edge, "slab", outward)
    w2a, part2, acc = call(
        near_b_body, "near_b", 20,
        (wide(nl - 3), plane_stack, sums),
        [held(1)],
        (flats, coef, w1a, w1h, acc, inv34, from_in), 3,
    )
    from_first, acc = lax.optimization_barrier((from_first, acc))
    swap_a = from_first[: dm.rows_yz]
    swap_b = lax.ppermute(swap_a, "field", [(i, i ^ 1) for i in range(fields)])
    w0b, w1b, w2b, acc, edge, inv0 = call(
        far_0_body, "far_0", 20,
        (wide(1), wide(1), wide(1), sums, shape(2, dm.plane, LANES), wide(1)),
        [],
        (flats, coef, w0a, w1a, w2a, part1, part2, acc, inv12, from_first), 2,
    )
    to_rest, acc = lax.optimization_barrier((to_rest, acc))
    from_rest = lax.ppermute(to_rest, "slab", outward)
    w0h, w1c, w2c, part3, acc, inv1 = call(
        far_a_body, "far_a", 20,
        (wide(1), wide(1), wide(1), plane_stack, sums, wide(1)),
        [pltpu.VMEM((dm.plane, LANES), f32)],
        (flats, coef, w0a, w0b, w1a, w1b, w2b, acc, inv12, inv0, edge, from_edge), 4,
    )
    w2d, acc, w1h, inv2, w0f, shared = call(
        far_b_body, "far_b", 20,
        (wide(1), sums, wide(1), wide(1), wide(1), shape(dm.rows_yz + dm.rows_x, LANES)),
        [],
        (flats, coef, w0b, w0h, w1c, w2c, part3, acc, edge, inv0, inv1, from_edge, swap_a, swap_b), 3,
    )
    moments, _ = call(
        far_c_body, "far_c", 20,
        (shape(1, LANES), sums),
        [half_stack] * 3,
        (w0h, w0f, w1c, w1h, w2d, acc, edge, inv1, inv2, from_rest, shared), 2,
    )

    everywhere = jnp.broadcast_to(moments[None], (count, 1, LANES))
    gathered = lax.all_to_all(everywhere, "slab", 0, 0)

    return pl.pallas_call(
        functools.partial(combine_body, dm, nk),
        out_shape=jax.ShapeDtypeStruct(right_side.shape, f32),
        in_specs=[vmem] * 11,
        out_specs=pl.BlockSpec(memory_space=pl.ANY),
        scratch_shapes=[pltpu.VMEM(right_side.shape, f32), pltpu.SemaphoreType.DMA((nl,))],
        compiler_params=params(20),
        name="combine",
    )(gathered, scalars, w0a, w0b, w1a, w1b, w1c, w2a, w2b, w2c, w2d)


def solution(mesh):
    return jax.shard_map(
        on_device,
        mesh=mesh,
        in_specs=(
            P(("field", "slab"), None, None),
            P("slab", None, None),
            P("slab", None, None),
            P("slab", None, None),
            P("slab", None, None),
            P(),
            P(),
        ),
        out_specs=P(("field", "slab"), None, None),
        check_vma=False,
    )
```

```python
import functools
import jax
import jax.numpy as jnp
from jax import lax
from jax.experimental import pallas as pl
from jax.experimental.pallas import tpu as pltpu
from jax.sharding import PartitionSpec as P

LANES = 128
PAD = 8
MIB = 1024 * 1024


class Dims:
    def __init__(self, shape):
        self.nl, self.nz, self.ny = shape
        self.nc = self.ny // LANES
        self.plane = self.nc * self.nz
        self.slot = self.plane + PAD
        self.half = self.nz // 2
        self.more = self.half + 8
        full, half = self.plane, self.nc * self.half
        more = self.nc * self.more
        yz = [("pad", PAD), ("fz1", full), ("fy1", full)]
        x = [("fx2h", more), ("d2", full), ("d3", half)]
        edge = [("d1", full), ("b1", full), ("g2", full)]
        rest = [("fy2", half), ("g3", half), ("fz2", more)]
        self.at_yz, self.rows_yz = self.layout(yz)
        self.at_x, self.rows_x = self.layout(x)
        self.rows_swap = max(self.rows_yz, self.rows_x)
        self.at_first, self.rows_first = self.layout([("swapped", self.rows_swap), ("x1", full)])
        self.at_edge, self.rows_edge = self.layout(edge)
        self.at_rest, self.rows_rest = self.layout(rest)
        near = [("fx2", full), ("d2", full), ("x1", full), ("d1", full), ("b1", full), ("b2", full)]
        self.at_all, self.rows_all = self.layout(yz + near + [("d3", half)] + rest)

    @staticmethod
    def layout(parts):
        at, total = {}, 0
        for name, rows in parts:
            at[name] = total
            total += rows
        return at, total

    def stack_rows(self, slots):
        return slots * self.slot + PAD


class Plane:
    def __init__(self, ref, base, stride, zoff=0):
        self.ref, self.base, self.stride, self.zoff = ref, base, stride, zoff

    def row(self, c, z):
        return pl.multiple_of(z - self.zoff, 8) + (self.base + c * self.stride)

    def get(self, c, z, k=None, d=0):
        rows = pl.ds(self.row(c, z) + d, 8)
        return self.ref[rows, :] if k is None else self.ref[k, rows, :]

    def put(self, c, z, value, k=None):
        rows = pl.ds(self.row(c, z), 8)
        if k is None:
            self.ref[rows, :] = value
        else:
            self.ref[k, rows, :] = value


def lane_ids():
    return lax.broadcasted_iota(jnp.int32, (8, LANES), 1)


def row_ids():
    return lax.broadcasted_iota(jnp.int32, (8, LANES), 0)


def from_higher(tiles):
    lane = lane_ids()
    n = len(tiles)
    return [
        pltpu.roll(jnp.where(lane == 0, tiles[(c + 1) % n], tiles[c]), LANES - 1, 1)
        for c in range(n)
    ]


def from_lower(tiles):
    lane = lane_ids()
    n = len(tiles)
    return [
        pltpu.roll(jnp.where(lane == LANES - 1, tiles[(c - 1) % n], tiles[c]), 1, 1)
        for c in range(n)
    ]


def blocks(z_from, z_count, body, unroll=1):
    def step(n, carry):
        for u in range(unroll):
            body(pl.multiple_of(z_from + (n * unroll + u) * 8, 8))
        return carry

    lax.fori_loop(0, z_count // (8 * unroll), step, 0)


def own_planes(dm, ref):
    return [Plane(ref, PAD + p * dm.slot, dm.nz) for p in range(dm.nl)]


def prepare(dm, par, cx, cy, cz, kappa, b, flats):
    nc, nz, nl = dm.nc, dm.nz, dm.nl
    bf, df, xf, yf, zf, tf = [own_planes(dm, ref) for ref in flats]
    for ref in (flats[4], flats[5]):
        for p in range(nl + 1):
            ref[p * dm.slot : p * dm.slot + PAD, :] = jnp.zeros((PAD, LANES), jnp.float32)
    layers = [jnp.where(par == 0, p, nl - 1 - p) for p in range(nl)]

    def copy(z):
        for p in range(nl):
            for src, dst in ((b, bf), (cx, xf), (cz, tf)):
                block = src[layers[p], pl.ds(z, 8), :]
                for c in range(nc):
                    dst[p].put(c, z, block[:, c * LANES : (c + 1) * LANES])

    blocks(0, nz, copy)

    def faces(p, z):
        lane, sub = lane_ids(), row_ids()
        conds = cy[layers[p], pl.ds(z, 8), :]
        kap = kappa[layers[p], pl.ds(z, 8), :]
        ys = [conds[:, c * LANES : (c + 1) * LANES] for c in range(nc)]
        up, down = from_higher(ys), from_lower(ys)
        up[-1] = jnp.where(lane == LANES - 1, 0.0, up[-1])
        down[0] = jnp.where(lane == 0, 0.0, down[0])
        for c in range(nc):
            high_y = 0.5 * (ys[c] + up[c])
            low_y = 0.5 * (ys[c] + down[c])
            here = tf[p].get(c, z)
            high_z = 0.5 * (here + jnp.where(sub + z == nz - 1, 0.0, tf[p].get(c, z, d=1)))
            low_z = 0.5 * (here + jnp.where(sub + z == 0, 0.0, tf[p].get(c, z, d=-1)))
            mine = xf[p].get(c, z)
            total = kap[:, c * LANES : (c + 1) * LANES]
            total = total + 0.5 * (mine + xf[p - 1].get(c, z) if p > 0 else mine)
            total = total + 0.5 * (mine + xf[p + 1].get(c, z) if p < nl - 1 else mine)
            df[p].put(c, z, total + low_z + high_z + low_y + high_y)
            if c == nc - 1:
                high_y = jnp.where(lane == LANES - 1, 0.0, high_y)
            yf[p].put(c, z, high_y)
            zf[p].put(c, z, jnp.where(sub + z == nz - 1, 0.0, high_z))

    def all_faces(z):
        for p in range(nl):
            faces(p, z)

    blocks(0, nz, all_faces)


def pack_body(
    dm, nk, conds, cz, kappa, b, shifts, weights, to_swap, to_edge, to_rest, to_in, coef, scalars, temp,
):
    par = lax.rem(lax.axis_index("slab"), 2)
    side_field = lax.rem(lax.axis_index("field"), 2)
    nc, nz, nl = dm.nc, dm.nz, dm.nl
    for k in range(nk):
        scalars[k * 8 : k * 8 + 8, :] = jnp.broadcast_to(shifts[:, k : k + 1], (8, LANES))
    scalars[nk * 8 :, :] = jnp.zeros((8, LANES), jnp.float32)
    scalars[nk * 8 : nk * 8 + 1, 0:nk] = weights[...]
    raw = [conds.at[0], conds.at[1], cz, kappa, b]
    prepare(dm, par, *raw, [coef.at[n] for n in range(5)] + [temp])
    bf, df, xf, yf, zf = [own_planes(dm, coef.at[n]) for n in range(5)]
    zs = pl.multiple_of((1 - par) * dm.half, 8)
    zm = pl.multiple_of((1 - par) * (nz - dm.more), 8)

    def x_face(c, z, one, two):
        return 0.5 * (xf[one].get(c, z) + xf[two].get(c, z))

    def fill(out, at, z_count, sources):
        def body(n):
            for name, value in sources:
                for c in range(nc):
                    out[pl.ds(pl.multiple_of(n, 8) + (at[name] + c * z_count), 8), :] = value(c, n)

        blocks(0, z_count, body, min(4, z_count // 8) if z_count % 32 == 0 else 1)

    def yz(out, at, one):
        out[at["pad"] : at["pad"] + PAD, :] = jnp.zeros((PAD, LANES), jnp.float32)
        fill(out, at, nz, [
            ("fz1", lambda c, n: zf[one].get(c, n)),
            ("fy1", lambda c, n: yf[one].get(c, n)),
        ])

    def rest(out, at, two, three):
        fill(out, at, dm.half, [
            ("fy2", lambda c, n: yf[two].get(c, zs + n)),
            ("g3", lambda c, n: x_face(c, zs + n, two, three) * bf[three].get(c, zs + n)),
        ])
        fill(out, at, dm.more, [("fz2", lambda c, n: zf[two].get(c, zm + n))])

    def third(out, at, three):
        fill(out, at, dm.half, [("d3", lambda c, n: df[three].get(c, zs + n))])

    @pl.when(side_field == 0)
    def _():
        yz(to_swap, dm.at_yz, 0)
        if dm.rows_swap > dm.rows_yz:
            to_swap[dm.rows_yz : dm.rows_swap, :] = jnp.zeros((dm.rows_swap - dm.rows_yz, LANES), jnp.float32)

    @pl.when(side_field == 1)
    def _():
        fill(to_swap, dm.at_x, dm.more, [("fx2h", lambda c, n: x_face(c, zm + n, 0, 1))])
        fill(to_swap, dm.at_x, nz, [("d2", lambda c, n: df[1].get(c, n))])
        third(to_swap, dm.at_x, 2)

    fill(to_swap, dm.at_first, nz, [("x1", lambda c, n: xf[0].get(c, n))])
    fill(to_edge, dm.at_edge, nz, [
        ("d1", lambda c, n: df[0].get(c, n)),
        ("b1", lambda c, n: bf[0].get(c, n)),
        ("g2", lambda c, n: x_face(c, n, 0, 1) * bf[1].get(c, n)),
    ])
    rest(to_rest, dm.at_rest, 1, 2)
    one, two, three = nl - 1, nl - 2, nl - 3
    yz(to_in, dm.at_all, one)
    fill(to_in, dm.at_all, nz, [
        ("fx2", lambda c, n: x_face(c, n, one, two)),
        ("d2", lambda c, n: df[two].get(c, n)),
        ("x1", lambda c, n: xf[one].get(c, n)),
        ("d1", lambda c, n: df[one].get(c, n)),
        ("b1", lambda c, n: bf[one].get(c, n)),
        ("b2", lambda c, n: bf[two].get(c, n)),
    ])
    third(to_in, dm.at_all, three)
    rest(to_in, dm.at_all, two, three)


class Steps:
    def __init__(self, dm, nk, par, acc, shifts):
        self.dm, self.nk, self.acc, self.shifts = dm, nk, acc, shifts
        self.zs = pl.multiple_of(par * dm.half, 8)
        self.zm = pl.multiple_of(par * (dm.nz - dm.more), 8)

    def sweep(self, half, body, unroll=4):
        if half:
            blocks(self.zs, self.dm.half, body, unroll)
        else:
            blocks(0, self.dm.nz, body, unroll)

    def add(self, j, k, value):
        at = (j * self.nk + k) * 8
        self.acc[at : at + 8, :] += value

    def total(self, first, second):
        return functools.reduce(jnp.add, [p * q for p, q in zip(first, second)])

    def tiles(self, plane, z, k=None, d=0):
        return [plane.get(c, z, k, d) for c in range(self.dm.nc)]

    def start(self, d, b, w, r=None, half=False, own=False):
        def body(z):
            diagonal, rhs = self.tiles(d, z), self.tiles(b, z)
            for k in range(self.nk):
                s = self.shifts[pl.ds(k * 8, 8), :]
                inverse = [1.0 / (t + s) for t in diagonal]
                value = [x * y for x, y in zip(rhs, inverse)]
                for c in range(self.dm.nc):
                    if r is not None:
                        r.put(c, z, inverse[c], k)
                    w.put(c, z, value[c], k)
                if own:
                    self.add(0, k, self.total(rhs, value))

        self.sweep(half, body, 2)

    def apply(self, v, sides, out, r=None, yz=None, base=None, half=False, moment=None):
        nc = self.dm.nc

        def body(z):
            xs = [(None if x is None else self.tiles(x, z), w) for x, w in sides]
            if yz is not None:
                fy, fz = yz
                lane, sub = lane_ids(), row_ids()
                y_high = self.tiles(fy, z)
                y_low = from_lower(y_high)
                y_low[0] = jnp.where(lane == 0, 0.0, y_low[0])
                z_high = self.tiles(fz, z)
                z_low = self.tiles(fz, z, d=-1)
                if half:
                    z_low = [jnp.where(sub + z == 0, 0.0, t) for t in z_low]
            for k in range(self.nk):
                value = self.tiles(v, z, k) if v is not None else None
                image = None if base is None else self.tiles(base, z, k)
                parts = []
                if yz is not None:
                    below, above = self.tiles(v, z, k, -1), self.tiles(v, z, k, 1)
                    left, right = from_lower(value), from_higher(value)
                    parts.append([z_low[c] * below[c] + z_high[c] * above[c] for c in range(nc)])
                for x, w in xs:
                    near = self.tiles(w, z, k)
                    parts.append(near if x is None else [x[c] * near[c] for c in range(nc)])
                if yz is not None:
                    parts.append([y_low[c] * left[c] + y_high[c] * right[c] for c in range(nc)])
                for part in parts:
                    image = part if image is None else [p + q for p, q in zip(image, part)]
                if r is None:
                    for c in range(nc):
                        out.put(c, z, image[c], k)
                    continue
                result = [p * q for p, q in zip(image, self.tiles(r, z, k))]
                for c in range(nc):
                    out.put(c, z, result[c], k)
                if moment is not None:
                    self.add(moment, k, self.total(value, image))
                    self.add(moment + 1, k, self.total(result, image))

        self.sweep(half, body)

    def face_sum(self, v, side=None, yz=None, half=False):
        nc = self.dm.nc

        def body(z):
            x = self.tiles(side[0], z) if side is not None else None
            if yz is not None:
                y_high, z_high = self.tiles(yz[0], z), self.tiles(yz[1], z)
            for k in range(self.nk):
                value = self.tiles(v, z, k)
                parts = []
                if yz is not None:
                    above, right = self.tiles(v, z, k, 1), from_higher(value)
                    parts.append([z_high[c] * above[c] + y_high[c] * right[c] for c in range(nc)])
                if side is not None:
                    near = self.tiles(side[1], z, k)
                    parts.append([x[c] * near[c] for c in range(nc)])
                image = parts[0]
                if len(parts) == 2:
                    image = [p + q for p, q in zip(*parts)]
                self.add(5, k, 2.0 * self.total(value, image))

        self.sweep(half, body)


def stack(dm, ref, planes):
    return {p: Plane(ref, PAD + n * dm.slot, dm.nz) for n, p in enumerate(planes)}


def clear_pads(dm, nk, ref):
    for n in range((ref.shape[1] - PAD) // dm.slot + 1):
        for k in range(nk):
            ref[k, n * dm.slot : n * dm.slot + PAD, :] = jnp.zeros((PAD, LANES), jnp.float32)


def halo_planes(dm, st, *parts):
    planes = {}
    for ref, at in parts:
        for name, row in at.items():
            if name in ("fy2", "d3", "g3"):
                planes[name] = Plane(ref, row, dm.half, st.zs)
            elif name in ("fz2", "fx2h"):
                planes[name] = Plane(ref, row, dm.more, st.zm)
            else:
                planes[name] = Plane(ref, row, dm.nz)
    return planes


def near_a_body(
    dm, nk, flats, from_in, shifts, w0a, w1a, w1h, part1, acc, coef, inv12, inv34,
    extra, w0h, inv5,
):
    par = lax.rem(lax.axis_index("slab"), 2)
    nl, nc, nz = dm.nl, dm.nc, dm.nz
    last = nl - 1
    bf, df, raw_x, yf, zf = [own_planes(dm, flats.at[n]) for n in range(5)]
    xf = own_planes(dm, coef)
    st = Steps(dm, nk, par, acc, shifts)
    hp = halo_planes(dm, st, (from_in, dm.at_all))
    acc[...] = jnp.zeros(acc.shape, jnp.float32)
    for ref in (w0a, w1a, w0h, w1h):
        clear_pads(dm, nk, ref)
    d_last, d_next = Plane(extra.at[0], 0, nz), Plane(extra.at[1], 0, nz)

    def edges(z):
        for c in range(nc):
            here, there = raw_x[last].get(c, z), hp["x1"].get(c, z)
            d_last.put(c, z, df[last].get(c, z) + 0.5 * there)
            d_next.put(c, z, hp["d1"].get(c, z) + 0.5 * here)
            for p in range(last):
                xf[p].put(c, z, 0.5 * (raw_x[p].get(c, z) + raw_x[p + 1].get(c, z)))
            xf[last].put(c, z, 0.5 * (here + there))

    blocks(0, nz, edges, 2)
    df[last] = d_last

    W0 = stack(dm, w0a, range(1, nl)) | stack(dm, w0h, (nl, nl + 1))
    far = Plane(w0h, PAD + 2 * dm.slot, dm.half, st.zs)
    W1 = stack(dm, w1a, range(2, nl)) | stack(dm, w1h, (nl, nl + 1))
    R = stack(dm, inv12, (1, 2)) | stack(dm, inv34, range(3, nl + 1)) | stack(dm, inv5, (nl + 1,))

    for p in range(1, nl):
        st.start(df[p], bf[p], W0[p], R[p], own=True)
    st.start(d_next, hp["b1"], W0[nl], R[nl])
    st.start(hp["d2"], hp["b2"], W0[nl + 1], R[nl + 1])
    st.start(hp["d3"], hp["g3"], far, half=True)

    st.apply(W0[1], [(xf[1], W0[2])], Plane(part1, 0, nz), yz=(yf[1], zf[1]))
    for p in range(2, nl):
        st.apply(
            W0[p], [(xf[p - 1], W0[p - 1]), (xf[p], W0[p + 1])], W1[p], R[p], (yf[p], zf[p]), moment=1
        )
    st.apply(
        W0[nl], [(xf[last], W0[last]), (hp["fx2"], W0[nl + 1])], W1[nl], R[nl], (hp["fy1"], hp["fz1"])
    )
    st.apply(
        W0[nl + 1], [(hp["fx2"], W0[nl]), (None, far)], W1[nl + 1], R[nl + 1],
        (hp["fy2"], hp["fz2"]), half=True,
    )


def near_b_body(
    dm, nk, flats, coef, w1a, w1h, acc_in, inv34, from_in, shifts, w2a, part2, acc, w2h,
):
    par = lax.rem(lax.axis_index("slab"), 2)
    nl, nz = dm.nl, dm.nz
    last = nl - 1
    bf, df, raw_x, yf, zf = [own_planes(dm, flats.at[n]) for n in range(5)]
    xf = own_planes(dm, coef)
    st = Steps(dm, nk, par, acc, shifts)
    hp = halo_planes(dm, st, (from_in, dm.at_all))
    acc[...] = acc_in[...]
    for ref in (w2a, w2h):
        clear_pads(dm, nk, ref)
    W1 = stack(dm, w1a, range(2, nl)) | stack(dm, w1h, (nl, nl + 1))
    W2 = stack(dm, w2a, range(3, nl)) | stack(dm, w2h, (nl,))
    R = stack(dm, inv34, range(3, nl + 1))

    st.apply(W1[2], [(xf[2], W1[3])], Plane(part2, 0, nz), yz=(yf[2], zf[2]))
    for p in range(3, nl):
        st.apply(
            W1[p], [(xf[p - 1], W1[p - 1]), (xf[p], W1[p + 1])], W2[p], R[p], (yf[p], zf[p]), moment=3
        )
    st.apply(
        W1[nl], [(xf[last], W1[last]), (hp["fx2"], W1[nl + 1])], W2[nl], R[nl],
        (hp["fy1"], hp["fz1"]), half=True,
    )
    for p in range(3, nl):
        st.face_sum(W2[p], None if p == last else (xf[p], W2[p + 1]), (yf[p], zf[p]))
    st.face_sum(W2[last], (xf[last], W2[nl]), half=True)


def far_0_body(
    dm, nk, flats, coef, w0a, w1a, w2a, part1, part2, acc_in, inv, from_first, shifts,
    w0b, w1b, w2b, acc, edge, inv_out, part0, part3,
):
    index = lax.axis_index("slab")
    par = lax.rem(index, 2)
    has_off = jnp.where(jnp.logical_and(index > 0, index < lax.axis_size("slab") - 1), 0.5, 0.0)
    nl, nc, nz = dm.nl, dm.nc, dm.nz
    bf, df, raw_x, yf, zf = [own_planes(dm, flats.at[n]) for n in range(5)]
    xf = own_planes(dm, coef)
    st = Steps(dm, nk, par, acc, shifts)
    x1 = Plane(from_first, dm.at_first["x1"], nz)
    acc[...] = acc_in[...]
    for ref in (w0b, w1b, w2b):
        clear_pads(dm, nk, ref)
    d_here, x_edge = [Plane(edge.at[n], 0, nz) for n in range(2)]

    def edges(z):
        for c in range(nc):
            here, there = raw_x[0].get(c, z), x1.get(c, z)
            d_here.put(c, z, df[0].get(c, z) + 0.5 * there)
            x_edge.put(c, z, has_off * (here + there))

    blocks(0, nz, edges, 4)

    W0 = stack(dm, w0a, range(1, nl)) | stack(dm, w0b, (0,))
    W1 = stack(dm, w1a, range(2, nl)) | stack(dm, w1b, (1,))
    W2 = stack(dm, w2a, range(3, nl)) | stack(dm, w2b, (2,))
    R = stack(dm, inv_out, (0,)) | stack(dm, inv, (1, 2))
    I1, I2 = Plane(part1, 0, nz), Plane(part2, 0, nz)

    st.start(d_here, bf[0], W0[0], R[0], own=True)
    st.apply(W0[1], [(xf[0], W0[0])], W1[1], R[1], base=I1, moment=1)
    st.apply(W1[2], [(xf[1], W1[1])], W2[2], R[2], base=I2, moment=3)
    st.apply(W0[0], [(xf[0], W0[1])], Plane(part0, 0, nz), yz=(yf[0], zf[0]))
    st.apply(W1[1], [(xf[1], W1[2])], Plane(part3, 0, nz), yz=(yf[1], zf[1]))
    st.face_sum(W2[2], (xf[2], W2[3]), (yf[2], zf[2]))


def far_a_body(
    dm, nk, flats, coef, w0b, w1b, w2b, part0, part3, acc_in, inv, inv0, edge, from_edge, shifts,
    w0h, w1c, w2c, part4, acc, inv_out, d_ref,
):
    par = lax.rem(lax.axis_index("slab"), 2)
    nl, nc, nz = dm.nl, dm.nc, dm.nz
    bf, df, raw_x, yf, zf = [own_planes(dm, flats.at[n]) for n in range(5)]
    xf = own_planes(dm, coef)
    st = Steps(dm, nk, par, acc, shifts)
    hp = halo_planes(dm, st, (from_edge, dm.at_edge))
    acc[...] = acc_in[...]
    for ref in (w0h, w1c, w2c):
        clear_pads(dm, nk, ref)
    x_edge, d_next = Plane(edge.at[1], 0, nz), Plane(d_ref, 0, nz)

    def edges(z):
        for c in range(nc):
            d_next.put(c, z, hp["d1"].get(c, z) + 0.5 * raw_x[0].get(c, z))

    blocks(0, nz, edges, 4)

    W0 = stack(dm, w0b, (0,)) | stack(dm, w0h, (-1,))
    W1 = stack(dm, w1b, (1,)) | stack(dm, w1c, (0,))
    W2 = stack(dm, w2b, (2,)) | stack(dm, w2c, (1,))
    R = stack(dm, inv_out, (-1,)) | stack(dm, inv0, (0,)) | stack(dm, inv, (1, 2))

    st.start(d_next, hp["b1"], W0[-1], R[-1])
    st.apply(W0[0], [(x_edge, W0[-1])], W1[0], R[0], base=Plane(part0, 0, nz), moment=1)
    st.apply(W1[1], [(xf[0], W1[0])], W2[1], R[1], base=Plane(part3, 0, nz), moment=3)
    st.apply(W1[0], [(xf[0], W1[1])], Plane(part4, 0, nz), yz=(yf[0], zf[0]))
    st.face_sum(W2[1], (xf[1], W2[2]), (yf[1], zf[1]))


def far_b_body(
    dm, nk, flats, coef, w0b, w0h, w1c, w2c, part4, acc_in, edge, inv0, inv1, from_edge,
    swap_a, swap_b, shifts, w2d, acc, w1h, inv_out, shared, w0x,
):
    par = lax.rem(lax.axis_index("slab"), 2)
    side_field = lax.rem(lax.axis_index("field"), 2)
    nl, nc, nz = dm.nl, dm.nc, dm.nz
    bf, df, raw_x, yf, zf = [own_planes(dm, flats.at[n]) for n in range(5)]
    xf = own_planes(dm, coef)
    st = Steps(dm, nk, par, acc, shifts)

    @pl.when(side_field == 0)
    def _():
        shared[0 : dm.rows_swap, :] = swap_a[...]
        shared[dm.rows_swap :, :] = swap_b[...]

    @pl.when(side_field == 1)
    def _():
        shared[0 : dm.rows_swap, :] = swap_b[...]
        shared[dm.rows_swap :, :] = swap_a[...]

    at_x = {name: row + dm.rows_swap for name, row in dm.at_x.items()}
    hp = halo_planes(dm, st, (from_edge, dm.at_edge), (shared, dm.at_yz), (shared, at_x))
    acc[...] = acc_in[...]
    for ref in (w2d, w1h):
        clear_pads(dm, nk, ref)
    x_edge = Plane(edge.at[1], 0, nz)
    W0 = stack(dm, w0b, (0,)) | stack(dm, w0h, (-1,))
    behind = Plane(w0x, 0, nz)
    W1 = stack(dm, w1c, (0,)) | stack(dm, w1h, (-1,))
    W2 = stack(dm, w2c, (1,)) | stack(dm, w2d, (0,))
    R = stack(dm, inv0, (0,)) | stack(dm, inv1, (-1,)) | stack(dm, inv_out, (-2,))
    st.start(hp["d2"], hp["g2"], behind, R[-2])
    st.apply(W0[-1], [(None, behind), (x_edge, W0[0])], W1[-1], R[-1], (hp["fy1"], hp["fz1"]))
    st.apply(W1[0], [(x_edge, W1[-1])], W2[0], R[0], base=Plane(part4, 0, nz), moment=3)
    st.face_sum(W2[0], (xf[0], W2[1]), (yf[0], zf[0]))


def far_c_body(
    dm, nk, w0h, w1c, w1h, w2d, acc_in, edge, inv1, inv2, from_edge, rest_a, rest_b, shared, shifts,
    moments, acc, w0g, w1g, w2g, w0m, rest,
):
    par = lax.rem(lax.axis_index("slab"), 2)
    nz, nc = dm.nz, dm.nc
    st = Steps(dm, nk, par, acc, shifts)
    rest[...] = rest_a[...] + rest_b[...]
    at_x = {name: row + dm.rows_swap for name, row in dm.at_x.items()}
    hp = halo_planes(dm, st, (from_edge, dm.at_edge), (rest, dm.at_rest), (shared, dm.at_yz), (shared, at_x))
    acc[...] = acc_in[...]
    x_edge = Plane(edge.at[1], 0, nz)
    far, near, w2 = [Plane(ref, 0, dm.half, st.zs) for ref in (w0g, w1g, w2g)]
    behind = Plane(w0m, PAD, dm.more, st.zm)
    W0 = stack(dm, w0h, (-1,))
    W1 = stack(dm, w1c, (0,)) | stack(dm, w1h, (-1,))
    W2 = stack(dm, w2d, (0,))
    R = stack(dm, inv1, (-1,)) | stack(dm, inv2, (-2,))
    for k in range(nk):
        w0m[k, 0:PAD, :] = jnp.zeros((PAD, LANES), jnp.float32)
        w0m[k, PAD + nc * dm.more :, :] = jnp.zeros((PAD, LANES), jnp.float32)

    def right_side(z):
        for c in range(nc):
            rhs = hp["g2"].get(c, z) / jnp.maximum(hp["fx2h"].get(c, z), 0.1)
            for k in range(nk):
                behind.put(c, z, rhs * R[-2].get(c, z, k), k)

    blocks(st.zm, dm.more, right_side)
    st.start(hp["d3"], hp["g3"], far, half=True)
    st.apply(
        behind, [(None, far), (hp["fx2h"], W0[-1])], near, R[-2], (hp["fy2"], hp["fz2"]), half=True
    )
    st.apply(
        W1[-1], [(hp["fx2h"], near), (x_edge, W1[0])], w2, R[-1], (hp["fy1"], hp["fz1"]), half=True
    )
    st.face_sum(W2[0], (x_edge, w2), half=True)

    number = 6 * nk
    sums = jnp.sum(acc[...].reshape(number, 8, LANES), axis=1)
    sums = jnp.concatenate([sums, jnp.zeros((LANES - number, LANES), jnp.float32)], axis=0)
    moments[...] = jnp.sum(jnp.transpose(sums), axis=0, keepdims=True)


def coefficients(sums, nk):
    nu = [sums] + [pltpu.roll(sums, LANES - j * nk, 1) for j in range(1, 6)]

    def inner(p, q, shift=0):
        total = None
        for i, x in enumerate(p):
            for j, y in enumerate(q):
                term = x * y * nu[i + j + shift]
                total = term if total is None else total + term
        return total

    one = jnp.ones((8, LANES), jnp.float32)
    zero = jnp.zeros((8, LANES), jnp.float32)
    z = [one]
    p = [one]
    x = [zero, zero, zero]
    norm = nu[0]
    for number in range(3):
        step = norm / (inner(p, p) - inner(p, p, 1))
        x = [x[j] + step * p[j] if j < len(p) else x[j] for j in range(3)]
        if number < 2:
            p, z = p + [zero], z + [zero]
            z = [z[j] - step * (p[j] - (p[j - 1] if j else zero)) for j in range(len(p))]
            norm_next = inner(z, z)
            beta = norm_next / norm
            p = [z[j] + beta * p[j] for j in range(len(z))]
            norm = norm_next
    return x


def combine_body(dm, nk, moments, scalars, w0a, w0b, w1a, w1b, w1c, w2a, w2b, w2c, w2d, out, made, sems):
    par = lax.rem(lax.axis_index("slab"), 2)
    nl, nc, nz = dm.nl, dm.nc, dm.nz
    sums = jnp.sum(moments[...].reshape(-1, LANES), axis=0, keepdims=True)
    x = coefficients(jnp.broadcast_to(sums, (8, LANES)), nk)
    x = [t * scalars[nk * 8 : nk * 8 + 1, :] for t in x]
    scale = [[jnp.broadcast_to(t[:, k : k + 1], (8, LANES)) for k in range(nk)] for t in x]
    W0 = stack(dm, w0a, range(1, nl)) | stack(dm, w0b, (0,))
    W1 = stack(dm, w1a, range(2, nl)) | stack(dm, w1b, (1,)) | stack(dm, w1c, (0,))
    W2 = stack(dm, w2a, range(3, nl)) | stack(dm, w2b, (2,)) | stack(dm, w2c, (1,)) | stack(dm, w2d, (0,))
    copies = []
    for p in range(nl):

        def body(z, p=p):
            for c in range(nc):
                terms = [
                    scale[j][k] * w[p].get(c, z, k) for j, w in enumerate((W0, W1, W2)) for k in range(nk)
                ]
                while len(terms) > 1:
                    terms = [sum(terms[n : n + 2][1:], terms[n]) for n in range(0, len(terms), 2)]
                made[p, pl.ds(z, 8), c * LANES : (c + 1) * LANES] = terms[0]

        blocks(0, nz, body)
        layer = jnp.where(par == 0, p, nl - 1 - p)
        copy = pltpu.make_async_copy(made.at[p], out.at[layer], sems.at[p])
        copy.start()
        copies.append(copy)
    for copy in copies:
        copy.wait()


def on_device(right_side, cond_x, cond_y, cond_z, kappa_sq, shifts, weights):
    dm = Dims(right_side.shape)
    nk = shifts.shape[0]
    nl = dm.nl
    count = lax.axis_size("slab")
    f32 = jnp.float32
    vmem = pl.BlockSpec(memory_space=pltpu.VMEM)

    def params(mib):
        return pltpu.CompilerParams(vmem_limit_bytes=mib * MIB)

    def shape(*dims):
        return jax.ShapeDtypeStruct(dims, f32)

    def stacked(slots):
        return (nk, dm.stack_rows(slots), LANES)

    own = (dm.stack_rows(nl), LANES)
    half_stack = pltpu.VMEM((nk, dm.nc * dm.half, LANES), f32)
    plane_stack = shape(nk, dm.plane, LANES)
    sums = shape(6 * nk * 8, LANES)

    to_swap, to_edge, to_rest, to_in, flats, scalars = pl.pallas_call(
        functools.partial(pack_body, dm, nk),
        out_shape=(
            shape(dm.rows_first, LANES), shape(dm.rows_edge, LANES), shape(dm.rows_rest, LANES),
            shape(dm.rows_all, LANES), shape(5, *own), shape(nk * 8 + 8, LANES),
        ),
        in_specs=[vmem] * 6,
        out_specs=(vmem,) * 6,
        scratch_shapes=[
            pltpu.VMEM(own, f32),
        ],
        compiler_params=params(20),
        name="pack",
    )(jnp.stack([cond_x, cond_y]), cond_z, kappa_sq, right_side, shifts[None], weights[None])

    outward = [pair for i in range(1, count - 1, 2) for pair in ((i, i + 1), (i + 1, i))]
    from_first = lax.ppermute(to_swap, "slab", outward)
    from_in = lax.ppermute(to_in, "slab", [(i, i ^ 1) for i in range(count)])
    fields = lax.axis_size("field")

    def call(body, name, mib, results, scratch, operands, cost):
        return pl.pallas_call(
            functools.partial(body, dm, nk),
            out_shape=results,
            in_specs=[vmem] * (len(operands) + 1),
            out_specs=(vmem,) * len(results),
            scratch_shapes=scratch,
            compiler_params=params(mib),
            cost_estimate=pl.CostEstimate(
                flops=10**6, bytes_accessed=cost * 3 * 10**6, transcendentals=0
            ),
            name=name,
        )(*operands, scalars)

    def wide(slots):
        return shape(*stacked(slots))

    def held(slots):
        return pltpu.VMEM(stacked(slots), f32)

    w0a, w1a, w1h, part1, acc, coef, inv12, inv34 = call(
        near_a_body, "near_a", 20,
        (wide(nl - 1), wide(nl - 2), wide(2), plane_stack, sums, shape(*own), wide(2), wide(nl - 2)),
        [pltpu.VMEM((2, dm.plane, LANES), f32), held(3), held(1)],
        (flats, from_in), 6,
    )
    to_edge, acc = lax.optimization_barrier((to_edge, acc))
    from_edge = lax.ppermute(to_edge, "slab", outward)
    w2a, part2, acc = call(
        near_b_body, "near_b", 20,
        (wide(nl - 3), plane_stack, sums),
        [held(1)],
        (flats, coef, w1a, w1h, acc, inv34, from_in), 3,
    )
    from_first, acc = lax.optimization_barrier((from_first, acc))
    swap_a = from_first[: dm.rows_swap]
    swap_b = lax.ppermute(swap_a, "field", [(i, i ^ 1) for i in range(fields)])
    w0b, w1b, w2b, acc, edge, inv0, part0, part3 = call(
        far_0_body, "far_0", 20,
        (wide(1), wide(1), wide(1), sums, shape(2, dm.plane, LANES), wide(1), plane_stack, plane_stack),
        [],
        (flats, coef, w0a, w1a, w2a, part1, part2, acc, inv12, from_first), 2,
    )
    to_rest, acc = lax.optimization_barrier((to_rest, acc))
    rest_a = lax.ppermute(to_rest, "slab", outward[0::4] + outward[1::4])
    w0h, w1c, w2c, part4, acc, inv1 = call(
        far_a_body, "far_a", 20,
        (wide(1), wide(1), wide(1), plane_stack, sums, wide(1)),
        [pltpu.VMEM((dm.plane, LANES), f32)],
        (flats, coef, w0b, w1b, w2b, part0, part3, acc, inv12, inv0, edge, from_edge), 4,
    )
    to_rest, from_edge = lax.optimization_barrier((to_rest, from_edge))
    rest_b = lax.ppermute(to_rest, "slab", outward[2::4] + outward[3::4])
    w2d, acc, w1h, inv2, shared = call(
        far_b_body, "far_b", 20,
        (wide(1), sums, wide(1), wide(1), shape(2 * dm.rows_swap, LANES)),
        [pltpu.VMEM((nk, dm.plane, LANES), f32)],
        (flats, coef, w0b, w0h, w1c, w2c, part4, acc, edge, inv0, inv1, from_edge, swap_a, swap_b), 3,
    )
    moments, _ = call(
        far_c_body, "far_c", 20,
        (shape(1, LANES), sums),
        [half_stack] * 3
        + [pltpu.VMEM((nk, dm.nc * dm.more + 2 * PAD, LANES), f32), pltpu.VMEM((dm.rows_rest, LANES), f32)],
        (w0h, w1c, w1h, w2d, acc, edge, inv1, inv2, from_edge, rest_a, rest_b, shared), 2,
    )

    everywhere = jnp.broadcast_to(moments[None], (count, 1, LANES))
    gathered = lax.all_to_all(everywhere, "slab", 0, 0)

    return pl.pallas_call(
        functools.partial(combine_body, dm, nk),
        out_shape=jax.ShapeDtypeStruct(right_side.shape, f32),
        in_specs=[vmem] * 11,
        out_specs=pl.BlockSpec(memory_space=pl.ANY),
        scratch_shapes=[pltpu.VMEM(right_side.shape, f32), pltpu.SemaphoreType.DMA((nl,))],
        compiler_params=params(20),
        name="combine",
    )(gathered, scalars, w0a, w0b, w1a, w1b, w1c, w2a, w2b, w2c, w2d)


def solution(mesh):
    return jax.shard_map(
        on_device,
        mesh=mesh,
        in_specs=(
            P(("field", "slab"), None, None),
            P("slab", None, None),
            P("slab", None, None),
            P("slab", None, None),
            P("slab", None, None),
            P(),
            P(),
        ),
        out_specs=P(("field", "slab"), None, None),
        check_vma=False,
    )
```

```python
import functools
import jax
import jax.numpy as jnp
from jax import lax
from jax.experimental import pallas as pl
from jax.experimental.pallas import tpu as pltpu
from jax.sharding import PartitionSpec as P

LANES = 128
PAD = 8
MIB = 1024 * 1024


class Dims:
    def __init__(self, shape):
        self.nl, self.nz, self.ny = shape
        self.nc = self.ny // LANES
        self.plane = self.nc * self.nz
        self.slot = self.plane + PAD
        self.half = self.nz // 2
        self.more = self.half + 8
        full, half = self.plane, self.nc * self.half
        more = self.nc * self.more
        yz = [("pad", PAD), ("fz1", full), ("fy1", full)]
        x = [("fx2h", more), ("d2", full), ("d3", half)]
        edge = [("d1", full), ("b1", full), ("g2", full)]
        rest = [("fy2", half), ("g3", half), ("fz2", more)]
        self.at_yz, self.rows_yz = self.layout(yz)
        self.at_x, self.rows_x = self.layout(x)
        self.rows_swap = max(self.rows_yz, self.rows_x)
        self.at_first, self.rows_first = self.layout([("swapped", self.rows_swap), ("x1", full)])
        self.at_edge, self.rows_edge = self.layout(edge)
        self.at_rest, self.rows_rest = self.layout(rest)
        near = [("fx2", full), ("d2", full), ("x1", full), ("d1", full), ("b1", full), ("b2", full)]
        self.at_all, self.rows_all = self.layout(yz + near + [("d3", half)] + rest)

    @staticmethod
    def layout(parts):
        at, total = {}, 0
        for name, rows in parts:
            at[name] = total
            total += rows
        return at, total

    def stack_rows(self, slots):
        return slots * self.slot + PAD


class Plane:
    def __init__(self, ref, base, stride, zoff=0):
        self.ref, self.base, self.stride, self.zoff = ref, base, stride, zoff

    def row(self, c, z):
        return pl.multiple_of(z - self.zoff, 8) + (self.base + c * self.stride)

    def get(self, c, z, k=None, d=0):
        rows = pl.ds(self.row(c, z) + d, 8)
        return self.ref[rows, :] if k is None else self.ref[k, rows, :]

    def put(self, c, z, value, k=None):
        rows = pl.ds(self.row(c, z), 8)
        if k is None:
            self.ref[rows, :] = value
        else:
            self.ref[k, rows, :] = value


def lane_ids():
    return lax.broadcasted_iota(jnp.int32, (8, LANES), 1)


def row_ids():
    return lax.broadcasted_iota(jnp.int32, (8, LANES), 0)


def from_higher(tiles):
    lane = lane_ids()
    n = len(tiles)
    return [
        pltpu.roll(jnp.where(lane == 0, tiles[(c + 1) % n], tiles[c]), LANES - 1, 1)
        for c in range(n)
    ]


def from_lower(tiles):
    lane = lane_ids()
    n = len(tiles)
    return [
        pltpu.roll(jnp.where(lane == LANES - 1, tiles[(c - 1) % n], tiles[c]), 1, 1)
        for c in range(n)
    ]


def blocks(z_from, z_count, body, unroll=1):
    def step(n, carry):
        for u in range(unroll):
            body(pl.multiple_of(z_from + (n * unroll + u) * 8, 8))
        return carry

    lax.fori_loop(0, z_count // (8 * unroll), step, 0)


def own_planes(dm, ref):
    return [Plane(ref, PAD + p * dm.slot, dm.nz) for p in range(dm.nl)]


def prepare(dm, par, cx, cy, cz, kappa, flats):
    nc, nz, nl = dm.nc, dm.nz, dm.nl
    df, xf, yf, zf, tf = [own_planes(dm, ref) for ref in flats]
    for ref in (flats[3], flats[4]):
        for p in range(nl + 1):
            ref[p * dm.slot : p * dm.slot + PAD, :] = jnp.zeros((PAD, LANES), jnp.float32)
    layers = [jnp.where(par == 0, p, nl - 1 - p) for p in range(nl)]

    def copy(z):
        for p in range(nl):
            for src, dst in ((cx, xf), (cz, tf)):
                block = src[layers[p], pl.ds(z, 8), :]
                for c in range(nc):
                    dst[p].put(c, z, block[:, c * LANES : (c + 1) * LANES])

    blocks(0, nz, copy)

    def faces(p, z):
        lane, sub = lane_ids(), row_ids()
        conds = cy[layers[p], pl.ds(z, 8), :]
        kap = kappa[layers[p], pl.ds(z, 8), :]
        ys = [conds[:, c * LANES : (c + 1) * LANES] for c in range(nc)]
        up, down = from_higher(ys), from_lower(ys)
        up[-1] = jnp.where(lane == LANES - 1, 0.0, up[-1])
        down[0] = jnp.where(lane == 0, 0.0, down[0])
        for c in range(nc):
            high_y = 0.5 * (ys[c] + up[c])
            low_y = 0.5 * (ys[c] + down[c])
            here = tf[p].get(c, z)
            high_z = 0.5 * (here + jnp.where(sub + z == nz - 1, 0.0, tf[p].get(c, z, d=1)))
            low_z = 0.5 * (here + jnp.where(sub + z == 0, 0.0, tf[p].get(c, z, d=-1)))
            mine = xf[p].get(c, z)
            total = kap[:, c * LANES : (c + 1) * LANES]
            total = total + 0.5 * (mine + xf[p - 1].get(c, z) if p > 0 else mine)
            total = total + 0.5 * (mine + xf[p + 1].get(c, z) if p < nl - 1 else mine)
            df[p].put(c, z, total + low_z + high_z + low_y + high_y)
            if c == nc - 1:
                high_y = jnp.where(lane == LANES - 1, 0.0, high_y)
            yf[p].put(c, z, high_y)
            zf[p].put(c, z, jnp.where(sub + z == nz - 1, 0.0, high_z))

    def all_faces(z):
        for p in range(nl):
            faces(p, z)

    blocks(0, nz, all_faces)


class Packer:
    def __init__(self, dm, par):
        self.dm = dm
        self.zs = pl.multiple_of((1 - par) * dm.half, 8)
        self.zm = pl.multiple_of((1 - par) * (dm.nz - dm.more), 8)

    def fill(self, out, at, z_count, sources):
        def body(n):
            for name, value in sources:
                for c in range(self.dm.nc):
                    out[pl.ds(pl.multiple_of(n, 8) + (at[name] + c * z_count), 8), :] = value(c, n)

        blocks(0, z_count, body, min(4, z_count // 8) if z_count % 32 == 0 else 1)

    def yz(self, out, at, yf, zf, one):
        out[at["pad"] : at["pad"] + PAD, :] = jnp.zeros((PAD, LANES), jnp.float32)
        self.fill(out, at, self.dm.nz, [
            ("fz1", lambda c, n: zf[one].get(c, n)),
            ("fy1", lambda c, n: yf[one].get(c, n)),
        ])

    def third(self, out, at, df, three):
        self.fill(out, at, self.dm.half, [("d3", lambda c, n: df[three].get(c, self.zs + n))])


def x_face_of(xf):
    return lambda c, z, one, two: 0.5 * (xf[one].get(c, z) + xf[two].get(c, z))


def pack_faces_body(dm, nk, conds, cz, kappa, shifts, weights, to_swap, coef, scalars, temp):
    par = lax.rem(lax.axis_index("slab"), 2)
    side_field = lax.rem(lax.axis_index("field"), 2)
    prepare(dm, par, conds.at[0], conds.at[1], cz, kappa, [coef.at[n] for n in range(4)] + [temp])
    df, xf, yf, zf = [own_planes(dm, coef.at[n]) for n in range(4)]
    x_face = x_face_of(xf)
    to = Packer(dm, par)

    @pl.when(side_field == 0)
    def _():
        to.yz(to_swap, dm.at_yz, yf, zf, 0)
        if dm.rows_swap > dm.rows_yz:
            to_swap[dm.rows_yz : dm.rows_swap, :] = jnp.zeros((dm.rows_swap - dm.rows_yz, LANES), jnp.float32)

    @pl.when(side_field == 1)
    def _():
        to.fill(to_swap, dm.at_x, dm.more, [("fx2h", lambda c, n: x_face(c, to.zm + n, 0, 1))])
        to.fill(to_swap, dm.at_x, dm.nz, [("d2", lambda c, n: df[1].get(c, n))])
        to.third(to_swap, dm.at_x, df, 2)

    to.fill(to_swap, dm.at_first, dm.nz, [("x1", lambda c, n: xf[0].get(c, n))])
    for k in range(nk):
        scalars[k * 8 : k * 8 + 8, :] = jnp.broadcast_to(shifts[:, k : k + 1], (8, LANES))
    scalars[nk * 8 :, :] = jnp.zeros((8, LANES), jnp.float32)
    scalars[nk * 8 : nk * 8 + 1, 0:nk] = weights[...]


def pack_body(dm, b, coef, to_edge, to_rest, to_in, rhs):
    par = lax.rem(lax.axis_index("slab"), 2)
    nc, nz, nl = dm.nc, dm.nz, dm.nl
    df, xf, yf, zf = [own_planes(dm, coef.at[n]) for n in range(4)]
    bf = own_planes(dm, rhs)
    layers = [jnp.where(par == 0, p, nl - 1 - p) for p in range(nl)]

    def copy(z):
        for p in range(nl):
            block = b[layers[p], pl.ds(z, 8), :]
            for c in range(nc):
                bf[p].put(c, z, block[:, c * LANES : (c + 1) * LANES])

    blocks(0, nz, copy)
    x_face = x_face_of(xf)
    to = Packer(dm, par)
    zs, zm = to.zs, to.zm

    def rest(out, at, two, three):
        to.fill(out, at, dm.half, [
            ("fy2", lambda c, n: yf[two].get(c, zs + n)),
            ("g3", lambda c, n: x_face(c, zs + n, two, three) * bf[three].get(c, zs + n)),
        ])
        to.fill(out, at, dm.more, [("fz2", lambda c, n: zf[two].get(c, zm + n))])

    one, two, three = nl - 1, nl - 2, nl - 3
    to.yz(to_in, dm.at_all, yf, zf, one)
    to.fill(to_in, dm.at_all, nz, [
        ("fx2", lambda c, n: x_face(c, n, one, two)),
        ("d2", lambda c, n: df[two].get(c, n)),
        ("x1", lambda c, n: xf[one].get(c, n)),
        ("d1", lambda c, n: df[one].get(c, n)),
        ("b1", lambda c, n: bf[one].get(c, n)),
        ("b2", lambda c, n: bf[two].get(c, n)),
    ])
    to.third(to_in, dm.at_all, df, three)
    rest(to_in, dm.at_all, two, three)
    to.fill(to_edge, dm.at_edge, nz, [
        ("d1", lambda c, n: df[0].get(c, n)),
        ("b1", lambda c, n: bf[0].get(c, n)),
        ("g2", lambda c, n: x_face(c, n, 0, 1) * bf[1].get(c, n)),
    ])
    rest(to_rest, dm.at_rest, 1, 2)


class Steps:
    def __init__(self, dm, nk, par, acc, shifts):
        self.dm, self.nk, self.acc, self.shifts = dm, nk, acc, shifts
        self.zs = pl.multiple_of(par * dm.half, 8)
        self.zm = pl.multiple_of(par * (dm.nz - dm.more), 8)

    def sweep(self, half, body, unroll=4):
        if half:
            blocks(self.zs, self.dm.half, body, unroll)
        else:
            blocks(0, self.dm.nz, body, unroll)

    def add(self, j, k, value):
        at = (j * self.nk + k) * 8
        self.acc[at : at + 8, :] += value

    def total(self, first, second):
        return functools.reduce(jnp.add, [p * q for p, q in zip(first, second)])

    def tiles(self, plane, z, k=None, d=0):
        return [plane.get(c, z, k, d) for c in range(self.dm.nc)]

    def fused(self, *bodies, unroll=4):
        def body(z):
            for one in bodies:
                one(z)

        self.sweep(False, body, unroll)

    def start(self, d, b, w, r=None, half=False, own=False, run=True):
        def body(z):
            diagonal, rhs = self.tiles(d, z), self.tiles(b, z)
            for k in range(self.nk):
                s = self.shifts[pl.ds(k * 8, 8), :]
                inverse = [1.0 / (t + s) for t in diagonal]
                value = [x * y for x, y in zip(rhs, inverse)]
                for c in range(self.dm.nc):
                    if r is not None:
                        r.put(c, z, inverse[c], k)
                    w.put(c, z, value[c], k)
                if own:
                    self.add(0, k, self.total(rhs, value))

        if not run:
            return body
        self.sweep(half, body, 2)

    def apply(self, v, sides, out, r=None, yz=None, base=None, half=False, moment=None, run=True):
        nc = self.dm.nc

        def body(z):
            xs = [(None if x is None else self.tiles(x, z), w) for x, w in sides]
            if yz is not None:
                fy, fz = yz
                lane, sub = lane_ids(), row_ids()
                y_high = self.tiles(fy, z)
                y_low = from_lower(y_high)
                y_low[0] = jnp.where(lane == 0, 0.0, y_low[0])
                z_high = self.tiles(fz, z)
                z_low = self.tiles(fz, z, d=-1)
                if half:
                    z_low = [jnp.where(sub + z == 0, 0.0, t) for t in z_low]
            for k in range(self.nk):
                value = self.tiles(v, z, k) if v is not None else None
                image = None if base is None else self.tiles(base, z, k)
                parts = []
                if yz is not None:
                    below, above = self.tiles(v, z, k, -1), self.tiles(v, z, k, 1)
                    left, right = from_lower(value), from_higher(value)
                    parts.append([z_low[c] * below[c] + z_high[c] * above[c] for c in range(nc)])
                for x, w in xs:
                    near = self.tiles(w, z, k)
                    parts.append(near if x is None else [x[c] * near[c] for c in range(nc)])
                if yz is not None:
                    parts.append([y_low[c] * left[c] + y_high[c] * right[c] for c in range(nc)])
                for part in parts:
                    image = part if image is None else [p + q for p, q in zip(image, part)]
                if r is None:
                    for c in range(nc):
                        out.put(c, z, image[c], k)
                    continue
                result = [p * q for p, q in zip(image, self.tiles(r, z, k))]
                for c in range(nc):
                    out.put(c, z, result[c], k)
                if moment is not None:
                    self.add(moment, k, self.total(value, image))
                    self.add(moment + 1, k, self.total(result, image))

        if not run:
            return body
        self.sweep(half, body)

    def face_sum(self, v, side=None, yz=None, half=False, run=True):
        nc = self.dm.nc

        def body(z):
            x = self.tiles(side[0], z) if side is not None else None
            if yz is not None:
                y_high, z_high = self.tiles(yz[0], z), self.tiles(yz[1], z)
            for k in range(self.nk):
                value = self.tiles(v, z, k)
                parts = []
                if yz is not None:
                    above, right = self.tiles(v, z, k, 1), from_higher(value)
                    parts.append([z_high[c] * above[c] + y_high[c] * right[c] for c in range(nc)])
                if side is not None:
                    near = self.tiles(side[1], z, k)
                    parts.append([x[c] * near[c] for c in range(nc)])
                image = parts[0]
                if len(parts) == 2:
                    image = [p + q for p, q in zip(*parts)]
                self.add(5, k, 2.0 * self.total(value, image))

        if not run:
            return body
        self.sweep(half, body)


def stack(dm, ref, planes):
    return {p: Plane(ref, PAD + n * dm.slot, dm.nz) for n, p in enumerate(planes)}


def clear_pads(dm, nk, ref):
    for n in range((ref.shape[1] - PAD) // dm.slot + 1):
        for k in range(nk):
            ref[k, n * dm.slot : n * dm.slot + PAD, :] = jnp.zeros((PAD, LANES), jnp.float32)


def halo_planes(dm, st, *parts):
    planes = {}
    for ref, at in parts:
        for name, row in at.items():
            if name in ("fy2", "d3", "g3"):
                planes[name] = Plane(ref, row, dm.half, st.zs)
            elif name in ("fz2", "fx2h"):
                planes[name] = Plane(ref, row, dm.more, st.zm)
            else:
                planes[name] = Plane(ref, row, dm.nz)
    return planes


def near_a_body(
    dm, nk, flats, rhs, from_in, shifts, w0a, w1a, w1h, part1, acc, coef, inv12, inv34,
    extra, w0h, inv5,
):
    par = lax.rem(lax.axis_index("slab"), 2)
    nl, nc, nz = dm.nl, dm.nc, dm.nz
    last = nl - 1
    df, raw_x, yf, zf = [own_planes(dm, flats.at[n]) for n in range(4)]
    xf = own_planes(dm, coef)
    bf = own_planes(dm, rhs)
    st = Steps(dm, nk, par, acc, shifts)
    hp = halo_planes(dm, st, (from_in, dm.at_all))
    acc[...] = jnp.zeros(acc.shape, jnp.float32)
    for ref in (w0a, w1a, w0h, w1h):
        clear_pads(dm, nk, ref)
    d_last, d_next = Plane(extra.at[0], 0, nz), Plane(extra.at[1], 0, nz)

    def edges(z):
        for c in range(nc):
            here, there = raw_x[last].get(c, z), hp["x1"].get(c, z)
            d_last.put(c, z, df[last].get(c, z) + 0.5 * there)
            d_next.put(c, z, hp["d1"].get(c, z) + 0.5 * here)
            for p in range(last):
                xf[p].put(c, z, 0.5 * (raw_x[p].get(c, z) + raw_x[p + 1].get(c, z)))
            xf[last].put(c, z, 0.5 * (here + there))

    blocks(0, nz, edges, 2)
    df[last] = d_last

    W0 = stack(dm, w0a, range(1, nl)) | stack(dm, w0h, (nl, nl + 1))
    far = Plane(w0h, PAD + 2 * dm.slot, dm.half, st.zs)
    W1 = stack(dm, w1a, range(2, nl)) | stack(dm, w1h, (nl, nl + 1))
    R = stack(dm, inv12, (1, 2)) | stack(dm, inv34, range(3, nl + 1)) | stack(dm, inv5, (nl + 1,))

    for p in range(1, nl):
        st.start(df[p], bf[p], W0[p], R[p], own=True)
    st.start(d_next, hp["b1"], W0[nl], R[nl])
    st.start(hp["d2"], hp["b2"], W0[nl + 1], R[nl + 1])
    st.start(hp["d3"], hp["g3"], far, half=True)

    st.apply(W0[1], [(xf[1], W0[2])], Plane(part1, 0, nz), yz=(yf[1], zf[1]))
    for p in range(2, nl):
        st.apply(
            W0[p], [(xf[p - 1], W0[p - 1]), (xf[p], W0[p + 1])], W1[p], R[p], (yf[p], zf[p]), moment=1
        )
    st.apply(
        W0[nl], [(xf[last], W0[last]), (hp["fx2"], W0[nl + 1])], W1[nl], R[nl], (hp["fy1"], hp["fz1"])
    )
    st.apply(
        W0[nl + 1], [(hp["fx2"], W0[nl]), (None, far)], W1[nl + 1], R[nl + 1],
        (hp["fy2"], hp["fz2"]), half=True,
    )


def near_b_body(
    dm, nk, flats, coef, w1a, w1h, acc_in, inv34, from_in, shifts, w2a, part2, acc, w2h,
):
    par = lax.rem(lax.axis_index("slab"), 2)
    nl, nz = dm.nl, dm.nz
    last = nl - 1
    df, raw_x, yf, zf = [own_planes(dm, flats.at[n]) for n in range(4)]
    xf = own_planes(dm, coef)
    st = Steps(dm, nk, par, acc, shifts)
    hp = halo_planes(dm, st, (from_in, dm.at_all))
    acc[...] = acc_in[...]
    for ref in (w2a, w2h):
        clear_pads(dm, nk, ref)
    W1 = stack(dm, w1a, range(2, nl)) | stack(dm, w1h, (nl, nl + 1))
    W2 = stack(dm, w2a, range(3, nl)) | stack(dm, w2h, (nl,))
    R = stack(dm, inv34, range(3, nl + 1))

    st.apply(W1[2], [(xf[2], W1[3])], Plane(part2, 0, nz), yz=(yf[2], zf[2]))
    for p in range(3, nl):
        st.apply(
            W1[p], [(xf[p - 1], W1[p - 1]), (xf[p], W1[p + 1])], W2[p], R[p], (yf[p], zf[p]), moment=3
        )
    st.apply(
        W1[nl], [(xf[last], W1[last]), (hp["fx2"], W1[nl + 1])], W2[nl], R[nl],
        (hp["fy1"], hp["fz1"]), half=True,
    )
    for p in range(3, nl):
        st.face_sum(W2[p], None if p == last else (xf[p], W2[p + 1]), (yf[p], zf[p]))
    st.face_sum(W2[last], (xf[last], W2[nl]), half=True)


def far_0_body(
    dm, nk, flats, rhs, coef, w0a, w1a, w2a, part1, part2, acc_in, inv, from_first, shifts,
    w0b, w1b, w2b, acc, edge, inv_out, part0, part3,
):
    index = lax.axis_index("slab")
    par = lax.rem(index, 2)
    has_off = jnp.where(jnp.logical_and(index > 0, index < lax.axis_size("slab") - 1), 0.5, 0.0)
    nl, nc, nz = dm.nl, dm.nc, dm.nz
    df, raw_x, yf, zf = [own_planes(dm, flats.at[n]) for n in range(4)]
    xf = own_planes(dm, coef)
    st = Steps(dm, nk, par, acc, shifts)
    x1 = Plane(from_first, dm.at_first["x1"], nz)
    acc[...] = acc_in[...]
    for ref in (w0b, w1b, w2b):
        clear_pads(dm, nk, ref)
    d_here, x_edge = [Plane(edge.at[n], 0, nz) for n in range(2)]

    def edges(z):
        for c in range(nc):
            here, there = raw_x[0].get(c, z), x1.get(c, z)
            d_here.put(c, z, df[0].get(c, z) + 0.5 * there)
            x_edge.put(c, z, has_off * (here + there))

    blocks(0, nz, edges, 4)

    W0 = stack(dm, w0a, range(1, nl)) | stack(dm, w0b, (0,))
    W1 = stack(dm, w1a, range(2, nl)) | stack(dm, w1b, (1,))
    W2 = stack(dm, w2a, range(3, nl)) | stack(dm, w2b, (2,))
    R = stack(dm, inv_out, (0,)) | stack(dm, inv, (1, 2))
    I1, I2 = Plane(part1, 0, nz), Plane(part2, 0, nz)

    st.start(d_here, own_planes(dm, rhs)[0], W0[0], R[0], own=True)
    st.apply(W0[1], [(xf[0], W0[0])], W1[1], R[1], base=I1, moment=1)
    st.apply(W1[2], [(xf[1], W1[1])], W2[2], R[2], base=I2, moment=3)
    st.apply(W0[0], [(xf[0], W0[1])], Plane(part0, 0, nz), yz=(yf[0], zf[0]))
    st.apply(W1[1], [(xf[1], W1[2])], Plane(part3, 0, nz), yz=(yf[1], zf[1]))
    st.face_sum(W2[2], (xf[2], W2[3]), (yf[2], zf[2]))


def far_a_body(
    dm, nk, flats, coef, w0b, w1b, w2b, part0, part3, acc_in, inv, inv0, edge, from_edge, shifts,
    w0h, w1c, w2c, part4, acc, inv_out, d_ref,
):
    par = lax.rem(lax.axis_index("slab"), 2)
    nl, nc, nz = dm.nl, dm.nc, dm.nz
    df, raw_x, yf, zf = [own_planes(dm, flats.at[n]) for n in range(4)]
    xf = own_planes(dm, coef)
    st = Steps(dm, nk, par, acc, shifts)
    hp = halo_planes(dm, st, (from_edge, dm.at_edge))
    acc[...] = acc_in[...]
    for ref in (w0h, w1c, w2c):
        clear_pads(dm, nk, ref)
    x_edge, d_next = Plane(edge.at[1], 0, nz), Plane(d_ref, 0, nz)

    def edges(z):
        for c in range(nc):
            d_next.put(c, z, hp["d1"].get(c, z) + 0.5 * raw_x[0].get(c, z))

    blocks(0, nz, edges, 4)

    W0 = stack(dm, w0b, (0,)) | stack(dm, w0h, (-1,))
    W1 = stack(dm, w1b, (1,)) | stack(dm, w1c, (0,))
    W2 = stack(dm, w2b, (2,)) | stack(dm, w2c, (1,))
    R = stack(dm, inv_out, (-1,)) | stack(dm, inv0, (0,)) | stack(dm, inv, (1, 2))

    st.fused(
        st.start(d_next, hp["b1"], W0[-1], R[-1], run=False),
        st.apply(W0[0], [(x_edge, W0[-1])], W1[0], R[0], base=Plane(part0, 0, nz), moment=1, run=False),
    )
    st.fused(
        st.apply(W1[0], [(xf[0], W1[1])], Plane(part4, 0, nz), yz=(yf[0], zf[0]), run=False),
        st.apply(
            W1[1], [(xf[0], W1[0])], W2[1], R[1], base=Plane(part3, 0, nz), moment=3, run=False
        ),
    )
    st.face_sum(W2[1], (xf[1], W2[2]), (yf[1], zf[1]))


def far_b_body(
    dm, nk, flats, coef, w0b, w0h, w1c, w2c, part4, acc_in, edge, inv0, inv1, from_edge,
    swap_a, swap_b, shifts, w2d, acc, w1h, inv_out, shared, w0x,
):
    par = lax.rem(lax.axis_index("slab"), 2)
    side_field = lax.rem(lax.axis_index("field"), 2)
    nl, nc, nz = dm.nl, dm.nc, dm.nz
    df, raw_x, yf, zf = [own_planes(dm, flats.at[n]) for n in range(4)]
    xf = own_planes(dm, coef)
    st = Steps(dm, nk, par, acc, shifts)

    @pl.when(side_field == 0)
    def _():
        shared[0 : dm.rows_swap, :] = swap_a[...]
        shared[dm.rows_swap :, :] = swap_b[...]

    @pl.when(side_field == 1)
    def _():
        shared[0 : dm.rows_swap, :] = swap_b[...]
        shared[dm.rows_swap :, :] = swap_a[...]

    at_x = {name: row + dm.rows_swap for name, row in dm.at_x.items()}
    hp = halo_planes(dm, st, (from_edge, dm.at_edge), (shared, dm.at_yz), (shared, at_x))
    acc[...] = acc_in[...]
    for ref in (w2d, w1h):
        clear_pads(dm, nk, ref)
    x_edge = Plane(edge.at[1], 0, nz)
    W0 = stack(dm, w0b, (0,)) | stack(dm, w0h, (-1,))
    behind = Plane(w0x, 0, nz)
    W1 = stack(dm, w1c, (0,)) | stack(dm, w1h, (-1,))
    W2 = stack(dm, w2c, (1,)) | stack(dm, w2d, (0,))
    R = stack(dm, inv0, (0,)) | stack(dm, inv1, (-1,)) | stack(dm, inv_out, (-2,))
    st.start(hp["d2"], hp["g2"], behind, R[-2])
    st.fused(
        st.apply(
            W0[-1], [(None, behind), (x_edge, W0[0])], W1[-1], R[-1], (hp["fy1"], hp["fz1"]), run=False
        ),
        st.apply(W1[0], [(x_edge, W1[-1])], W2[0], R[0], base=Plane(part4, 0, nz), moment=3, run=False),
    )
    st.face_sum(W2[0], (xf[0], W2[1]), (yf[0], zf[0]))


def far_c_body(
    dm, nk, w0h, w1c, w1h, w2d, acc_in, edge, inv1, inv2, from_edge, rest, shared, shifts,
    moments, acc, w0g, w1g, w2g, w0m,
):
    par = lax.rem(lax.axis_index("slab"), 2)
    nz, nc = dm.nz, dm.nc
    st = Steps(dm, nk, par, acc, shifts)
    at_x = {name: row + dm.rows_swap for name, row in dm.at_x.items()}
    hp = halo_planes(dm, st, (from_edge, dm.at_edge), (rest, dm.at_rest), (shared, dm.at_yz), (shared, at_x))
    acc[...] = acc_in[...]
    x_edge = Plane(edge.at[1], 0, nz)
    far, near, w2 = [Plane(ref, 0, dm.half, st.zs) for ref in (w0g, w1g, w2g)]
    behind = Plane(w0m, PAD, dm.more, st.zm)
    W0 = stack(dm, w0h, (-1,))
    W1 = stack(dm, w1c, (0,)) | stack(dm, w1h, (-1,))
    W2 = stack(dm, w2d, (0,))
    R = stack(dm, inv1, (-1,)) | stack(dm, inv2, (-2,))
    for k in range(nk):
        w0m[k, 0:PAD, :] = jnp.zeros((PAD, LANES), jnp.float32)
        w0m[k, PAD + nc * dm.more :, :] = jnp.zeros((PAD, LANES), jnp.float32)

    def right_side(z):
        for c in range(nc):
            rhs = hp["g2"].get(c, z) / jnp.maximum(hp["fx2h"].get(c, z), 0.1)
            for k in range(nk):
                behind.put(c, z, rhs * R[-2].get(c, z, k), k)

    blocks(st.zm, dm.more, right_side, 5 if dm.more % 40 == 0 else 1)
    st.start(hp["d3"], hp["g3"], far, half=True)
    st.apply(
        behind, [(None, far), (hp["fx2h"], W0[-1])], near, R[-2], (hp["fy2"], hp["fz2"]), half=True
    )
    st.apply(
        W1[-1], [(hp["fx2h"], near), (x_edge, W1[0])], w2, R[-1], (hp["fy1"], hp["fz1"]), half=True
    )
    st.face_sum(W2[0], (x_edge, w2), half=True)

    number = 6 * nk
    sums = jnp.sum(acc[...].reshape(number, 8, LANES), axis=1)
    sums = jnp.concatenate([sums, jnp.zeros((LANES - number, LANES), jnp.float32)], axis=0)
    moments[...] = jnp.sum(jnp.transpose(sums), axis=0, keepdims=True)


def coefficients(sums, nk):
    nu = [sums] + [pltpu.roll(sums, LANES - j * nk, 1) for j in range(1, 6)]

    def inner(p, q, shift=0):
        total = None
        for i, x in enumerate(p):
            for j, y in enumerate(q):
                term = x * y * nu[i + j + shift]
                total = term if total is None else total + term
        return total

    one = jnp.ones((8, LANES), jnp.float32)
    zero = jnp.zeros((8, LANES), jnp.float32)
    z = [one]
    p = [one]
    x = [zero, zero, zero]
    norm = nu[0]
    for number in range(3):
        step = norm / (inner(p, p) - inner(p, p, 1))
        x = [x[j] + step * p[j] if j < len(p) else x[j] for j in range(3)]
        if number < 2:
            p, z = p + [zero], z + [zero]
            z = [z[j] - step * (p[j] - (p[j - 1] if j else zero)) for j in range(len(p))]
            norm_next = inner(z, z)
            beta = norm_next / norm
            p = [z[j] + beta * p[j] for j in range(len(z))]
            norm = norm_next
    return x


def combine_body(dm, nk, moments, scalars, w0a, w0b, w1a, w1b, w1c, w2a, w2b, w2c, w2d, out, made, sems):
    par = lax.rem(lax.axis_index("slab"), 2)
    nl, nc, nz = dm.nl, dm.nc, dm.nz
    sums = jnp.sum(moments[...].reshape(-1, LANES), axis=0, keepdims=True)
    x = coefficients(jnp.broadcast_to(sums, (8, LANES)), nk)
    x = [t * scalars[nk * 8 : nk * 8 + 1, :] for t in x]
    scale = [[jnp.broadcast_to(t[:, k : k + 1], (8, LANES)) for k in range(nk)] for t in x]
    W0 = stack(dm, w0a, range(1, nl)) | stack(dm, w0b, (0,))
    W1 = stack(dm, w1a, range(2, nl)) | stack(dm, w1b, (1,)) | stack(dm, w1c, (0,))
    W2 = stack(dm, w2a, range(3, nl)) | stack(dm, w2b, (2,)) | stack(dm, w2c, (1,)) | stack(dm, w2d, (0,))
    copies = []
    for p in range(nl):

        def body(z, p=p):
            for c in range(nc):
                terms = [
                    scale[j][k] * w[p].get(c, z, k) for j, w in enumerate((W0, W1, W2)) for k in range(nk)
                ]
                while len(terms) > 1:
                    terms = [sum(terms[n : n + 2][1:], terms[n]) for n in range(0, len(terms), 2)]
                made[p, pl.ds(z, 8), c * LANES : (c + 1) * LANES] = terms[0]

        blocks(0, nz, body, 2)
        layer = jnp.where(par == 0, p, nl - 1 - p)
        copy = pltpu.make_async_copy(made.at[p], out.at[layer], sems.at[p])
        copy.start()
        copies.append(copy)
    for copy in copies:
        copy.wait()


def on_device(right_side, cond_x, cond_y, cond_z, kappa_sq, shifts, weights):
    dm = Dims(right_side.shape)
    nk = shifts.shape[0]
    nl = dm.nl
    count = lax.axis_size("slab")
    f32 = jnp.float32
    vmem = pl.BlockSpec(memory_space=pltpu.VMEM)

    def params(mib):
        return pltpu.CompilerParams(vmem_limit_bytes=mib * MIB)

    def shape(*dims):
        return jax.ShapeDtypeStruct(dims, f32)

    def stacked(slots):
        return (nk, dm.stack_rows(slots), LANES)

    own = (dm.stack_rows(nl), LANES)
    half_stack = pltpu.VMEM((nk, dm.nc * dm.half, LANES), f32)
    plane_stack = shape(nk, dm.plane, LANES)
    sums = shape(6 * nk * 8, LANES)

    to_swap, flats, scalars = pl.pallas_call(
        functools.partial(pack_faces_body, dm, nk),
        out_shape=(shape(dm.rows_first, LANES), shape(4, *own), shape(nk * 8 + 8, LANES)),
        in_specs=[vmem] * 5,
        out_specs=(vmem,) * 3,
        scratch_shapes=[pltpu.VMEM(own, f32)],
        compiler_params=params(20),
        name="pack_faces",
    )(jnp.stack([cond_x, cond_y]), cond_z, kappa_sq, shifts[None], weights[None])
    to_edge, to_rest, to_in, rhs = pl.pallas_call(
        functools.partial(pack_body, dm),
        out_shape=(
            shape(dm.rows_edge, LANES), shape(dm.rows_rest, LANES), shape(dm.rows_all, LANES), shape(*own),
        ),
        in_specs=[vmem] * 2,
        out_specs=(vmem,) * 4,
        compiler_params=params(20),
        name="pack",
    )(right_side, flats)

    outward = [pair for i in range(1, count - 1, 2) for pair in ((i, i + 1), (i + 1, i))]
    from_first = lax.ppermute(to_swap, "slab", outward)
    from_in = lax.ppermute(to_in, "slab", [(i, i ^ 1) for i in range(count)])
    fields = lax.axis_size("field")

    def call(body, name, mib, results, scratch, operands, cost):
        return pl.pallas_call(
            functools.partial(body, dm, nk),
            out_shape=results,
            in_specs=[vmem] * (len(operands) + 1),
            out_specs=(vmem,) * len(results),
            scratch_shapes=scratch,
            compiler_params=params(mib),
            cost_estimate=pl.CostEstimate(
                flops=10**6, bytes_accessed=cost * 3 * 10**6, transcendentals=0
            ),
            name=name,
        )(*operands, scalars)

    def wide(slots):
        return shape(*stacked(slots))

    def held(slots):
        return pltpu.VMEM(stacked(slots), f32)

    w0a, w1a, w1h, part1, acc, coef, inv12, inv34 = call(
        near_a_body, "near_a", 20,
        (wide(nl - 1), wide(nl - 2), wide(2), plane_stack, sums, shape(*own), wide(2), wide(nl - 2)),
        [pltpu.VMEM((2, dm.plane, LANES), f32), held(3), held(1)],
        (flats, rhs, from_in), 6,
    )
    to_edge, acc = lax.optimization_barrier((to_edge, acc))
    from_edge = lax.ppermute(to_edge, "slab", outward)
    w2a, part2, acc = call(
        near_b_body, "near_b", 20,
        (wide(nl - 3), plane_stack, sums),
        [held(1)],
        (flats, coef, w1a, w1h, acc, inv34, from_in), 3,
    )
    from_first, acc = lax.optimization_barrier((from_first, acc))
    swap_a = from_first[: dm.rows_swap]
    swap_b = lax.ppermute(swap_a, "field", [(i, i ^ 1) for i in range(fields)])
    w0b, w1b, w2b, acc, edge, inv0, part0, part3 = call(
        far_0_body, "far_0", 20,
        (wide(1), wide(1), wide(1), sums, shape(2, dm.plane, LANES), wide(1), plane_stack, plane_stack),
        [],
        (flats, rhs, coef, w0a, w1a, w2a, part1, part2, acc, inv12, from_first), 2,
    )
    to_rest, acc = lax.optimization_barrier((to_rest, acc))
    from_rest = lax.ppermute(to_rest, "slab", outward)
    w0h, w1c, w2c, part4, acc, inv1 = call(
        far_a_body, "far_a", 20,
        (wide(1), wide(1), wide(1), plane_stack, sums, wide(1)),
        [pltpu.VMEM((dm.plane, LANES), f32)],
        (flats, coef, w0b, w1b, w2b, part0, part3, acc, inv12, inv0, edge, from_edge), 4,
    )
    w2d, acc, w1h, inv2, shared = call(
        far_b_body, "far_b", 20,
        (wide(1), sums, wide(1), wide(1), shape(2 * dm.rows_swap, LANES)),
        [pltpu.VMEM((nk, dm.plane, LANES), f32)],
        (flats, coef, w0b, w0h, w1c, w2c, part4, acc, edge, inv0, inv1, from_edge, swap_a, swap_b), 3,
    )
    moments, _ = call(
        far_c_body, "far_c", 20,
        (shape(1, LANES), sums),
        [half_stack] * 3
        + [pltpu.VMEM((nk, dm.nc * dm.more + 2 * PAD, LANES), f32)],
        (w0h, w1c, w1h, w2d, acc, edge, inv1, inv2, from_edge, from_rest, shared), 2,
    )

    everywhere = jnp.broadcast_to(moments[None], (count, 1, LANES))
    gathered = lax.all_to_all(everywhere, "slab", 0, 0)

    return pl.pallas_call(
        functools.partial(combine_body, dm, nk),
        out_shape=jax.ShapeDtypeStruct(right_side.shape, f32),
        in_specs=[vmem] * 11,
        out_specs=pl.BlockSpec(memory_space=pl.ANY),
        scratch_shapes=[pltpu.VMEM(right_side.shape, f32), pltpu.SemaphoreType.DMA((nl,))],
        compiler_params=params(20),
        name="combine",
    )(gathered, scalars, w0a, w0b, w1a, w1b, w1c, w2a, w2b, w2c, w2d)


def solution(mesh):
    return jax.shard_map(
        on_device,
        mesh=mesh,
        in_specs=(
            P(("field", "slab"), None, None),
            P("slab", None, None),
            P("slab", None, None),
            P("slab", None, None),
            P("slab", None, None),
            P(),
            P(),
        ),
        out_specs=P(("field", "slab"), None, None),
        check_vma=False,
    )
```

```python
import functools
import jax
import jax.numpy as jnp
from jax import lax
from jax.experimental import pallas as pl
from jax.experimental.pallas import tpu as pltpu
from jax.sharding import PartitionSpec as P

LANES = 128
PAD = 8
MIB = 1024 * 1024


class Dims:
    def __init__(self, shape):
        self.nl, self.nz, self.ny = shape
        self.nc = self.ny // LANES
        self.plane = self.nc * self.nz
        self.slot = self.plane + PAD
        self.half = self.nz // 2
        self.more = self.half + 8
        full, half = self.plane, self.nc * self.half
        more = self.nc * self.more
        yz = [("pad", PAD), ("fz1", full), ("fy1", full)]
        x = [("fx2h", more), ("d2", full), ("d3", half)]
        edge = [("d1", full), ("b1", full), ("g2", full)]
        rest = [("fy2", half), ("g3", half), ("fz2", more)]
        self.at_yz, self.rows_yz = self.layout(yz)
        self.at_x, self.rows_x = self.layout(x)
        self.rows_swap = max(self.rows_yz, self.rows_x)
        self.at_first, self.rows_first = self.layout([("swapped", self.rows_swap), ("x1", full)])
        self.at_edge, self.rows_edge = self.layout(edge)
        self.at_rest, self.rows_rest = self.layout(rest)
        near = [("fx2", full), ("d2", full), ("x1", full), ("d1", full), ("b1", full), ("b2", full)]
        self.at_all, self.rows_all = self.layout(yz + near + [("d3", half)] + rest)

    @staticmethod
    def layout(parts):
        at, total = {}, 0
        for name, rows in parts:
            at[name] = total
            total += rows
        return at, total

    def stack_rows(self, slots):
        return slots * self.slot + PAD


class Plane:
    def __init__(self, ref, base, stride, zoff=0):
        self.ref, self.base, self.stride, self.zoff = ref, base, stride, zoff

    def row(self, c, z):
        return pl.multiple_of(z - self.zoff, 8) + (self.base + c * self.stride)

    def get(self, c, z, k=None, d=0):
        rows = pl.ds(self.row(c, z) + d, 8)
        return self.ref[rows, :] if k is None else self.ref[k, rows, :]

    def put(self, c, z, value, k=None):
        rows = pl.ds(self.row(c, z), 8)
        if k is None:
            self.ref[rows, :] = value
        else:
            self.ref[k, rows, :] = value


def lane_ids():
    return lax.broadcasted_iota(jnp.int32, (8, LANES), 1)


def row_ids():
    return lax.broadcasted_iota(jnp.int32, (8, LANES), 0)


def from_higher(tiles):
    lane = lane_ids()
    n = len(tiles)
    return [
        pltpu.roll(jnp.where(lane == 0, tiles[(c + 1) % n], tiles[c]), LANES - 1, 1)
        for c in range(n)
    ]


def from_lower(tiles):
    lane = lane_ids()
    n = len(tiles)
    return [
        pltpu.roll(jnp.where(lane == LANES - 1, tiles[(c - 1) % n], tiles[c]), 1, 1)
        for c in range(n)
    ]


def blocks(z_from, z_count, body, unroll=1):
    def step(n, carry):
        for u in range(unroll):
            body(pl.multiple_of(z_from + (n * unroll + u) * 8, 8))
        return carry

    lax.fori_loop(0, z_count // (8 * unroll), step, 0)


def own_planes(dm, ref):
    return [Plane(ref, PAD + p * dm.slot, dm.nz) for p in range(dm.nl)]


def prepare(dm, par, cx, cy, cz, kappa, flats):
    nc, nz, nl = dm.nc, dm.nz, dm.nl
    df, xf, yf, zf, tf = [own_planes(dm, ref) for ref in flats]
    for ref in (flats[3], flats[4]):
        for p in range(nl + 1):
            ref[p * dm.slot : p * dm.slot + PAD, :] = jnp.zeros((PAD, LANES), jnp.float32)
    layers = [jnp.where(par == 0, p, nl - 1 - p) for p in range(nl)]

    def copy(z):
        for p in range(nl):
            for src, dst in ((cx, xf), (cz, tf)):
                block = src[layers[p], pl.ds(z, 8), :]
                for c in range(nc):
                    dst[p].put(c, z, block[:, c * LANES : (c + 1) * LANES])

    blocks(0, nz, copy)

    def faces(p, z):
        lane, sub = lane_ids(), row_ids()
        conds = cy[layers[p], pl.ds(z, 8), :]
        kap = kappa[layers[p], pl.ds(z, 8), :]
        ys = [conds[:, c * LANES : (c + 1) * LANES] for c in range(nc)]
        up, down = from_higher(ys), from_lower(ys)
        up[-1] = jnp.where(lane == LANES - 1, 0.0, up[-1])
        down[0] = jnp.where(lane == 0, 0.0, down[0])
        for c in range(nc):
            high_y = 0.5 * (ys[c] + up[c])
            low_y = 0.5 * (ys[c] + down[c])
            here = tf[p].get(c, z)
            high_z = 0.5 * (here + jnp.where(sub + z == nz - 1, 0.0, tf[p].get(c, z, d=1)))
            low_z = 0.5 * (here + jnp.where(sub + z == 0, 0.0, tf[p].get(c, z, d=-1)))
            mine = xf[p].get(c, z)
            total = kap[:, c * LANES : (c + 1) * LANES]
            total = total + 0.5 * (mine + xf[p - 1].get(c, z) if p > 0 else mine)
            total = total + 0.5 * (mine + xf[p + 1].get(c, z) if p < nl - 1 else mine)
            df[p].put(c, z, total + low_z + high_z + low_y + high_y)
            if c == nc - 1:
                high_y = jnp.where(lane == LANES - 1, 0.0, high_y)
            yf[p].put(c, z, high_y)
            zf[p].put(c, z, jnp.where(sub + z == nz - 1, 0.0, high_z))

    def all_faces(z):
        for p in range(nl):
            faces(p, z)

    blocks(0, nz, all_faces)


class Packer:
    def __init__(self, dm, par):
        self.dm = dm
        self.zs = pl.multiple_of((1 - par) * dm.half, 8)
        self.zm = pl.multiple_of((1 - par) * (dm.nz - dm.more), 8)

    def fill(self, out, at, z_count, sources):
        def body(n):
            for name, value in sources:
                for c in range(self.dm.nc):
                    out[pl.ds(pl.multiple_of(n, 8) + (at[name] + c * z_count), 8), :] = value(c, n)

        blocks(0, z_count, body, min(4, z_count // 8) if z_count % 32 == 0 else 1)

    def yz(self, out, at, yf, zf, one):
        out[at["pad"] : at["pad"] + PAD, :] = jnp.zeros((PAD, LANES), jnp.float32)
        self.fill(out, at, self.dm.nz, [
            ("fz1", lambda c, n: zf[one].get(c, n)),
            ("fy1", lambda c, n: yf[one].get(c, n)),
        ])

    def third(self, out, at, df, three):
        self.fill(out, at, self.dm.half, [("d3", lambda c, n: df[three].get(c, self.zs + n))])


def x_face_of(xf):
    return lambda c, z, one, two: 0.5 * (xf[one].get(c, z) + xf[two].get(c, z))


def pack_faces_body(dm, nk, conds, cz, kappa, shifts, weights, to_swap, coef, scalars, temp):
    par = lax.rem(lax.axis_index("slab"), 2)
    side_field = lax.rem(lax.axis_index("field"), 2)
    prepare(dm, par, conds.at[0], conds.at[1], cz, kappa, [coef.at[n] for n in range(4)] + [temp])
    df, xf, yf, zf = [own_planes(dm, coef.at[n]) for n in range(4)]
    x_face = x_face_of(xf)
    to = Packer(dm, par)

    @pl.when(side_field == 0)
    def _():
        to.yz(to_swap, dm.at_yz, yf, zf, 0)
        if dm.rows_swap > dm.rows_yz:
            to_swap[dm.rows_yz : dm.rows_swap, :] = jnp.zeros((dm.rows_swap - dm.rows_yz, LANES), jnp.float32)

    @pl.when(side_field == 1)
    def _():
        to.fill(to_swap, dm.at_x, dm.more, [("fx2h", lambda c, n: x_face(c, to.zm + n, 0, 1))])
        to.fill(to_swap, dm.at_x, dm.nz, [("d2", lambda c, n: df[1].get(c, n))])
        to.third(to_swap, dm.at_x, df, 2)

    to.fill(to_swap, dm.at_first, dm.nz, [("x1", lambda c, n: xf[0].get(c, n))])
    for k in range(nk):
        scalars[k * 8 : k * 8 + 8, :] = jnp.broadcast_to(shifts[:, k : k + 1], (8, LANES))
    scalars[nk * 8 :, :] = jnp.zeros((8, LANES), jnp.float32)
    scalars[nk * 8 : nk * 8 + 1, 0:nk] = weights[...]


def pack_body(dm, b, coef, to_edge, to_rest, to_in, rhs):
    par = lax.rem(lax.axis_index("slab"), 2)
    nc, nz, nl = dm.nc, dm.nz, dm.nl
    df, xf, yf, zf = [own_planes(dm, coef.at[n]) for n in range(4)]
    bf = own_planes(dm, rhs)
    layers = [jnp.where(par == 0, p, nl - 1 - p) for p in range(nl)]

    def copy(z):
        for p in range(nl):
            block = b[layers[p], pl.ds(z, 8), :]
            for c in range(nc):
                bf[p].put(c, z, block[:, c * LANES : (c + 1) * LANES])

    blocks(0, nz, copy)
    x_face = x_face_of(xf)
    to = Packer(dm, par)
    zs, zm = to.zs, to.zm

    def rest(out, at, two, three):
        to.fill(out, at, dm.half, [
            ("fy2", lambda c, n: yf[two].get(c, zs + n)),
            ("g3", lambda c, n: x_face(c, zs + n, two, three) * bf[three].get(c, zs + n)),
        ])
        to.fill(out, at, dm.more, [("fz2", lambda c, n: zf[two].get(c, zm + n))])

    one, two, three = nl - 1, nl - 2, nl - 3
    to.yz(to_in, dm.at_all, yf, zf, one)
    to.fill(to_in, dm.at_all, nz, [
        ("fx2", lambda c, n: x_face(c, n, one, two)),
        ("d2", lambda c, n: df[two].get(c, n)),
        ("x1", lambda c, n: xf[one].get(c, n)),
        ("d1", lambda c, n: df[one].get(c, n)),
        ("b1", lambda c, n: bf[one].get(c, n)),
        ("b2", lambda c, n: bf[two].get(c, n)),
    ])
    to.third(to_in, dm.at_all, df, three)
    rest(to_in, dm.at_all, two, three)
    to.fill(to_edge, dm.at_edge, nz, [
        ("d1", lambda c, n: df[0].get(c, n)),
        ("b1", lambda c, n: bf[0].get(c, n)),
        ("g2", lambda c, n: x_face(c, n, 0, 1) * bf[1].get(c, n)),
    ])
    rest(to_rest, dm.at_rest, 1, 2)


class Steps:
    def __init__(self, dm, nk, par, acc, shifts, unroll=4):
        self.unroll = unroll
        self.dm, self.nk, self.acc, self.shifts = dm, nk, acc, shifts
        self.zs = pl.multiple_of(par * dm.half, 8)
        self.zm = pl.multiple_of(par * (dm.nz - dm.more), 8)

    def sweep(self, half, body, unroll=None):
        unroll = unroll or self.unroll
        if half:
            blocks(self.zs, self.dm.half, body, min(unroll, 4))
        else:
            blocks(0, self.dm.nz, body, unroll)

    def add(self, j, k, value):
        at = (j * self.nk + k) * 8
        self.acc[at : at + 8, :] += value

    def total(self, first, second):
        return functools.reduce(jnp.add, [p * q for p, q in zip(first, second)])

    def tiles(self, plane, z, k=None, d=0):
        return [plane.get(c, z, k, d) for c in range(self.dm.nc)]

    def fused(self, *bodies, unroll=None):
        def body(z):
            for one in bodies:
                one(z)

        self.sweep(False, body, unroll)

    def start(self, d, b, w, r=None, half=False, own=False, run=True):
        def body(z):
            diagonal, rhs = self.tiles(d, z), self.tiles(b, z)
            for k in range(self.nk):
                s = self.shifts[pl.ds(k * 8, 8), :]
                inverse = [1.0 / (t + s) for t in diagonal]
                value = [x * y for x, y in zip(rhs, inverse)]
                for c in range(self.dm.nc):
                    if r is not None:
                        r.put(c, z, inverse[c], k)
                    w.put(c, z, value[c], k)
                if own:
                    self.add(0, k, self.total(rhs, value))

        if not run:
            return body
        self.sweep(half, body, 4)

    def apply(self, v, sides, out, r=None, yz=None, base=None, half=False, moment=None, run=True):
        nc = self.dm.nc

        def body(z):
            xs = [(None if x is None else self.tiles(x, z), w) for x, w in sides]
            if yz is not None:
                fy, fz = yz
                lane, sub = lane_ids(), row_ids()
                y_high = self.tiles(fy, z)
                y_low = from_lower(y_high)
                y_low[0] = jnp.where(lane == 0, 0.0, y_low[0])
                z_high = self.tiles(fz, z)
                z_low = self.tiles(fz, z, d=-1)
                if half:
                    z_low = [jnp.where(sub + z == 0, 0.0, t) for t in z_low]
            for k in range(self.nk):
                value = self.tiles(v, z, k) if v is not None else None
                image = None if base is None else self.tiles(base, z, k)
                parts = []
                if yz is not None:
                    below, above = self.tiles(v, z, k, -1), self.tiles(v, z, k, 1)
                    left, right = from_lower(value), from_higher(value)
                    parts.append([z_low[c] * below[c] + z_high[c] * above[c] for c in range(nc)])
                for x, w in xs:
                    near = self.tiles(w, z, k)
                    parts.append(near if x is None else [x[c] * near[c] for c in range(nc)])
                if yz is not None:
                    parts.append([y_low[c] * left[c] + y_high[c] * right[c] for c in range(nc)])
                for part in parts:
                    image = part if image is None else [p + q for p, q in zip(image, part)]
                if r is None:
                    for c in range(nc):
                        out.put(c, z, image[c], k)
                    continue
                result = [p * q for p, q in zip(image, self.tiles(r, z, k))]
                for c in range(nc):
                    out.put(c, z, result[c], k)
                if moment is not None:
                    self.add(moment, k, self.total(value, image))
                    self.add(moment + 1, k, self.total(result, image))

        if not run:
            return body
        self.sweep(half, body)

    def face_sum(self, v, side=None, yz=None, half=False, run=True):
        nc = self.dm.nc

        def body(z):
            x = self.tiles(side[0], z) if side is not None else None
            if yz is not None:
                y_high, z_high = self.tiles(yz[0], z), self.tiles(yz[1], z)
            for k in range(self.nk):
                value = self.tiles(v, z, k)
                parts = []
                if yz is not None:
                    above, right = self.tiles(v, z, k, 1), from_higher(value)
                    parts.append([z_high[c] * above[c] + y_high[c] * right[c] for c in range(nc)])
                if side is not None:
                    near = self.tiles(side[1], z, k)
                    parts.append([x[c] * near[c] for c in range(nc)])
                image = parts[0]
                if len(parts) == 2:
                    image = [p + q for p, q in zip(*parts)]
                self.add(5, k, 2.0 * self.total(value, image))

        if not run:
            return body
        self.sweep(half, body)


def stack(dm, ref, planes):
    return {p: Plane(ref, PAD + n * dm.slot, dm.nz) for n, p in enumerate(planes)}


def clear_pads(dm, nk, ref):
    for n in range((ref.shape[1] - PAD) // dm.slot + 1):
        for k in range(nk):
            ref[k, n * dm.slot : n * dm.slot + PAD, :] = jnp.zeros((PAD, LANES), jnp.float32)


def halo_planes(dm, st, *parts):
    planes = {}
    for ref, at in parts:
        for name, row in at.items():
            if name in ("fy2", "d3", "g3"):
                planes[name] = Plane(ref, row, dm.half, st.zs)
            elif name in ("fz2", "fx2h"):
                planes[name] = Plane(ref, row, dm.more, st.zm)
            else:
                planes[name] = Plane(ref, row, dm.nz)
    return planes


def near_a_body(
    dm, nk, flats, rhs, from_in, shifts, w0a, w1a, w1h, part1, acc, coef, inv12, inv34,
    extra, w0h, inv5,
):
    par = lax.rem(lax.axis_index("slab"), 2)
    nl, nc, nz = dm.nl, dm.nc, dm.nz
    last = nl - 1
    df, raw_x, yf, zf = [own_planes(dm, flats.at[n]) for n in range(4)]
    xf = own_planes(dm, coef)
    bf = own_planes(dm, rhs)
    st = Steps(dm, nk, par, acc, shifts)
    hp = halo_planes(dm, st, (from_in, dm.at_all))
    acc[...] = jnp.zeros(acc.shape, jnp.float32)
    for ref in (w0a, w1a, w0h, w1h):
        clear_pads(dm, nk, ref)
    d_last, d_next = Plane(extra.at[0], 0, nz), Plane(extra.at[1], 0, nz)

    def edges(z):
        for c in range(nc):
            here, there = raw_x[last].get(c, z), hp["x1"].get(c, z)
            d_last.put(c, z, df[last].get(c, z) + 0.5 * there)
            d_next.put(c, z, hp["d1"].get(c, z) + 0.5 * here)
            for p in range(last):
                xf[p].put(c, z, 0.5 * (raw_x[p].get(c, z) + raw_x[p + 1].get(c, z)))
            xf[last].put(c, z, 0.5 * (here + there))

    blocks(0, nz, edges, 2)
    df[last] = d_last

    W0 = stack(dm, w0a, range(1, nl)) | stack(dm, w0h, (nl, nl + 1))
    far = Plane(w0h, PAD + 2 * dm.slot, dm.half, st.zs)
    W1 = stack(dm, w1a, range(2, nl)) | stack(dm, w1h, (nl, nl + 1))
    R = stack(dm, inv12, (1, 2)) | stack(dm, inv34, range(3, nl + 1)) | stack(dm, inv5, (nl + 1,))

    for p in range(1, nl):
        st.start(df[p], bf[p], W0[p], R[p], own=True)
    st.start(d_next, hp["b1"], W0[nl], R[nl])
    st.start(hp["d2"], hp["b2"], W0[nl + 1], R[nl + 1])
    st.start(hp["d3"], hp["g3"], far, half=True)

    st.apply(W0[1], [(xf[1], W0[2])], Plane(part1, 0, nz), yz=(yf[1], zf[1]))
    for p in range(2, nl):
        st.apply(
            W0[p], [(xf[p - 1], W0[p - 1]), (xf[p], W0[p + 1])], W1[p], R[p], (yf[p], zf[p]), moment=1
        )
    st.apply(
        W0[nl], [(xf[last], W0[last]), (hp["fx2"], W0[nl + 1])], W1[nl], R[nl], (hp["fy1"], hp["fz1"])
    )
    st.apply(
        W0[nl + 1], [(hp["fx2"], W0[nl]), (None, far)], W1[nl + 1], R[nl + 1],
        (hp["fy2"], hp["fz2"]), half=True,
    )


def near_b_body(
    dm, nk, flats, coef, w1a, w1h, acc_in, inv34, from_in, shifts, w2a, part2, acc, w2h,
):
    par = lax.rem(lax.axis_index("slab"), 2)
    nl, nz = dm.nl, dm.nz
    last = nl - 1
    df, raw_x, yf, zf = [own_planes(dm, flats.at[n]) for n in range(4)]
    xf = own_planes(dm, coef)
    st = Steps(dm, nk, par, acc, shifts)
    hp = halo_planes(dm, st, (from_in, dm.at_all))
    acc[...] = acc_in[...]
    for ref in (w2a, w2h):
        clear_pads(dm, nk, ref)
    W1 = stack(dm, w1a, range(2, nl)) | stack(dm, w1h, (nl, nl + 1))
    W2 = stack(dm, w2a, range(3, nl)) | stack(dm, w2h, (nl,))
    R = stack(dm, inv34, range(3, nl + 1))

    st.apply(W1[2], [(xf[2], W1[3])], Plane(part2, 0, nz), yz=(yf[2], zf[2]))
    for p in range(3, nl):
        st.apply(
            W1[p], [(xf[p - 1], W1[p - 1]), (xf[p], W1[p + 1])], W2[p], R[p], (yf[p], zf[p]), moment=3
        )
    st.apply(
        W1[nl], [(xf[last], W1[last]), (hp["fx2"], W1[nl + 1])], W2[nl], R[nl],
        (hp["fy1"], hp["fz1"]), half=True,
    )
    for p in range(3, nl):
        st.face_sum(W2[p], None if p == last else (xf[p], W2[p + 1]), (yf[p], zf[p]))
    st.face_sum(W2[last], (xf[last], W2[nl]), half=True)


def far_0_body(
    dm, nk, flats, rhs, coef, w0a, w1a, w2a, part1, part2, acc_in, inv, from_first, shifts,
    w0b, w1b, w2b, acc, edge, inv_out, part0, part3,
):
    index = lax.axis_index("slab")
    par = lax.rem(index, 2)
    has_off = jnp.where(jnp.logical_and(index > 0, index < lax.axis_size("slab") - 1), 0.5, 0.0)
    nl, nc, nz = dm.nl, dm.nc, dm.nz
    df, raw_x, yf, zf = [own_planes(dm, flats.at[n]) for n in range(4)]
    xf = own_planes(dm, coef)
    st = Steps(dm, nk, par, acc, shifts, 8)
    x1 = Plane(from_first, dm.at_first["x1"], nz)
    acc[...] = acc_in[...]
    for ref in (w0b, w1b, w2b):
        clear_pads(dm, nk, ref)
    d_here, x_edge = [Plane(edge.at[n], 0, nz) for n in range(2)]

    def edges(z):
        for c in range(nc):
            here, there = raw_x[0].get(c, z), x1.get(c, z)
            d_here.put(c, z, df[0].get(c, z) + 0.5 * there)
            x_edge.put(c, z, has_off * (here + there))

    blocks(0, nz, edges, 4)

    W0 = stack(dm, w0a, range(1, nl)) | stack(dm, w0b, (0,))
    W1 = stack(dm, w1a, range(2, nl)) | stack(dm, w1b, (1,))
    W2 = stack(dm, w2a, range(3, nl)) | stack(dm, w2b, (2,))
    R = stack(dm, inv_out, (0,)) | stack(dm, inv, (1, 2))
    I1, I2 = Plane(part1, 0, nz), Plane(part2, 0, nz)

    st.start(d_here, own_planes(dm, rhs)[0], W0[0], R[0], own=True)
    st.apply(W0[1], [(xf[0], W0[0])], W1[1], R[1], base=I1, moment=1)
    st.apply(W1[2], [(xf[1], W1[1])], W2[2], R[2], base=I2, moment=3)
    st.apply(W0[0], [(xf[0], W0[1])], Plane(part0, 0, nz), yz=(yf[0], zf[0]))
    st.apply(W1[1], [(xf[1], W1[2])], Plane(part3, 0, nz), yz=(yf[1], zf[1]))
    st.face_sum(W2[2], (xf[2], W2[3]), (yf[2], zf[2]))


def far_a_body(
    dm, nk, flats, coef, w0b, w1b, w2b, part0, part3, acc_in, inv, inv0, edge, from_edge, shifts,
    w0h, w1c, w2c, part4, acc, inv_out, d_ref,
):
    par = lax.rem(lax.axis_index("slab"), 2)
    nl, nc, nz = dm.nl, dm.nc, dm.nz
    df, raw_x, yf, zf = [own_planes(dm, flats.at[n]) for n in range(4)]
    xf = own_planes(dm, coef)
    st = Steps(dm, nk, par, acc, shifts, 8)
    hp = halo_planes(dm, st, (from_edge, dm.at_edge))
    acc[...] = acc_in[...]
    for ref in (w0h, w1c, w2c):
        clear_pads(dm, nk, ref)
    x_edge, d_next = Plane(edge.at[1], 0, nz), Plane(d_ref, 0, nz)

    def edges(z):
        for c in range(nc):
            d_next.put(c, z, hp["d1"].get(c, z) + 0.5 * raw_x[0].get(c, z))

    blocks(0, nz, edges, 4)

    W0 = stack(dm, w0b, (0,)) | stack(dm, w0h, (-1,))
    W1 = stack(dm, w1b, (1,)) | stack(dm, w1c, (0,))
    W2 = stack(dm, w2b, (2,)) | stack(dm, w2c, (1,))
    R = stack(dm, inv_out, (-1,)) | stack(dm, inv0, (0,)) | stack(dm, inv, (1, 2))

    st.fused(
        st.start(d_next, hp["b1"], W0[-1], R[-1], run=False),
        st.apply(W0[0], [(x_edge, W0[-1])], W1[0], R[0], base=Plane(part0, 0, nz), moment=1, run=False),
    )
    st.fused(
        st.apply(W1[0], [(xf[0], W1[1])], Plane(part4, 0, nz), yz=(yf[0], zf[0]), run=False),
        st.apply(
            W1[1], [(xf[0], W1[0])], W2[1], R[1], base=Plane(part3, 0, nz), moment=3, run=False
        ),
    )
    st.face_sum(W2[1], (xf[1], W2[2]), (yf[1], zf[1]))


def far_b_body(
    dm, nk, flats, coef, w0b, w0h, w1c, w2c, part4, acc_in, edge, inv0, inv1, from_edge,
    swap_a, swap_b, shifts, w2d, acc, w1h, inv_out, shared, w0x,
):
    par = lax.rem(lax.axis_index("slab"), 2)
    side_field = lax.rem(lax.axis_index("field"), 2)
    nl, nc, nz = dm.nl, dm.nc, dm.nz
    df, raw_x, yf, zf = [own_planes(dm, flats.at[n]) for n in range(4)]
    xf = own_planes(dm, coef)
    st = Steps(dm, nk, par, acc, shifts)

    @pl.when(side_field == 0)
    def _():
        shared[0 : dm.rows_swap, :] = swap_a[...]
        shared[dm.rows_swap :, :] = swap_b[...]

    @pl.when(side_field == 1)
    def _():
        shared[0 : dm.rows_swap, :] = swap_b[...]
        shared[dm.rows_swap :, :] = swap_a[...]

    at_x = {name: row + dm.rows_swap for name, row in dm.at_x.items()}
    hp = halo_planes(dm, st, (from_edge, dm.at_edge), (shared, dm.at_yz), (shared, at_x))
    acc[...] = acc_in[...]
    for ref in (w2d, w1h):
        clear_pads(dm, nk, ref)
    x_edge = Plane(edge.at[1], 0, nz)
    W0 = stack(dm, w0b, (0,)) | stack(dm, w0h, (-1,))
    behind = Plane(w0x, 0, nz)
    W1 = stack(dm, w1c, (0,)) | stack(dm, w1h, (-1,))
    W2 = stack(dm, w2c, (1,)) | stack(dm, w2d, (0,))
    R = stack(dm, inv0, (0,)) | stack(dm, inv1, (-1,)) | stack(dm, inv_out, (-2,))
    st.start(hp["d2"], hp["g2"], behind, R[-2])
    st.fused(
        st.apply(
            W0[-1], [(None, behind), (x_edge, W0[0])], W1[-1], R[-1], (hp["fy1"], hp["fz1"]), run=False
        ),
        st.apply(W1[0], [(x_edge, W1[-1])], W2[0], R[0], base=Plane(part4, 0, nz), moment=3, run=False),
    )
    st.face_sum(W2[0], (xf[0], W2[1]), (yf[0], zf[0]))


def far_c_body(
    dm, nk, w0h, w1c, w1h, w2d, acc_in, edge, inv1, inv2, from_edge, rest, shared, shifts,
    moments, acc, w0g, w1g, w2g, w0m,
):
    par = lax.rem(lax.axis_index("slab"), 2)
    nz, nc = dm.nz, dm.nc
    st = Steps(dm, nk, par, acc, shifts)
    at_x = {name: row + dm.rows_swap for name, row in dm.at_x.items()}
    hp = halo_planes(dm, st, (from_edge, dm.at_edge), (rest, dm.at_rest), (shared, dm.at_yz), (shared, at_x))
    acc[...] = acc_in[...]
    x_edge = Plane(edge.at[1], 0, nz)
    far, near, w2 = [Plane(ref, 0, dm.half, st.zs) for ref in (w0g, w1g, w2g)]
    behind = Plane(w0m, PAD, dm.more, st.zm)
    W0 = stack(dm, w0h, (-1,))
    W1 = stack(dm, w1c, (0,)) | stack(dm, w1h, (-1,))
    W2 = stack(dm, w2d, (0,))
    R = stack(dm, inv1, (-1,)) | stack(dm, inv2, (-2,))
    for k in range(nk):
        w0m[k, 0:PAD, :] = jnp.zeros((PAD, LANES), jnp.float32)
        w0m[k, PAD + nc * dm.more :, :] = jnp.zeros((PAD, LANES), jnp.float32)

    def right_side(z):
        for c in range(nc):
            rhs = hp["g2"].get(c, z) / jnp.maximum(hp["fx2h"].get(c, z), 0.1)
            for k in range(nk):
                behind.put(c, z, rhs * R[-2].get(c, z, k), k)

    blocks(st.zm, dm.more, right_side, 5 if dm.more % 40 == 0 else 1)
    st.start(hp["d3"], hp["g3"], far, half=True)
    st.apply(
        behind, [(None, far), (hp["fx2h"], W0[-1])], near, R[-2], (hp["fy2"], hp["fz2"]), half=True
    )
    st.apply(
        W1[-1], [(hp["fx2h"], near), (x_edge, W1[0])], w2, R[-1], (hp["fy1"], hp["fz1"]), half=True
    )
    st.face_sum(W2[0], (x_edge, w2), half=True)

    number = 6 * nk
    sums = jnp.sum(acc[...].reshape(number, 8, LANES), axis=1)
    sums = jnp.concatenate([sums, jnp.zeros((LANES - number, LANES), jnp.float32)], axis=0)
    moments[...] = jnp.sum(jnp.transpose(sums), axis=0, keepdims=True)


def coefficients(sums, nk):
    nu = [sums] + [pltpu.roll(sums, LANES - j * nk, 1) for j in range(1, 6)]

    def inner(p, q, shift=0):
        total = None
        for i, x in enumerate(p):
            for j, y in enumerate(q):
                term = x * y * nu[i + j + shift]
                total = term if total is None else total + term
        return total

    one = jnp.ones((8, LANES), jnp.float32)
    zero = jnp.zeros((8, LANES), jnp.float32)
    z = [one]
    p = [one]
    x = [zero, zero, zero]
    norm = nu[0]
    for number in range(3):
        step = norm / (inner(p, p) - inner(p, p, 1))
        x = [x[j] + step * p[j] if j < len(p) else x[j] for j in range(3)]
        if number < 2:
            p, z = p + [zero], z + [zero]
            z = [z[j] - step * (p[j] - (p[j - 1] if j else zero)) for j in range(len(p))]
            norm_next = inner(z, z)
            beta = norm_next / norm
            p = [z[j] + beta * p[j] for j in range(len(z))]
            norm = norm_next
    return x


def combine_body(dm, nk, moments, scalars, w0a, w0b, w1a, w1b, w1c, w2a, w2b, w2c, w2d, out, made, sems):
    par = lax.rem(lax.axis_index("slab"), 2)
    nl, nc, nz = dm.nl, dm.nc, dm.nz
    sums = jnp.sum(moments[...].reshape(-1, LANES), axis=0, keepdims=True)
    x = coefficients(jnp.broadcast_to(sums, (8, LANES)), nk)
    x = [t * scalars[nk * 8 : nk * 8 + 1, :] for t in x]
    scale = [[jnp.broadcast_to(t[:, k : k + 1], (8, LANES)) for k in range(nk)] for t in x]
    W0 = stack(dm, w0a, range(1, nl)) | stack(dm, w0b, (0,))
    W1 = stack(dm, w1a, range(2, nl)) | stack(dm, w1b, (1,)) | stack(dm, w1c, (0,))
    W2 = stack(dm, w2a, range(3, nl)) | stack(dm, w2b, (2,)) | stack(dm, w2c, (1,)) | stack(dm, w2d, (0,))
    copies = []
    for p in range(nl):

        def body(z, p=p):
            for c in range(nc):
                terms = [
                    scale[j][k] * w[p].get(c, z, k) for j, w in enumerate((W0, W1, W2)) for k in range(nk)
                ]
                while len(terms) > 1:
                    terms = [sum(terms[n : n + 2][1:], terms[n]) for n in range(0, len(terms), 2)]
                made[p, pl.ds(z, 8), c * LANES : (c + 1) * LANES] = terms[0]

        blocks(0, nz, body, 2)
        layer = jnp.where(par == 0, p, nl - 1 - p)
        copy = pltpu.make_async_copy(made.at[p], out.at[layer], sems.at[p])
        copy.start()
        copies.append(copy)
    for copy in copies:
        copy.wait()


def on_device(right_side, cond_x, cond_y, cond_z, kappa_sq, shifts, weights):
    dm = Dims(right_side.shape)
    nk = shifts.shape[0]
    nl = dm.nl
    count = lax.axis_size("slab")
    f32 = jnp.float32
    vmem = pl.BlockSpec(memory_space=pltpu.VMEM)

    def params(mib):
        return pltpu.CompilerParams(vmem_limit_bytes=mib * MIB)

    def shape(*dims):
        return jax.ShapeDtypeStruct(dims, f32)

    def stacked(slots):
        return (nk, dm.stack_rows(slots), LANES)

    own = (dm.stack_rows(nl), LANES)
    half_stack = pltpu.VMEM((nk, dm.nc * dm.half, LANES), f32)
    plane_stack = shape(nk, dm.plane, LANES)
    sums = shape(6 * nk * 8, LANES)

    to_swap, flats, scalars = pl.pallas_call(
        functools.partial(pack_faces_body, dm, nk),
        out_shape=(shape(dm.rows_first, LANES), shape(4, *own), shape(nk * 8 + 8, LANES)),
        in_specs=[vmem] * 5,
        out_specs=(vmem,) * 3,
        scratch_shapes=[pltpu.VMEM(own, f32)],
        compiler_params=params(20),
        name="pack_faces",
    )(jnp.stack([cond_x, cond_y]), cond_z, kappa_sq, shifts[None], weights[None])
    to_edge, to_rest, to_in, rhs = pl.pallas_call(
        functools.partial(pack_body, dm),
        out_shape=(
            shape(dm.rows_edge, LANES), shape(dm.rows_rest, LANES), shape(dm.rows_all, LANES), shape(*own),
        ),
        in_specs=[vmem] * 2,
        out_specs=(vmem,) * 4,
        compiler_params=params(20),
        name="pack",
    )(right_side, flats)

    outward = [pair for i in range(1, count - 1, 2) for pair in ((i, i + 1), (i + 1, i))]
    from_first = lax.ppermute(to_swap, "slab", outward)
    from_in = lax.ppermute(to_in, "slab", [(i, i ^ 1) for i in range(count)])
    fields = lax.axis_size("field")

    def call(body, name, mib, results, scratch, operands, cost):
        return pl.pallas_call(
            functools.partial(body, dm, nk),
            out_shape=results,
            in_specs=[vmem] * (len(operands) + 1),
            out_specs=(vmem,) * len(results),
            scratch_shapes=scratch,
            compiler_params=params(mib),
            cost_estimate=pl.CostEstimate(
                flops=10**6, bytes_accessed=cost * 3 * 10**6, transcendentals=0
            ),
            name=name,
        )(*operands, scalars)

    def wide(slots):
        return shape(*stacked(slots))

    def held(slots):
        return pltpu.VMEM(stacked(slots), f32)

    w0a, w1a, w1h, part1, acc, coef, inv12, inv34 = call(
        near_a_body, "near_a", 20,
        (wide(nl - 1), wide(nl - 2), wide(2), plane_stack, sums, shape(*own), wide(2), wide(nl - 2)),
        [pltpu.VMEM((2, dm.plane, LANES), f32), held(3), held(1)],
        (flats, rhs, from_in), 6,
    )
    to_edge, acc = lax.optimization_barrier((to_edge, acc))
    from_edge = lax.ppermute(to_edge, "slab", outward)
    w2a, part2, acc = call(
        near_b_body, "near_b", 20,
        (wide(nl - 3), plane_stack, sums),
        [held(1)],
        (flats, coef, w1a, w1h, acc, inv34, from_in), 3,
    )
    from_first, acc = lax.optimization_barrier((from_first, acc))
    swap_a = from_first[: dm.rows_swap]
    swap_b = lax.ppermute(swap_a, "field", [(i, i ^ 1) for i in range(fields)])
    w0b, w1b, w2b, acc, edge, inv0, part0, part3 = call(
        far_0_body, "far_0", 20,
        (wide(1), wide(1), wide(1), sums, shape(2, dm.plane, LANES), wide(1), plane_stack, plane_stack),
        [],
        (flats, rhs, coef, w0a, w1a, w2a, part1, part2, acc, inv12, from_first), 2,
    )
    to_rest, acc = lax.optimization_barrier((to_rest, acc))
    from_rest = lax.ppermute(to_rest, "slab", outward)
    w0h, w1c, w2c, part4, acc, inv1 = call(
        far_a_body, "far_a", 20,
        (wide(1), wide(1), wide(1), plane_stack, sums, wide(1)),
        [pltpu.VMEM((dm.plane, LANES), f32)],
        (flats, coef, w0b, w1b, w2b, part0, part3, acc, inv12, inv0, edge, from_edge), 4,
    )
    w2d, acc, w1h, inv2, shared = call(
        far_b_body, "far_b", 20,
        (wide(1), sums, wide(1), wide(1), shape(2 * dm.rows_swap, LANES)),
        [pltpu.VMEM((nk, dm.plane, LANES), f32)],
        (flats, coef, w0b, w0h, w1c, w2c, part4, acc, edge, inv0, inv1, from_edge, swap_a, swap_b), 3,
    )
    moments, _ = call(
        far_c_body, "far_c", 20,
        (shape(1, LANES), sums),
        [half_stack] * 3
        + [pltpu.VMEM((nk, dm.nc * dm.more + 2 * PAD, LANES), f32)],
        (w0h, w1c, w1h, w2d, acc, edge, inv1, inv2, from_edge, from_rest, shared), 2,
    )

    everywhere = jnp.broadcast_to(moments[None], (count, 1, LANES))
    gathered = lax.all_to_all(everywhere, "slab", 0, 0)

    return pl.pallas_call(
        functools.partial(combine_body, dm, nk),
        out_shape=jax.ShapeDtypeStruct(right_side.shape, f32),
        in_specs=[vmem] * 11,
        out_specs=pl.BlockSpec(memory_space=pl.ANY),
        scratch_shapes=[pltpu.VMEM(right_side.shape, f32), pltpu.SemaphoreType.DMA((nl,))],
        compiler_params=params(20),
        name="combine",
    )(gathered, scalars, w0a, w0b, w1a, w1b, w1c, w2a, w2b, w2c, w2d)


def solution(mesh):
    return jax.shard_map(
        on_device,
        mesh=mesh,
        in_specs=(
            P(("field", "slab"), None, None),
            P("slab", None, None),
            P("slab", None, None),
            P("slab", None, None),
            P("slab", None, None),
            P(),
            P(),
        ),
        out_specs=P(("field", "slab"), None, None),
        check_vma=False,
    )
```
